32 devices in a mesh: gx: 2 (over y), gy: 4 (over x, core), gz: 4 (over z).
Axes of the slice: x: 2, y: 2, z: 4, core: 2. Of those that a mesh axis runs over, the one named last changes fastest.
Arguments:
- magnetic: float32 [3, 32, 128, 512], P(None, 'gx', 'gy', 'gz'), may hold values from -11 to 11
Outputs:
- cleaned: float32 [3, 32, 128, 512], P(None, 'gx', 'gy', 'gz')
The draws below stay inside these ranges and needn't reach their ends.
All inputs are finite; a program needn't handle non-finite values.
Results may differ from the reference program's by a relative error of at most 0.00018.
Values sent between devices are 32-bit elements; how exact they have to be, the bound alone decides.
No kernel may reach another device: no remote copies, remote signals or barrier semaphores. Data moves between devices by JAX's collectives and lax.ppermute only.
A program may use at most 128 MiB of HBM per device.

```python
import math
import jax
import jax.numpy as jnp
from jax import lax

LEVELS = 5
SWEEPS = 3
COARSE_ITERS = 24
NX = 32
NY = 128
NZ = 512


def smooth_profile(key, extent, low_amp, high_amp):
    position_line = jnp.arange(extent).astype(jnp.float32)
    profile = jnp.zeros((extent,), jnp.float32)
    for level_order in range(3):
        period_cells = 2 ** (LEVELS - 1) * 2 ** (3 - level_order)
        wave_count = max(1, extent // period_cells)
        amp_key, shift_key, sign_key = jax.random.split(jax.random.fold_in(key, level_order), 3)
        amplitude = jax.random.uniform(amp_key, (), jnp.float32, low_amp, high_amp)
        sign_value = jnp.where(jax.random.bernoulli(sign_key), 1.0, -1.0).astype(jnp.float32)
        phase_shift = jax.random.uniform(shift_key, (), jnp.float32, 0.0, 2.0 * math.pi)
        angle_line = 2.0 * math.pi * wave_count * position_line / extent + phase_shift
        profile = profile + sign_value * amplitude * jnp.sin(angle_line)
    return profile


def draw_magnetic(key, part):
    noise_key, smooth_key = jax.random.split(key, 2)
    extents = (NX, NY, NZ)
    noise_field = jnp.clip(jax.random.normal(noise_key, (3, NX, NY, NZ), jnp.float32), -6.0, 6.0)
    low_amp, high_amp = (0.6, 1.2)
    pieces = []
    for component in range(3):
        profile = smooth_profile(jax.random.fold_in(smooth_key, component), extents[component], low_amp, high_amp)
        shape_list = [1, 1, 1]
        shape_list[component] = extents[component]
        pieces.append(noise_field[component] + profile.reshape(shape_list))
    return jnp.stack(pieces).astype(jnp.float32)


def setup_inputs(seed: int = 0) -> dict:
    splits = jax.random.split(jax.random.key(seed), 2)
    magnetic = draw_magnetic(jax.random.fold_in(splits[1], 71), 0)
    return {"magnetic": magnetic}


relax_weight = 6.0 / 7.0


def apply_local(values, stretch):
    beside = jnp.roll(values, -1, 0) + jnp.roll(values, 1, 0)
    beside = beside + jnp.roll(values, -1, 1) + jnp.roll(values, 1, 1)
    beside = beside + jnp.roll(values, -1, 2) + jnp.roll(values, 1, 2)
    return (6.0 * values - beside) * stretch


def restrict(values):
    extent = values.shape
    blocks = values.reshape(extent[0] // 2, 2, extent[1] // 2, 2, extent[2] // 2, 2)
    return jnp.sum(blocks, axis=(1, 3, 5)) * 0.125


def prolong(values):
    extent = values.shape
    spread = jnp.broadcast_to(values[:, None, :, None, :, None], (extent[0], 2, extent[1], 2, extent[2], 2))
    return spread.reshape(extent[0] * 2, extent[1] * 2, extent[2] * 2)


def cycle_whole(source, level_index):
    stretch = 0.25 ** level_index
    factor = relax_weight * 4.0 ** level_index / 6.0
    solution = factor * source
    if level_index == LEVELS - 1:
        def coarse_sweep(iteration, current):
            return current + factor * (source - apply_local(current, stretch))
        return lax.fori_loop(0, COARSE_ITERS - 1, coarse_sweep, solution)
    for repeat in range(SWEEPS - 1):
        solution = solution + factor * (source - apply_local(solution, stretch))
    residual_field = source - apply_local(solution, stretch)
    correction = cycle_whole(restrict(residual_field), level_index + 1)
    solution = solution + prolong(correction)
    for repeat in range(SWEEPS):
        solution = solution + factor * (source - apply_local(solution, stretch))
    return solution


def reference(magnetic):
    along_x, along_y, along_z = magnetic[0], magnetic[1], magnetic[2]
    divergence = (along_x - jnp.roll(along_x, 1, 0)) + (along_y - jnp.roll(along_y, 1, 1)) + (along_z - jnp.roll(along_z, 1, 2))
    potential = cycle_whole(-divergence, 0)
    cleaned_x = along_x - (jnp.roll(potential, -1, 0) - potential)
    cleaned_y = along_y - (jnp.roll(potential, -1, 1) - potential)
    cleaned_z = along_z - (jnp.roll(potential, -1, 2) - potential)
    return jnp.stack([cleaned_x, cleaned_y, cleaned_z])
```

```python
import functools

import jax
import jax.numpy as jnp
from jax import lax
from jax.experimental import pallas as pl
from jax.experimental.pallas import tpu as pltpu
from jax.sharding import PartitionSpec as P

LEVELS = 5
SWEEPS = 3
COARSE_ITERS = 24


F32 = jnp.float32
LANES = 128
VMEM_LIMIT = 16 * 1024 * 1024


def weight(level):
    return 4.0**level / 7.0


def shape(*extent):
    return jax.ShapeDtypeStruct(extent, F32)


def call(kernel, outs, scratch, flops, *args):
    bytes_accessed = 4 * sum(a.size for a in args)
    return pl.pallas_call(
        kernel,
        out_shape=outs,
        scratch_shapes=[pltpu.VMEM(s, F32) for s in scratch],
        compiler_params=pltpu.CompilerParams(vmem_limit_bytes=VMEM_LIMIT),
        cost_estimate=pl.CostEstimate(flops=flops, bytes_accessed=bytes_accessed, transcendentals=0),
    )(*args)


def iota(extent, dim):
    return lax.broadcasted_iota(jnp.int32, extent, dim)


def one_hot(condition):
    rows = iota((LANES, LANES), 0)
    columns = iota((LANES, LANES), 1)
    return jnp.where(condition(rows, columns), 1.0, 0.0).astype(F32)


def dot(left, right):
    return lax.dot_general(
        left,
        right,
        (((1,), (0,)), ((), ())),
        precision=lax.Precision.HIGHEST,
        preferred_element_type=F32,
    )


def seven_sum(source, plane, below, above):
    tiles = source.shape[0]
    rows = source.shape[2]
    center = [source[t, plane] for t in range(tiles)]
    left = [pltpu.roll(v, 1, 1) for v in center]
    right = [pltpu.roll(v, LANES - 1, 1) for v in center]
    if tiles > 1:
        lane = iota((rows, LANES), 1)
        left = [jnp.where(lane == 0, left[t - 1], left[t]) for t in range(tiles)]
        right = [
            jnp.where(lane == LANES - 1, right[(t + 1) % tiles], right[t]) for t in range(tiles)
        ]
    out = []
    for t in range(tiles):
        v = center[t]
        total = v + (source[t, below] + source[t, above])
        total = total + (pltpu.roll(v, 1, 0) + pltpu.roll(v, rows - 1, 0))
        out.append(total + (left[t] + right[t]))
    return out


def sweep(target, source, low, high, base=None, scale=None, period=None, base_shift=0):
    def step(plane, carry):
        if period is None:
            below, above = plane - 1, plane + 1
        else:
            below = lax.rem(plane + period - 1, period)
            above = lax.rem(plane + 1, period)
        for t, value in enumerate(seven_sum(source, plane, below, above)):
            if scale is not None:
                value = value * scale
            if base is not None:
                value = value + base[t, plane + base_shift]
            target[t, plane] = value
        return carry

    lax.fori_loop(low, high, step, 0, unroll=False)


PLANE0 = 6
ROW0 = 8
SPILL = 5


def fill_source(field, target):
    planes, rows = field.shape[1], field.shape[2]
    lane = iota((rows, LANES), 1)
    row = iota((rows, LANES), 0)
    row8 = iota((8, LANES), 0)
    zero8 = jnp.zeros((8, LANES), F32)
    zeros = jnp.zeros((rows, LANES), F32)

    def one_plane(i, before):
        along_x, along_y, along_z = field[0, i], field[1, i], field[2, i]
        value = before - along_x - along_y - along_z
        value = value + jnp.where(row == 0, 0.0, pltpu.roll(along_y, 1, 0))
        turned = pltpu.roll(along_z, 1, 1)
        value = value + jnp.where(lane == 0, 0.0, turned)
        p = PLANE0 + i
        target[0, p, 0:ROW0] = zero8
        target[0, p, ROW0 : ROW0 + rows] = value
        last = pltpu.roll(along_y[rows - 8 : rows], 1, 0)
        target[0, p, ROW0 + rows : ROW0 + rows + 8] = jnp.where(row8 == 0, last, 0.0)
        target[1, p, 0:ROW0] = zero8
        target[1, p, ROW0 : ROW0 + rows] = jnp.where(lane == 0, turned, 0.0)
        target[1, p, ROW0 + rows : ROW0 + rows + 8] = zero8

    one_plane(0, zeros)

    def step(i, carry):
        one_plane(i, field[0, i - 1])
        return carry

    lax.fori_loop(1, planes, step, 0)
    p = PLANE0 + planes
    target[0, p] = jnp.zeros(target.shape[2:], F32)
    target[1, p] = jnp.zeros(target.shape[2:], F32)
    target[0, p, ROW0 : ROW0 + rows] = field[0, planes - 1]


def clear_planes(target, planes):
    for t in range(target.shape[0]):
        for p in planes:
            target[t, p] = jnp.zeros(target.shape[2:], F32)


def pack_lanes(read, count, first, width, spacing, rows):
    lane = iota((rows, LANES), 1)
    per_tile = LANES // spacing
    tiles = []
    for start in range(0, count, per_tile):
        packed = jnp.zeros((rows, LANES), F32)
        for k in range(min(per_tile, count - start)):
            turned = pltpu.roll(read(start + k), (spacing * k - first) % LANES, 1)
            inside = (lane >= spacing * k) & (lane < spacing * k + width)
            packed = jnp.where(inside, turned, packed)
        tiles.append(packed)
    return tiles


def unpacked(packed, k, spacing, offset, width, first, rows):
    lane = iota((rows, LANES), 1)
    turned = pltpu.roll(packed, (first - spacing * k - offset) % LANES, 1)
    inside = (lane >= first) & (lane < first + width)
    return jnp.where(inside, turned, 0.0)


def spread_kernel(field, up, down, far, g1_out, first, second, g1_a, g1_b):
    planes = field.shape[1]
    count = first.shape[1]
    edge = [p for p in range(count) if p < PLANE0 or p > PLANE0 + planes]
    clear_planes(first, edge)
    clear_planes(second, edge)
    fill_source(field, first)
    low, high = PLANE0, PLANE0 + planes + 1
    sweep(second, first, low - 1, high + 1)
    sweep(first, second, low - 2, high + 2)
    sweep(second, first, low - 3, high + 3)

    n1 = planes // 2
    rows1 = first.shape[2] // 2
    pieces = []
    for t in range(2):
        parts = []
        for c in range(-2, n1 + 2):
            p = PLANE0 + 2 * c
            total = second[t, p, pl.ds(0, rows1, stride=2), :]
            total = total + second[t, p, pl.ds(1, rows1, stride=2), :]
            total = total + second[t, p + 1, pl.ds(0, rows1, stride=2), :]
            total = total + second[t, p + 1, pl.ds(1, rows1, stride=2), :]
            parts.append(total)
        pieces.append(jnp.concatenate(parts, axis=0))
    main = one_hot(lambda r, c: c == 32 + r // 2)
    side = one_hot(lambda r, c: c == jnp.where(r < 64, 96 + r // 2, r // 2 - 32))
    g1 = (dot(pieces[0], main) + dot(pieces[1], side)) * (0.125 / 343.0)
    share = n1 + 4
    g1 = g1.reshape(share, rows1, LANES)
    g1_out[...] = g1

    clear_planes(g1_a, range(g1_a.shape[1]))
    clear_planes(g1_b, range(g1_b.shape[1]))
    for c in range(share):
        g1_a[0, 4 + c, 4 : 4 + rows1] = g1[c]
    sweep(g1_b, g1_a, 3, 5 + share)
    sweep(g1_a, g1_b, 2, 6 + share)
    sweep(g1_b, g1_a, 1, 7 + share)
    rows2 = g1_a.shape[2] // 2
    parts = []
    for c in range(g1_a.shape[1] // 2):
        total = g1_b[0, 2 * c, pl.ds(0, rows2, stride=2), :]
        total = total + g1_b[0, 2 * c, pl.ds(1, rows2, stride=2), :]
        total = total + g1_b[0, 2 * c + 1, pl.ds(0, rows2, stride=2), :]
        total = total + g1_b[0, 2 * c + 1, pl.ds(1, rows2, stride=2), :]
        parts.append(total)
    even = jnp.concatenate(parts[0::2], axis=0)
    odd = jnp.concatenate(parts[1::2], axis=0)
    g2 = dot(even, one_hot(lambda r, c: c == r // 2))
    g2 = g2 + dot(odd, one_hot(lambda r, c: c == 64 + r // 2))
    g2 = g2 * (0.125 / 343.0)
    size = g2.shape[0]
    far[...] = g2
    up[0:size] = g2
    down[0:size] = g2
    up[size:] = pack_lanes(lambda c: g1[c], share, 89, 9, 10, rows1)[0]
    down[size:] = pack_lanes(lambda c: g1[c], share, 30, 9, 10, rows1)[0]


def gather_z_kernel(count, *refs):
    own, g1, received, (g2_out, g1_out) = refs[0], refs[1], refs[2 : 1 + count], refs[1 + count :]
    size = own.shape[0]
    period = 32 * count
    rows2 = 16
    tiles, planes = g2_out.shape[0], g2_out.shape[1]
    lane = iota((size, LANES), 1)
    for parity in range(2):
        totals = [jnp.zeros((size, LANES), F32) for _ in range(tiles)]
        for o in range(count):
            value = own[...] if o == 0 else received[o - 1][0:size]
            shift = (32 * o - 64 * parity) % LANES
            turned = pltpu.roll(value, shift, 1) if shift else value
            position = ((lane - shift) & (LANES - 1)) - 64 * parity
            inside = (position >= 0) & (position < 64)
            for t in range(tiles):
                lands = lax.rem(position + (32 * o + period), period) == lane + LANES * t
                totals[t] = totals[t] + jnp.where(inside & lands, turned, 0.0)
        for t in range(tiles):
            for k in range(planes // 2):
                g2_out[t, 2 * k + parity] = totals[t][rows2 * k : rows2 * (k + 1)]
    above = received[0][size:]
    below = received[count - 2][size:]
    rows1 = g1.shape[1]
    for c in range(g1.shape[0]):
        value = g1[c] + unpacked(below, c, 10, 0, 9, 25, rows1)
        g1_out[c] = value + unpacked(above, c, 10, 0, 9, 94, rows1)


def fold_x_kernel(count, *refs):
    shares, out = refs[:count], refs[count]
    tiles, period = out.shape[0], out.shape[1]
    for t in range(tiles):
        for x in range(period):
            total = None
            for o in range(count):
                for c in range(10):
                    if (c - 3 + 4 * o) % period == x:
                        value = shares[o][t, c]
                        total = value if total is None else total + value
            out[t, x] = total


def window_x_kernel(sources, *refs):
    inputs, (out, down, up) = refs[:-3], refs[-3:]
    planes = out.shape[0]
    for p in range(planes):
        total = None
        for index, offset, first, length in sources:
            k = p - 7 - 8 * offset + 2 - first
            inside = 0 <= p - 7 - 8 * offset + 2 < 12
            if inside and 0 <= k < length:
                value = inputs[index][k]
                total = value if total is None else total + value
        out[p] = total
        down[p] = total[2:10]
        up[p] = total[13:21]
        down[planes + p // 8, p % 8 : p % 8 + 1] = total[10:11]
        up[planes + p // 8, p % 8 : p % 8 + 1] = total[21:22]


def fine_tail_kernel(g1, above, below, out, base, first, second):
    planes, rows1 = g1.shape[0], g1.shape[1]

    def step(p, carry):
        base[0, p] = jnp.zeros(base.shape[2:], F32)
        base[0, p, 4 : 4 + rows1] = g1[p]
        base[0, p, 22:30] = base[0, p, 22:30] + above[p]
        base[0, p, 1:9] = base[0, p, 1:9] + below[p]
        return carry

    lax.fori_loop(0, planes, step, 0)
    for p in range(planes):
        ninth = p % 8
        base[0, p, 30:31] = base[0, p, 30:31] + above[planes + p // 8, ninth : ninth + 1]
        base[0, p, 9:10] = base[0, p, 9:10] + below[planes + p // 8, ninth : ninth + 1]
    seventh = 1.0 / 7.0
    sweep(first, base, 1, planes - 1, base, seventh)
    sweep(second, first, 2, planes - 2, base, seventh)
    sweep(first, second, 3, planes - 3, base, seventh)
    sweep(second, first, 4, planes - 4, base, seventh)
    sweep(first, second, 5, planes - 5, base, seventh)
    for c in range(out.shape[0]):
        out[c] = first[0, 5 + c] * weight(1)


def restrict_lanes(values, width, coarse_width, coarse_tiles):
    out = []
    for s in range(coarse_tiles):
        total = None
        for t, value in enumerate(values):
            matrix = one_hot(
                lambda r, c: ((LANES * t + r) // 2 == lax.rem(LANES * s + c, coarse_width))
                & (LANES * t + r < width)
            )
            term = dot(value, matrix)
            total = term if total is None else total + term
        out.append(total)
    return out


def prolong_lanes(values, width, fine_tiles):
    out = []
    for s in range(fine_tiles):
        total = None
        for t, value in enumerate(values):
            matrix = one_hot(lambda r, c: LANES * t + r == lax.rem(LANES * s + c, width) // 2)
            term = dot(value, matrix)
            total = term if total is None else total + term
        out.append(total)
    return out


def solve(level, width, buffers):
    g, a, b = buffers[level]
    tiles, planes, rows = g.shape[0], g.shape[1], g.shape[2]
    seventh = 1.0 / 7.0
    if level == LEVELS - 1:
        source = [[g[t, p] for t in range(tiles)] for p in range(planes)]

        def step(iteration, carry):
            out = []
            for p in range(planes):
                v = carry[p]
                total = v + carry[(p + 1) % planes] + carry[(p - 1) % planes]
                total = total + (pltpu.roll(v, 1, 0) + pltpu.roll(v, rows - 1, 0))
                total = total + (pltpu.roll(v, 1, 1) + pltpu.roll(v, LANES - 1, 1))
                out.append(source[p][0] + total * seventh)
            return tuple(out)

        start = tuple(source[p][0] for p in range(planes))
        final = lax.fori_loop(0, COARSE_ITERS - 1, step, start)
        for p in range(planes):
            g[0, p] = final[p] * weight(level)
        return
    w = weight(level)
    coarse = buffers[level + 1][0]
    sweep(a, g, 0, planes, None, seventh, planes)
    sweep(b, a, 0, planes, None, seventh, planes)
    for t in range(tiles):
        for p in range(planes):
            g[t, p] = (g[t, p] + a[t, p] + b[t, p]) * w
    sweep(a, b, 0, planes, None, seventh, planes)
    half = rows // 2
    values = []
    for t in range(tiles):
        parts = []
        for c in range(planes // 2):
            total = a[t, 2 * c, pl.ds(0, half, stride=2), :]
            total = total + a[t, 2 * c, pl.ds(1, half, stride=2), :]
            total = total + a[t, 2 * c + 1, pl.ds(0, half, stride=2), :]
            total = total + a[t, 2 * c + 1, pl.ds(1, half, stride=2), :]
            parts.append(total)
        values.append(jnp.concatenate(parts, axis=0))
    values = restrict_lanes(values, width, width // 2, coarse.shape[0])
    for t, value in enumerate(values):
        for c in range(planes // 2):
            coarse[t, c] = value[half * c : half * (c + 1)] * 0.125
    solve(level + 1, width // 2, buffers)
    values = [
        jnp.concatenate([coarse[t, c] for c in range(planes // 2)], axis=0)
        for t in range(coarse.shape[0])
    ]
    values = prolong_lanes(values, width, tiles)
    for t, value in enumerate(values):
        for c in range(planes // 2):
            part = value[half * c : half * (c + 1)]
            for p in (2 * c, 2 * c + 1):
                b[t, p, pl.ds(0, half, stride=2), :] = part
                b[t, p, pl.ds(1, half, stride=2), :] = part
        for p in range(planes):
            b[t, p] = b[t, p] + g[t, p]
    sweep(a, b, 0, planes, None, seventh, planes)
    sweep(b, a, 0, planes, None, seventh, planes)
    sweep(a, b, 0, planes, None, seventh, planes)
    for t in range(tiles):
        for p in range(planes):
            g[t, p] = g[t, p] + a[t, p]


def coarse_kernel(count, *refs):
    shares, out, scratch = refs[:count], refs[count], refs[count + 1 :]
    buffers = {level: scratch[3 * (level - 2) : 3 * (level - 1)] for level in (2, 3, 4)}
    g = buffers[2][0]
    tiles, planes = g.shape[0], g.shape[1]
    for t in range(tiles):
        for p in range(planes):
            for b in range(count):
                value = shares[b][t, p, 0:8] + shares[(b - 1) % count][t, p, 8:16]
                g[t, p, 8 * b : 8 * b + 8] = value
    solve(2, LANES * tiles, buffers)
    for c in range(out.shape[0]):
        out[c] = g[0, (c - 3) % planes, 0:16]


def finish_kernel(field, e2, f1, f0, below, above, out, u1_a, u1_b, u0_a, u0_b, pot):
    share2 = e2.shape[0]
    rows2 = e2.shape[1]
    value = e2[...].reshape(share2 * rows2, LANES)
    value = dot(value, one_hot(lambda r, c: r == c // 2))
    for c in range(share2):
        part = value[rows2 * c : rows2 * (c + 1)]
        for p in (2 * c, 2 * c + 1):
            u1_a[0, p, pl.ds(0, rows2, stride=2), :] = part
            u1_a[0, p, pl.ds(1, rows2, stride=2), :] = part
    count1 = 2 * share2
    sweep(u1_b, u1_a, 1, count1 - 1)
    sweep(u1_a, u1_b, 2, count1 - 2)
    sweep(u1_b, u1_a, 3, count1 - 3)
    share1 = f1.shape[0]
    rows1 = 24
    parts = []
    for c in range(share1):
        parts.append(f1[c, 4 : 4 + rows1] + u1_b[0, 4 + c, 4 : 4 + rows1] * (1.0 / 343.0))
    value = jnp.concatenate(parts, axis=0)
    main = dot(value, one_hot(lambda r, c: r == 32 + c // 2))
    side = dot(value, one_hot(lambda r, c: r == jnp.where(c < 64, 96 + c // 2, c // 2 - 32)))
    for t, value in enumerate((main, side)):
        for c in range(share1):
            part = value[rows1 * c : rows1 * (c + 1)]
            for p in (2 * c, 2 * c + 1):
                u0_a[t, p, pl.ds(0, rows1, stride=2), :] = part
                u0_a[t, p, pl.ds(1, rows1, stride=2), :] = part
    count0 = 2 * share1
    sweep(u0_b, u0_a, 1, count0 - 1)
    sweep(u0_a, u0_b, 2, count0 - 2)
    sweep(u0_b, u0_a, 3, count0 - 3)

    planes, rows = field.shape[1], field.shape[2]
    scale = 1.0 / 343.0
    for i in range(planes + 1):
        value = u0_b[0, 4 + i, ROW0 : ROW0 + rows] * scale + f0[fine_plane(i)]
        if i <= SPILL:
            value = value + below[2 + i]
        if i >= planes - SPILL:
            value = value + above[i - (planes - SPILL)]
        pot[i, 0:rows] = value
        edge = u0_b[0, 4 + i, ROW0 + rows : ROW0 + rows + 1] * scale
        if i < planes:
            edge = edge + f0[6, i + SPILL : i + SPILL + 1]
            if i <= SPILL:
                edge = edge + below[0, i + SPILL + planes : i + SPILL + planes + 1]
            if i >= planes - SPILL:
                edge = edge + above[6, i + SPILL - planes : i + SPILL - planes + 1]
            pot[i, rows : rows + 1] = edge
    column = f0[7] + pltpu.roll(below[1], LANES - planes, 1) + pltpu.roll(above[7], planes, 1)
    lane = iota((rows, LANES), 1)
    for i in range(planes):
        here = pot[i, 0:rows]
        out[0, i] = field[0, i] - (pot[i + 1, 0:rows] - here)
        out[1, i] = field[1, i] - (pot[i, 1 : rows + 1] - here)
        beyond = pltpu.roll(u0_b[1, 4 + i, ROW0 : ROW0 + rows], LANES - 1, 1) * scale
        beyond = beyond + pltpu.roll(column, LANES - 1 - (i + SPILL), 1)
        next_z = jnp.where(lane == LANES - 1, beyond, pltpu.roll(here, LANES - 1, 1))
        out[2, i] = field[2, i] - (next_z - here)


def fine_plane(i):
    return i + SPILL if i <= 0 else i + SPILL + 2


def fine_share_kernel(field, main, up, down, base, first, second):
    planes = field.shape[1]
    count = base.shape[1]
    edge = [p for p in range(count) if p < PLANE0 or p > PLANE0 + planes]
    clear_planes(base, edge)
    clear_planes(first, edge)
    clear_planes(second, edge)
    fill_source(field, base)
    low, high = PLANE0, PLANE0 + planes + 1
    seventh = 1.0 / 7.0
    sweep(first, base, low - 1, high + 1, base, seventh)
    sweep(second, first, low - 2, high + 2, base, seventh)
    sweep(first, second, low - 3, high + 3, base, seventh)
    sweep(second, first, low - 4, high + 4, base, seventh)
    sweep(first, second, low - 5, high + 5, base, seventh)
    share, rows = main.shape[0], main.shape[1]

    def step(p, carry):
        main[p] = first[0, p + 1] * weight(0)
        return carry

    lax.fori_loop(0, share, step, 0)

    def read_up(p):
        return first[1, p + 1]

    def read_down(p):
        lane = iota((rows, LANES), 1)
        turned = pltpu.roll(first[1, p + 1], SPILL, 1)
        return jnp.where(lane == SPILL, pltpu.roll(first[0, p + 1], SPILL, 1), turned)

    for k, packed in enumerate(pack_lanes(read_up, share, 0, 6, 8, rows)):
        up[k] = packed * weight(0)
    for k, packed in enumerate(pack_lanes(read_down, share, 0, 6, 8, rows)):
        down[k] = packed * weight(0)


def fine_z_kernel(main, own, above, below, out, column_out, down, up):
    share, rows = main.shape[0], main.shape[1]
    lane = iota((rows, LANES), 1)
    column = jnp.zeros((rows, LANES), F32)
    for p in range(share):
        tile, k = p // 16, p % 16
        value = main[p] + unpacked(below[tile], k, 8, 0, 6, 0, rows)
        value = value + unpacked(above[tile], k, 8, 0, 5, LANES - 5, rows)
        out[p] = value
        turned = pltpu.roll(own[tile], (p - 8 * k) % LANES, 1)
        turned = turned + pltpu.roll(above[tile], (p - 8 * k - 5) % LANES, 1)
        column = jnp.where(lane == p, turned, column)
        down[p] = value[1:9]
        up[p] = value[40:48]
    column_out[...] = column
    down[share] = column[1:9]
    up[share] = column[40:48]


def fine_y_kernel(main, column, above, below, out, work):
    share = main.shape[0]
    rows = out.shape[1]

    def folded(k, value):
        work[...] = value
        work[33:41] = work[33:41] + above[k]
        work[8:16] = work[8:16] + below[k]

    out[6] = jnp.zeros((rows, LANES), F32)
    for p in range(share):
        folded(p, main[p])
        place = p if p <= SPILL else p + 2
        out[place] = work[ROW0 : ROW0 + rows]
        out[6, p : p + 1] = work[ROW0 + rows : ROW0 + rows + 1]
    folded(share, column[...])
    out[7] = work[ROW0 : ROW0 + rows]


def body(field):
    nx, ny, nz = field.shape[1:]
    size_x, size_y, size_z = lax.axis_size("gx"), lax.axis_size("gy"), lax.axis_size("gz")
    n1 = nx // 2
    share1 = n1 + 4
    rows0 = ny + 16
    rows1 = ny // 2 + 8
    planes0 = nx + 13

    def from_offset(value, axis, offset):
        count = lax.axis_size(axis)
        pairs = [(source, (source - offset) % count) for source in range(count)]
        return lax.ppermute(value, axis, pairs)

    level0 = (2, planes0, rows0, LANES)
    level1 = (1, n1 + 12, ny // 2 + 16, LANES)
    packed = ((n1 // 2 + 6) // 2) * 16
    up, down, far, g1 = call(
        spread_kernel,
        [shape(packed + rows1, LANES), shape(packed + rows1, LANES), shape(packed, LANES),
         shape(share1, rows1, LANES)],
        [level0, level0, level1, level1],
        6_000_000,
        field,
    )
    received = []
    for o in range(1, size_z):
        message = down if o == 1 else (up if o == size_z - 1 else far)
        received.append(from_offset(message, "gz", o))
    share0 = nx + 11
    main, f_up, f_down = call(
        fine_share_kernel,
        [shape(share0, rows0, LANES), shape(2, rows0, LANES), shape(2, rows0, LANES)],
        [level0, level0, level0],
        20_000_000,
        field,
    )
    f_above = from_offset(f_down, "gz", 1)
    f_below = from_offset(f_up, "gz", -1)

    tiles = size_z * 32 // LANES
    g2, g1 = call(
        functools.partial(gather_z_kernel, size_z),
        [shape(tiles, n1 // 2 + 6, 16, LANES), shape(share1, rows1, LANES)],
        [],
        500_000,
        far, g1, *received,
    )
    shares = [g2] + [from_offset(g2, "gx", o) for o in range(1, size_x)]
    inputs = [g1]
    sources = [(0, 0, 0, share1)]
    spans = {1: (0, 9), -1: (3, 12), 2: (0, 1), -2: (11, 12)}
    residues = {}
    for offset, span in spans.items():
        residues.setdefault(offset % size_x, []).append((offset, span))
    for residue, members in residues.items():
        if residue == 0:
            sources.extend((0, offset, 0, share1) for offset, span in members)
            continue
        first = min(span[0] for offset, span in members)
        last = max(span[1] for offset, span in members)
        inputs.append(from_offset(g1[first:last], "gx", residue))
        sources.extend((len(inputs) - 1, offset, first, last - first) for offset, span in members)
    g2 = call(
        functools.partial(fold_x_kernel, size_x),
        shape(tiles, 4 * size_x, 16, LANES),
        [],
        100_000,
        *shares,
    )
    planes1 = n1 + 14
    extra = -(-planes1 // 8)
    g1, g1_down, g1_up = call(
        functools.partial(window_x_kernel, tuple(sources)),
        [shape(planes1, rows1, LANES), shape(planes1 + extra, 8, LANES),
         shape(planes1 + extra, 8, LANES)],
        [],
        100_000,
        *inputs,
    )
    shares = [g2] + [from_offset(g2, "gy", o) for o in range(1, size_y)]
    g1_above = from_offset(g1_down, "gy", 1)
    g1_below = from_offset(g1_up, "gy", -1)

    main, column, f_down, f_up = call(
        fine_z_kernel,
        [shape(share0, rows0, LANES), shape(rows0, LANES), shape(share0 + 1, 8, LANES),
         shape(share0 + 1, 8, LANES)],
        [],
        1_000_000,
        main, f_up, f_above, f_below,
    )
    f_above = from_offset(f_down, "gy", 1)
    f_below = from_offset(f_up, "gy", -1)
    f0 = call(
        fine_y_kernel,
        shape(share0 + 2, ny, LANES),
        [(rows0, LANES)],
        500_000,
        main, column, f_above, f_below,
    )
    f_down, f_up = f0[0:8], jnp.concatenate([f0[6:8], f0[share0 + 2 - 6 :]], axis=0)
    if size_x == 2:
        other = from_offset(jnp.concatenate([f_down, f_up[2:]], axis=0), "gx", 1)
        f_above, f_below = other[0:8], jnp.concatenate([other[6:8], other[8:]], axis=0)
    else:
        f_above = from_offset(f_down, "gx", 1)
        f_below = from_offset(f_up, "gx", -1)

    scratch = []
    for level in (2, 3, 4):
        cut = 2 ** (level - 2)
        extent = (max(1, tiles // cut), 4 * size_x // cut, 8 * size_y // cut, LANES)
        scratch.extend([extent] * 3)
    e2 = call(
        functools.partial(coarse_kernel, size_y),
        shape(n1 // 2 + 6, 16, LANES),
        scratch,
        5_000_000,
        *shares,
    )
    window = (1, planes1, ny // 2 + 16, LANES)
    f1 = call(
        fine_tail_kernel,
        shape(share1, ny // 2 + 16, LANES),
        [window, window, window],
        3_000_000,
        g1, g1_above, g1_below,
    )
    return call(
        finish_kernel,
        shape(*field.shape),
        [level1, level1, (2, nx + 8, rows0, LANES), (2, nx + 8, rows0, LANES),
         (nx + 1, ny + 8, LANES)],
        6_000_000,
        field, e2, f1, f0, f_below, f_above,
    )


def solution(mesh):
    in_specs = (P(None, "gx", "gy", "gz"),)
    out_specs = P(None, "gx", "gy", "gz")
    return jax.shard_map(body, mesh=mesh, in_specs=in_specs, out_specs=out_specs, check_vma=False)
```

```python
import functools

import jax
import jax.numpy as jnp
from jax import lax
from jax.experimental import pallas as pl
from jax.experimental.pallas import tpu as pltpu
from jax.sharding import PartitionSpec as P

LEVELS = 5
SWEEPS = 3
COARSE_ITERS = 24


F32 = jnp.float32
LANES = 128
VMEM_LIMIT = 16 * 1024 * 1024


def weight(level):
    return 4.0**level / 7.0


def shape(*extent):
    return jax.ShapeDtypeStruct(extent, F32)


def call(kernel, outs, scratch, flops, *args):
    bytes_accessed = 4 * sum(a.size for a in args)
    return pl.pallas_call(
        kernel,
        out_shape=outs,
        scratch_shapes=[pltpu.VMEM(s, F32) for s in scratch],
        compiler_params=pltpu.CompilerParams(vmem_limit_bytes=VMEM_LIMIT),
        cost_estimate=pl.CostEstimate(flops=flops, bytes_accessed=bytes_accessed, transcendentals=0),
    )(*args)


def iota(extent, dim):
    return lax.broadcasted_iota(jnp.int32, extent, dim)


def one_hot(condition):
    rows = iota((LANES, LANES), 0)
    columns = iota((LANES, LANES), 1)
    return jnp.where(condition(rows, columns), 1.0, 0.0).astype(F32)


def dot(left, right):
    return lax.dot_general(
        left,
        right,
        (((1,), (0,)), ((), ())),
        precision=lax.Precision.HIGHEST,
        preferred_element_type=F32,
    )


def seven_sum(source, plane, below, above):
    tiles = source.shape[0]
    rows = source.shape[2]
    center = [source[t, plane] for t in range(tiles)]
    left = [pltpu.roll(v, 1, 1) for v in center]
    right = [pltpu.roll(v, LANES - 1, 1) for v in center]
    if tiles > 1:
        lane = iota((rows, LANES), 1)
        left = [jnp.where(lane == 0, left[t - 1], left[t]) for t in range(tiles)]
        right = [
            jnp.where(lane == LANES - 1, right[(t + 1) % tiles], right[t]) for t in range(tiles)
        ]
    out = []
    for t in range(tiles):
        v = center[t]
        total = v + (source[t, below] + source[t, above])
        total = total + (pltpu.roll(v, 1, 0) + pltpu.roll(v, rows - 1, 0))
        out.append(total + (left[t] + right[t]))
    return out


def sweep(target, source, low, high, base=None, scale=None, period=None):
    for plane in range(low, high):
        below, above = plane - 1, plane + 1
        if period is not None:
            below, above = below % period, above % period
        for t, value in enumerate(seven_sum(source, plane, below, above)):
            if scale is not None:
                value = value * scale
            if base is not None:
                value = value + base[t, plane]
            target[t, plane] = value


PLANE0 = 6
ROW0 = 8
SPILL = 5


def fill_source(field, target):
    planes, rows = field.shape[1], field.shape[2]
    lane = iota((rows, LANES), 1)
    row = iota((rows, LANES), 0)
    row8 = iota((8, LANES), 0)
    zero8 = jnp.zeros((8, LANES), F32)
    zeros = jnp.zeros((rows, LANES), F32)

    def one_plane(i, before):
        along_x, along_y, along_z = field[0, i], field[1, i], field[2, i]
        value = before - along_x - along_y - along_z
        value = value + jnp.where(row == 0, 0.0, pltpu.roll(along_y, 1, 0))
        turned = pltpu.roll(along_z, 1, 1)
        value = value + jnp.where(lane == 0, 0.0, turned)
        p = PLANE0 + i
        target[0, p, 0:ROW0] = zero8
        target[0, p, ROW0 : ROW0 + rows] = value
        last = pltpu.roll(along_y[rows - 8 : rows], 1, 0)
        target[0, p, ROW0 + rows : ROW0 + rows + 8] = jnp.where(row8 == 0, last, 0.0)
        target[1, p, 0:ROW0] = zero8
        target[1, p, ROW0 : ROW0 + rows] = jnp.where(lane == 0, turned, 0.0)
        target[1, p, ROW0 + rows : ROW0 + rows + 8] = zero8

    for i in range(planes):
        one_plane(i, field[0, i - 1] if i else zeros)
    p = PLANE0 + planes
    target[0, p] = jnp.zeros(target.shape[2:], F32)
    target[1, p] = jnp.zeros(target.shape[2:], F32)
    target[0, p, ROW0 : ROW0 + rows] = field[0, planes - 1]


def clear_planes(target, planes):
    for t in range(target.shape[0]):
        for p in planes:
            target[t, p] = jnp.zeros(target.shape[2:], F32)


def pack_lanes(read, count, first, width, spacing, rows):
    lane = iota((rows, LANES), 1)
    per_tile = LANES // spacing
    tiles = []
    for start in range(0, count, per_tile):
        packed = jnp.zeros((rows, LANES), F32)
        for k in range(min(per_tile, count - start)):
            turned = pltpu.roll(read(start + k), (spacing * k - first) % LANES, 1)
            inside = (lane >= spacing * k) & (lane < spacing * k + width)
            packed = jnp.where(inside, turned, packed)
        tiles.append(packed)
    return tiles


def unpacked(packed, k, spacing, offset, width, first, rows):
    lane = iota((rows, LANES), 1)
    turned = pltpu.roll(packed, (first - spacing * k - offset) % LANES, 1)
    inside = (lane >= first) & (lane < first + width)
    return jnp.where(inside, turned, 0.0)


def spread_kernel(field, up, down, far, g1_out, first, second, g1_a, g1_b):
    planes = field.shape[1]
    count = first.shape[1]
    edge = [p for p in range(count) if p < PLANE0 or p > PLANE0 + planes]
    clear_planes(first, edge)
    clear_planes(second, edge)
    fill_source(field, first)
    low, high = PLANE0, PLANE0 + planes + 1
    sweep(second, first, low - 1, high + 1)
    sweep(first, second, low - 2, high + 2)
    sweep(second, first, low - 3, high + 3)

    n1 = planes // 2
    rows1 = first.shape[2] // 2
    pieces = []
    for t in range(2):
        parts = []
        for c in range(-2, n1 + 2):
            p = PLANE0 + 2 * c
            total = second[t, p, pl.ds(0, rows1, stride=2), :]
            total = total + second[t, p, pl.ds(1, rows1, stride=2), :]
            total = total + second[t, p + 1, pl.ds(0, rows1, stride=2), :]
            total = total + second[t, p + 1, pl.ds(1, rows1, stride=2), :]
            parts.append(total)
        pieces.append(jnp.concatenate(parts, axis=0))
    main = one_hot(lambda r, c: c == 32 + r // 2)
    side = one_hot(lambda r, c: c == jnp.where(r < 64, 96 + r // 2, r // 2 - 32))
    g1 = (dot(pieces[0], main) + dot(pieces[1], side)) * (0.125 / 343.0)
    share = n1 + 4
    g1 = g1.reshape(share, rows1, LANES)
    g1_out[...] = g1

    clear_planes(g1_a, range(g1_a.shape[1]))
    clear_planes(g1_b, range(g1_b.shape[1]))
    for c in range(share):
        g1_a[0, 4 + c, 4 : 4 + rows1] = g1[c]
    sweep(g1_b, g1_a, 3, 5 + share)
    sweep(g1_a, g1_b, 2, 6 + share)
    sweep(g1_b, g1_a, 1, 7 + share)
    rows2 = g1_a.shape[2] // 2
    parts = []
    for c in range(g1_a.shape[1] // 2):
        total = g1_b[0, 2 * c, pl.ds(0, rows2, stride=2), :]
        total = total + g1_b[0, 2 * c, pl.ds(1, rows2, stride=2), :]
        total = total + g1_b[0, 2 * c + 1, pl.ds(0, rows2, stride=2), :]
        total = total + g1_b[0, 2 * c + 1, pl.ds(1, rows2, stride=2), :]
        parts.append(total)
    even = jnp.concatenate(parts[0::2], axis=0)
    odd = jnp.concatenate(parts[1::2], axis=0)
    g2 = dot(even, one_hot(lambda r, c: c == r // 2))
    g2 = g2 + dot(odd, one_hot(lambda r, c: c == 64 + r // 2))
    g2 = g2 * (0.125 / 343.0)
    size = g2.shape[0]
    far[...] = g2
    up[0:size] = g2
    down[0:size] = g2
    up[size:] = pack_lanes(lambda c: g1[c], share, 89, 9, 10, rows1)[0]
    down[size:] = pack_lanes(lambda c: g1[c], share, 30, 9, 10, rows1)[0]


def gather_z_kernel(count, *refs):
    own, g1, received, (g2_out, g1_out) = refs[0], refs[1], refs[2 : 1 + count], refs[1 + count :]
    size = own.shape[0]
    period = 32 * count
    rows2 = 16
    tiles, planes = g2_out.shape[0], g2_out.shape[1]
    lane = iota((size, LANES), 1)
    for parity in range(2):
        totals = [jnp.zeros((size, LANES), F32) for _ in range(tiles)]
        for o in range(count):
            value = own[...] if o == 0 else received[o - 1][0:size]
            shift = (32 * o - 64 * parity) % LANES
            turned = pltpu.roll(value, shift, 1) if shift else value
            position = ((lane - shift) & (LANES - 1)) - 64 * parity
            inside = (position >= 0) & (position < 64)
            for t in range(tiles):
                lands = lax.rem(position + (32 * o + period), period) == lane + LANES * t
                totals[t] = totals[t] + jnp.where(inside & lands, turned, 0.0)
        for t in range(tiles):
            for k in range(planes // 2):
                g2_out[t, 2 * k + parity] = totals[t][rows2 * k : rows2 * (k + 1)]
    above = received[0][size:]
    below = received[count - 2][size:]
    rows1 = g1.shape[1]
    for c in range(g1.shape[0]):
        value = g1[c] + unpacked(below, c, 10, 0, 9, 25, rows1)
        g1_out[c] = value + unpacked(above, c, 10, 0, 9, 94, rows1)


def fold_x_kernel(count, *refs):
    shares, out = refs[:count], refs[count]
    tiles, period = out.shape[0], out.shape[1]
    for t in range(tiles):
        for x in range(period):
            total = None
            for o in range(count):
                for c in range(10):
                    if (c - 3 + 4 * o) % period == x:
                        value = shares[o][t, c]
                        total = value if total is None else total + value
            out[t, x] = total


def window_x_kernel(sources, *refs):
    inputs, (out, down, up) = refs[:-3], refs[-3:]
    planes = out.shape[0]
    for p in range(planes):
        total = None
        for index, offset, first, length in sources:
            k = p - 7 - 8 * offset + 2 - first
            inside = 0 <= p - 7 - 8 * offset + 2 < 12
            if inside and 0 <= k < length:
                value = inputs[index][k]
                total = value if total is None else total + value
        out[p] = total
        down[p] = total[2:10]
        up[p] = total[13:21]
        down[planes + p // 8, p % 8 : p % 8 + 1] = total[10:11]
        up[planes + p // 8, p % 8 : p % 8 + 1] = total[21:22]


def fine_tail_kernel(g1, above, below, out, base, first, second):
    planes, rows1 = g1.shape[0], g1.shape[1]

    for p in range(planes):
        base[0, p] = jnp.zeros(base.shape[2:], F32)
        base[0, p, 4 : 4 + rows1] = g1[p]
        base[0, p, 22:30] = base[0, p, 22:30] + above[p]
        base[0, p, 1:9] = base[0, p, 1:9] + below[p]
        ninth = p % 8
        base[0, p, 30:31] = base[0, p, 30:31] + above[planes + p // 8, ninth : ninth + 1]
        base[0, p, 9:10] = base[0, p, 9:10] + below[planes + p // 8, ninth : ninth + 1]
    seventh = 1.0 / 7.0
    sweep(first, base, 1, planes - 1, base, seventh)
    sweep(second, first, 2, planes - 2, base, seventh)
    sweep(first, second, 3, planes - 3, base, seventh)
    sweep(second, first, 4, planes - 4, base, seventh)
    sweep(first, second, 5, planes - 5, base, seventh)
    for c in range(out.shape[0]):
        out[c] = first[0, 5 + c] * weight(1)


def restrict_lanes(values, width, coarse_width, coarse_tiles):
    out = []
    for s in range(coarse_tiles):
        total = None
        for t, value in enumerate(values):
            matrix = one_hot(
                lambda r, c: ((LANES * t + r) // 2 == lax.rem(LANES * s + c, coarse_width))
                & (LANES * t + r < width)
            )
            term = dot(value, matrix)
            total = term if total is None else total + term
        out.append(total)
    return out


def prolong_lanes(values, width, fine_tiles):
    out = []
    for s in range(fine_tiles):
        total = None
        for t, value in enumerate(values):
            matrix = one_hot(lambda r, c: LANES * t + r == lax.rem(LANES * s + c, width) // 2)
            term = dot(value, matrix)
            total = term if total is None else total + term
        out.append(total)
    return out


def solve(level, width, buffers):
    g, a, b = buffers[level]
    tiles, planes, rows = g.shape[0], g.shape[1], g.shape[2]
    seventh = 1.0 / 7.0
    if level == LEVELS - 1:
        source = [[g[t, p] for t in range(tiles)] for p in range(planes)]

        def step(iteration, carry):
            out = []
            for p in range(planes):
                v = carry[p]
                total = v + carry[(p + 1) % planes] + carry[(p - 1) % planes]
                total = total + (pltpu.roll(v, 1, 0) + pltpu.roll(v, rows - 1, 0))
                total = total + (pltpu.roll(v, 1, 1) + pltpu.roll(v, LANES - 1, 1))
                out.append(source[p][0] + total * seventh)
            return tuple(out)

        start = tuple(source[p][0] for p in range(planes))
        final = lax.fori_loop(0, COARSE_ITERS - 1, step, start)
        for p in range(planes):
            g[0, p] = final[p] * weight(level)
        return
    w = weight(level)
    coarse = buffers[level + 1][0]
    sweep(a, g, 0, planes, None, seventh, planes)
    sweep(b, a, 0, planes, None, seventh, planes)
    for t in range(tiles):
        for p in range(planes):
            g[t, p] = (g[t, p] + a[t, p] + b[t, p]) * w
    sweep(a, b, 0, planes, None, seventh, planes)
    half = rows // 2
    values = []
    for t in range(tiles):
        parts = []
        for c in range(planes // 2):
            total = a[t, 2 * c, pl.ds(0, half, stride=2), :]
            total = total + a[t, 2 * c, pl.ds(1, half, stride=2), :]
            total = total + a[t, 2 * c + 1, pl.ds(0, half, stride=2), :]
            total = total + a[t, 2 * c + 1, pl.ds(1, half, stride=2), :]
            parts.append(total)
        values.append(jnp.concatenate(parts, axis=0))
    values = restrict_lanes(values, width, width // 2, coarse.shape[0])
    for t, value in enumerate(values):
        for c in range(planes // 2):
            coarse[t, c] = value[half * c : half * (c + 1)] * 0.125
    solve(level + 1, width // 2, buffers)
    values = [
        jnp.concatenate([coarse[t, c] for c in range(planes // 2)], axis=0)
        for t in range(coarse.shape[0])
    ]
    values = prolong_lanes(values, width, tiles)
    for t, value in enumerate(values):
        for c in range(planes // 2):
            part = value[half * c : half * (c + 1)]
            for p in (2 * c, 2 * c + 1):
                b[t, p, pl.ds(0, half, stride=2), :] = part
                b[t, p, pl.ds(1, half, stride=2), :] = part
        for p in range(planes):
            b[t, p] = b[t, p] + g[t, p]
    sweep(a, b, 0, planes, None, seventh, planes)
    sweep(b, a, 0, planes, None, seventh, planes)
    sweep(a, b, 0, planes, None, seventh, planes)
    for t in range(tiles):
        for p in range(planes):
            g[t, p] = g[t, p] + a[t, p]


def coarse_kernel(count, *refs):
    shares, out, scratch = refs[:count], refs[count], refs[count + 1 :]
    buffers = {level: scratch[3 * (level - 2) : 3 * (level - 1)] for level in (2, 3, 4)}
    g = buffers[2][0]
    tiles, planes = g.shape[0], g.shape[1]
    for t in range(tiles):
        for p in range(planes):
            for b in range(count):
                value = shares[b][t, p, 0:8] + shares[(b - 1) % count][t, p, 8:16]
                g[t, p, 8 * b : 8 * b + 8] = value
    solve(2, LANES * tiles, buffers)
    for c in range(out.shape[0]):
        out[c] = g[0, (c - 3) % planes, 0:16]


def finish_kernel(field, e2, f1, f0, below, above, out, u1_a, u1_b, u0_a, u0_b, pot):
    share2 = e2.shape[0]
    rows2 = e2.shape[1]
    value = e2[...].reshape(share2 * rows2, LANES)
    value = dot(value, one_hot(lambda r, c: r == c // 2))
    for c in range(share2):
        part = value[rows2 * c : rows2 * (c + 1)]
        for p in (2 * c, 2 * c + 1):
            u1_a[0, p, pl.ds(0, rows2, stride=2), :] = part
            u1_a[0, p, pl.ds(1, rows2, stride=2), :] = part
    count1 = 2 * share2
    sweep(u1_b, u1_a, 1, count1 - 1)
    sweep(u1_a, u1_b, 2, count1 - 2)
    sweep(u1_b, u1_a, 3, count1 - 3)
    share1 = f1.shape[0]
    rows1 = 24
    parts = []
    for c in range(share1):
        parts.append(f1[c, 4 : 4 + rows1] + u1_b[0, 4 + c, 4 : 4 + rows1] * (1.0 / 343.0))
    value = jnp.concatenate(parts, axis=0)
    main = dot(value, one_hot(lambda r, c: r == 32 + c // 2))
    side = dot(value, one_hot(lambda r, c: r == jnp.where(c < 64, 96 + c // 2, c // 2 - 32)))
    for t, value in enumerate((main, side)):
        for c in range(share1):
            part = value[rows1 * c : rows1 * (c + 1)]
            for p in (2 * c, 2 * c + 1):
                u0_a[t, p, pl.ds(0, rows1, stride=2), :] = part
                u0_a[t, p, pl.ds(1, rows1, stride=2), :] = part
    count0 = 2 * share1
    sweep(u0_b, u0_a, 1, count0 - 1)
    sweep(u0_a, u0_b, 2, count0 - 2)
    sweep(u0_b, u0_a, 3, count0 - 3)

    planes, rows = field.shape[1], field.shape[2]
    scale = 1.0 / 343.0
    for i in range(planes + 1):
        value = u0_b[0, 4 + i, ROW0 : ROW0 + rows] * scale + f0[fine_plane(i)]
        if i <= SPILL:
            value = value + below[2 + i]
        if i >= planes - SPILL:
            value = value + above[i - (planes - SPILL)]
        pot[i, 0:rows] = value
        edge = u0_b[0, 4 + i, ROW0 + rows : ROW0 + rows + 1] * scale
        if i < planes:
            edge = edge + f0[6, i + SPILL : i + SPILL + 1]
            if i <= SPILL:
                edge = edge + below[0, i + SPILL + planes : i + SPILL + planes + 1]
            if i >= planes - SPILL:
                edge = edge + above[6, i + SPILL - planes : i + SPILL - planes + 1]
            pot[i, rows : rows + 1] = edge
    column = f0[7] + pltpu.roll(below[1], LANES - planes, 1) + pltpu.roll(above[7], planes, 1)
    lane = iota((rows, LANES), 1)
    for i in range(planes):
        here = pot[i, 0:rows]
        out[0, i] = field[0, i] - (pot[i + 1, 0:rows] - here)
        out[1, i] = field[1, i] - (pot[i, 1 : rows + 1] - here)
        beyond = pltpu.roll(u0_b[1, 4 + i, ROW0 : ROW0 + rows], LANES - 1, 1) * scale
        beyond = beyond + pltpu.roll(column, LANES - 1 - (i + SPILL), 1)
        next_z = jnp.where(lane == LANES - 1, beyond, pltpu.roll(here, LANES - 1, 1))
        out[2, i] = field[2, i] - (next_z - here)


def fine_plane(i):
    return i + SPILL if i <= 0 else i + SPILL + 2


def fine_share_kernel(field, after, main, up, down, base, first, second):
    planes = field.shape[1]
    count = base.shape[1]
    edge = [p for p in range(count) if p < PLANE0 or p > PLANE0 + planes]
    clear_planes(base, edge)
    clear_planes(first, edge)
    clear_planes(second, edge)
    fill_source(field, base)
    low, high = PLANE0, PLANE0 + planes + 1
    seventh = 1.0 / 7.0
    sweep(first, base, low - 1, high + 1, base, seventh)
    sweep(second, first, low - 2, high + 2, base, seventh)
    sweep(first, second, low - 3, high + 3, base, seventh)
    sweep(second, first, low - 4, high + 4, base, seventh)
    sweep(first, second, low - 5, high + 5, base, seventh)
    share, rows = main.shape[0], main.shape[1]

    for p in range(share):
        main[p] = first[0, p + 1] * weight(0)

    def read_up(p):
        return first[1, p + 1]

    def read_down(p):
        lane = iota((rows, LANES), 1)
        turned = pltpu.roll(first[1, p + 1], SPILL, 1)
        return jnp.where(lane == SPILL, pltpu.roll(first[0, p + 1], SPILL, 1), turned)

    for k, packed in enumerate(pack_lanes(read_up, share, 0, 6, 8, rows)):
        up[k] = packed * weight(0)
    for k, packed in enumerate(pack_lanes(read_down, share, 0, 6, 8, rows)):
        down[k] = packed * weight(0)


def fine_z_kernel(main, own, above, below, out, column_out, down, up):
    share, rows = main.shape[0], main.shape[1]
    lane = iota((rows, LANES), 1)
    column = jnp.zeros((rows, LANES), F32)
    for p in range(share):
        tile, k = p // 16, p % 16
        value = main[p] + unpacked(below[tile], k, 8, 0, 6, 0, rows)
        value = value + unpacked(above[tile], k, 8, 0, 5, LANES - 5, rows)
        out[p] = value
        turned = pltpu.roll(own[tile], (p - 8 * k) % LANES, 1)
        turned = turned + pltpu.roll(above[tile], (p - 8 * k - 5) % LANES, 1)
        column = jnp.where(lane == p, turned, column)
        down[p] = value[1:9]
        up[p] = value[40:48]
    column_out[...] = column
    down[share] = column[1:9]
    up[share] = column[40:48]


def fine_y_kernel(main, column, above, below, out, work):
    share = main.shape[0]
    rows = out.shape[1]

    def folded(k, value):
        work[...] = value
        work[33:41] = work[33:41] + above[k]
        work[8:16] = work[8:16] + below[k]

    out[6] = jnp.zeros((rows, LANES), F32)
    for p in range(share):
        folded(p, main[p])
        place = p if p <= SPILL else p + 2
        out[place] = work[ROW0 : ROW0 + rows]
        out[6, p : p + 1] = work[ROW0 + rows : ROW0 + rows + 1]
    folded(share, column[...])
    out[7] = work[ROW0 : ROW0 + rows]


def body(field):
    nx, ny, nz = field.shape[1:]
    size_x, size_y, size_z = lax.axis_size("gx"), lax.axis_size("gy"), lax.axis_size("gz")
    n1 = nx // 2
    share1 = n1 + 4
    rows0 = ny + 16
    rows1 = ny // 2 + 8
    planes0 = nx + 13

    def from_offset(value, axis, offset):
        count = lax.axis_size(axis)
        pairs = [(source, (source - offset) % count) for source in range(count)]
        return lax.ppermute(value, axis, pairs)

    level0 = (2, planes0, rows0, LANES)
    level1 = (1, n1 + 12, ny // 2 + 16, LANES)
    packed = ((n1 // 2 + 6) // 2) * 16
    up, down, far, g1 = call(
        spread_kernel,
        [shape(packed + rows1, LANES), shape(packed + rows1, LANES), shape(packed, LANES),
         shape(share1, rows1, LANES)],
        [level0, level0, level1, level1],
        6_000_000,
        field,
    )
    received = []
    for o in range(1, size_z):
        message = down if o == 1 else (up if o == size_z - 1 else far)
        received.append(from_offset(message, "gz", o))
    share0 = nx + 11
    main, f_up, f_down = call(
        fine_share_kernel,
        [shape(share0, rows0, LANES), shape(2, rows0, LANES), shape(2, rows0, LANES)],
        [level0, level0, level0],
        20_000_000,
        field, far,
    )
    f_above = from_offset(f_down, "gz", 1)
    f_below = from_offset(f_up, "gz", -1)

    tiles = size_z * 32 // LANES
    g2, g1 = call(
        functools.partial(gather_z_kernel, size_z),
        [shape(tiles, n1 // 2 + 6, 16, LANES), shape(share1, rows1, LANES)],
        [],
        500_000,
        far, g1, *received,
    )
    shares = [g2] + [from_offset(g2, "gx", o) for o in range(1, size_x)]
    inputs = [g1]
    sources = [(0, 0, 0, share1)]
    spans = {1: (0, 9), -1: (3, 12), 2: (0, 1), -2: (11, 12)}
    residues = {}
    for offset, span in spans.items():
        residues.setdefault(offset % size_x, []).append((offset, span))
    for residue, members in residues.items():
        if residue == 0:
            sources.extend((0, offset, 0, share1) for offset, span in members)
            continue
        first = min(span[0] for offset, span in members)
        last = max(span[1] for offset, span in members)
        inputs.append(from_offset(g1[first:last], "gx", residue))
        sources.extend((len(inputs) - 1, offset, first, last - first) for offset, span in members)
    g2 = call(
        functools.partial(fold_x_kernel, size_x),
        shape(tiles, 4 * size_x, 16, LANES),
        [],
        100_000,
        *shares,
    )
    planes1 = n1 + 14
    extra = -(-planes1 // 8)
    g1, g1_down, g1_up = call(
        functools.partial(window_x_kernel, tuple(sources)),
        [shape(planes1, rows1, LANES), shape(planes1 + extra, 8, LANES),
         shape(planes1 + extra, 8, LANES)],
        [],
        100_000,
        *inputs,
    )
    shares = [g2] + [from_offset(g2, "gy", o) for o in range(1, size_y)]
    g1_above = from_offset(g1_down, "gy", 1)
    g1_below = from_offset(g1_up, "gy", -1)

    main, column, f_down, f_up = call(
        fine_z_kernel,
        [shape(share0, rows0, LANES), shape(rows0, LANES), shape(share0 + 1, 8, LANES),
         shape(share0 + 1, 8, LANES)],
        [],
        1_000_000,
        main, f_up, f_above, f_below,
    )
    f_above = from_offset(f_down, "gy", 1)
    f_below = from_offset(f_up, "gy", -1)
    f0 = call(
        fine_y_kernel,
        shape(share0 + 2, ny, LANES),
        [(rows0, LANES)],
        500_000,
        main, column, f_above, f_below,
    )
    f_down, f_up = f0[0:8], jnp.concatenate([f0[6:8], f0[share0 + 2 - 6 :]], axis=0)
    if size_x == 2:
        other = from_offset(jnp.concatenate([f_down, f_up[2:]], axis=0), "gx", 1)
        f_above, f_below = other[0:8], jnp.concatenate([other[6:8], other[8:]], axis=0)
    else:
        f_above = from_offset(f_down, "gx", 1)
        f_below = from_offset(f_up, "gx", -1)

    scratch = []
    for level in (2, 3, 4):
        cut = 2 ** (level - 2)
        extent = (max(1, tiles // cut), 4 * size_x // cut, 8 * size_y // cut, LANES)
        scratch.extend([extent] * 3)
    e2 = call(
        functools.partial(coarse_kernel, size_y),
        shape(n1 // 2 + 6, 16, LANES),
        scratch,
        5_000_000,
        *shares,
    )
    window = (1, planes1, ny // 2 + 16, LANES)
    f1 = call(
        fine_tail_kernel,
        shape(share1, ny // 2 + 16, LANES),
        [window, window, window],
        3_000_000,
        g1, g1_above, g1_below,
    )
    return call(
        finish_kernel,
        shape(*field.shape),
        [level1, level1, (2, nx + 8, rows0, LANES), (2, nx + 8, rows0, LANES),
         (nx + 1, ny + 8, LANES)],
        6_000_000,
        field, e2, f1, f0, f_below, f_above,
    )


def solution(mesh):
    in_specs = (P(None, "gx", "gy", "gz"),)
    out_specs = P(None, "gx", "gy", "gz")
    return jax.shard_map(body, mesh=mesh, in_specs=in_specs, out_specs=out_specs, check_vma=False)
```

```python
import functools

import jax
import jax.numpy as jnp
from jax import lax
from jax.experimental import pallas as pl
from jax.experimental.pallas import tpu as pltpu
from jax.sharding import PartitionSpec as P

LEVELS = 5
SWEEPS = 3
COARSE_ITERS = 24


F32 = jnp.float32
LANES = 128
VMEM_LIMIT = 16 * 1024 * 1024
PEAK_FLOPS_PER_US = 1.15e9


def weight(level):
    return 4.0**level / 7.0


def shape(*extent):
    return jax.ShapeDtypeStruct(extent, F32)


def call(kernel, outs, scratch, microseconds, *args):
    flops = int(microseconds * PEAK_FLOPS_PER_US)
    return pl.pallas_call(
        kernel,
        out_shape=outs,
        scratch_shapes=[pltpu.VMEM(s, F32) for s in scratch],
        compiler_params=pltpu.CompilerParams(vmem_limit_bytes=VMEM_LIMIT),
        cost_estimate=pl.CostEstimate(flops=flops, bytes_accessed=0, transcendentals=0),
    )(*args)


def iota(extent, dim):
    return lax.broadcasted_iota(jnp.int32, extent, dim)


def one_hot(condition):
    rows = iota((LANES, LANES), 0)
    columns = iota((LANES, LANES), 1)
    return jnp.where(condition(rows, columns), 1.0, 0.0).astype(F32)


def dot(left, right):
    return lax.dot_general(
        left,
        right,
        (((1,), (0,)), ((), ())),
        precision=lax.Precision.HIGHEST,
        preferred_element_type=F32,
    )


def seven_sum(source, plane, below, above):
    tiles = source.shape[0]
    rows = source.shape[2]
    center = [source[t, plane] for t in range(tiles)]
    left = [pltpu.roll(v, 1, 1) for v in center]
    right = [pltpu.roll(v, LANES - 1, 1) for v in center]
    if tiles > 1:
        lane = iota((rows, LANES), 1)
        left = [jnp.where(lane == 0, left[t - 1], left[t]) for t in range(tiles)]
        right = [
            jnp.where(lane == LANES - 1, right[(t + 1) % tiles], right[t]) for t in range(tiles)
        ]
    out = []
    for t in range(tiles):
        v = center[t]
        total = v + (source[t, below] + source[t, above])
        total = total + (pltpu.roll(v, 1, 0) + pltpu.roll(v, rows - 1, 0))
        out.append(total + (left[t] + right[t]))
    return out


def sweep(target, source, low, high, base=None, scale=None, period=None):
    for plane in range(low, high):
        below, above = plane - 1, plane + 1
        if period is not None:
            below, above = below % period, above % period
        for t, value in enumerate(seven_sum(source, plane, below, above)):
            if scale is not None:
                value = value * scale
            if base is not None:
                value = value + base[t, plane]
            target[t, plane] = value


PLANE0 = 6
ROW0 = 8
SPILL = 5


def fill_source(field, target):
    planes, rows = field.shape[1], field.shape[2]
    lane = iota((rows, LANES), 1)
    row = iota((rows, LANES), 0)
    row8 = iota((8, LANES), 0)
    zero8 = jnp.zeros((8, LANES), F32)
    zeros = jnp.zeros((rows, LANES), F32)

    def one_plane(i, before):
        along_x, along_y, along_z = field[0, i], field[1, i], field[2, i]
        value = before - along_x - along_y - along_z
        value = value + jnp.where(row == 0, 0.0, pltpu.roll(along_y, 1, 0))
        turned = pltpu.roll(along_z, 1, 1)
        value = value + jnp.where(lane == 0, 0.0, turned)
        p = PLANE0 + i
        target[0, p, 0:ROW0] = zero8
        target[0, p, ROW0 : ROW0 + rows] = value
        last = pltpu.roll(along_y[rows - 8 : rows], 1, 0)
        target[0, p, ROW0 + rows : ROW0 + rows + 8] = jnp.where(row8 == 0, last, 0.0)
        target[1, p, 0:ROW0] = zero8
        target[1, p, ROW0 : ROW0 + rows] = jnp.where(lane == 0, turned, 0.0)
        target[1, p, ROW0 + rows : ROW0 + rows + 8] = zero8

    for i in range(planes):
        one_plane(i, field[0, i - 1] if i else zeros)
    p = PLANE0 + planes
    target[0, p] = jnp.zeros(target.shape[2:], F32)
    target[1, p] = jnp.zeros(target.shape[2:], F32)
    target[0, p, ROW0 : ROW0 + rows] = field[0, planes - 1]


def clear_planes(target, planes):
    for t in range(target.shape[0]):
        for p in planes:
            target[t, p] = jnp.zeros(target.shape[2:], F32)


def pack_lanes(read, count, first, width, spacing, rows):
    lane = iota((rows, LANES), 1)
    per_tile = LANES // spacing
    tiles = []
    for start in range(0, count, per_tile):
        packed = jnp.zeros((rows, LANES), F32)
        for k in range(min(per_tile, count - start)):
            turned = pltpu.roll(read(start + k), (spacing * k - first) % LANES, 1)
            inside = (lane >= spacing * k) & (lane < spacing * k + width)
            packed = jnp.where(inside, turned, packed)
        tiles.append(packed)
    return tiles


def unpacked(packed, k, spacing, offset, width, first, rows):
    lane = iota((rows, LANES), 1)
    turned = pltpu.roll(packed, (first - spacing * k - offset) % LANES, 1)
    inside = (lane >= first) & (lane < first + width)
    return jnp.where(inside, turned, 0.0)


def spread_kernel(field, up, down, far, g1_out, first, second, g1_a, g1_b):
    planes = field.shape[1]
    count = first.shape[1]
    edge = [p for p in range(count) if p < PLANE0 or p > PLANE0 + planes]
    clear_planes(first, edge)
    clear_planes(second, edge)
    fill_source(field, first)
    low, high = PLANE0, PLANE0 + planes + 1
    sweep(second, first, low - 1, high + 1)
    sweep(first, second, low - 2, high + 2)
    sweep(second, first, low - 3, high + 3)

    n1 = planes // 2
    rows1 = first.shape[2] // 2
    pieces = []
    for t in range(2):
        parts = []
        for c in range(-2, n1 + 2):
            p = PLANE0 + 2 * c
            total = second[t, p, pl.ds(0, rows1, stride=2), :]
            total = total + second[t, p, pl.ds(1, rows1, stride=2), :]
            total = total + second[t, p + 1, pl.ds(0, rows1, stride=2), :]
            total = total + second[t, p + 1, pl.ds(1, rows1, stride=2), :]
            parts.append(total)
        pieces.append(jnp.concatenate(parts, axis=0))
    main = one_hot(lambda r, c: c == 32 + r // 2)
    side = one_hot(lambda r, c: c == jnp.where(r < 64, 96 + r // 2, r // 2 - 32))
    g1 = (dot(pieces[0], main) + dot(pieces[1], side)) * (0.125 / 343.0)
    share = n1 + 4
    g1 = g1.reshape(share, rows1, LANES)
    g1_out[...] = g1

    clear_planes(g1_a, range(g1_a.shape[1]))
    clear_planes(g1_b, range(g1_b.shape[1]))
    for c in range(share):
        g1_a[0, 4 + c, 4 : 4 + rows1] = g1[c]
    sweep(g1_b, g1_a, 3, 5 + share)
    sweep(g1_a, g1_b, 2, 6 + share)
    sweep(g1_b, g1_a, 1, 7 + share)
    rows2 = g1_a.shape[2] // 2
    parts = []
    for c in range(g1_a.shape[1] // 2):
        total = g1_b[0, 2 * c, pl.ds(0, rows2, stride=2), :]
        total = total + g1_b[0, 2 * c, pl.ds(1, rows2, stride=2), :]
        total = total + g1_b[0, 2 * c + 1, pl.ds(0, rows2, stride=2), :]
        total = total + g1_b[0, 2 * c + 1, pl.ds(1, rows2, stride=2), :]
        parts.append(total)
    even = jnp.concatenate(parts[0::2], axis=0)
    odd = jnp.concatenate(parts[1::2], axis=0)
    g2 = dot(even, one_hot(lambda r, c: c == r // 2))
    g2 = g2 + dot(odd, one_hot(lambda r, c: c == 64 + r // 2))
    g2 = g2 * (0.125 / 343.0)
    size = g2.shape[0]
    far[...] = g2
    up[0:size] = g2
    down[0:size] = g2
    up[size:] = pack_lanes(lambda c: g1[c], share, 89, 9, 10, rows1)[0]
    down[size:] = pack_lanes(lambda c: g1[c], share, 30, 9, 10, rows1)[0]


def gather_z_kernel(count, *refs):
    own, g1, received, (g2_out, g1_out) = refs[0], refs[1], refs[2 : 1 + count], refs[1 + count :]
    size = own.shape[0]
    period = 32 * count
    rows2 = 16
    tiles, planes = g2_out.shape[0], g2_out.shape[1]
    lane = iota((size, LANES), 1)
    for parity in range(2):
        totals = [jnp.zeros((size, LANES), F32) for _ in range(tiles)]
        for o in range(count):
            value = own[...] if o == 0 else received[o - 1][0:size]
            shift = (32 * o - 64 * parity) % LANES
            turned = pltpu.roll(value, shift, 1) if shift else value
            position = ((lane - shift) & (LANES - 1)) - 64 * parity
            inside = (position >= 0) & (position < 64)
            for t in range(tiles):
                lands = lax.rem(position + (32 * o + period), period) == lane + LANES * t
                totals[t] = totals[t] + jnp.where(inside & lands, turned, 0.0)
        for t in range(tiles):
            for k in range(planes // 2):
                g2_out[t, 2 * k + parity] = totals[t][rows2 * k : rows2 * (k + 1)]
    above = received[0][size:]
    below = received[count - 2][size:]
    rows1 = g1.shape[1]
    for c in range(g1.shape[0]):
        value = g1[c] + unpacked(below, c, 10, 0, 9, 25, rows1)
        g1_out[c] = value + unpacked(above, c, 10, 0, 9, 94, rows1)


def fold_x_kernel(count, *refs):
    shares, out = refs[:count], refs[count]
    tiles, period = out.shape[0], out.shape[1]
    for t in range(tiles):
        for x in range(period):
            total = None
            for o in range(count):
                for c in range(10):
                    if (c - 3 + 4 * o) % period == x:
                        value = shares[o][t, c]
                        total = value if total is None else total + value
            out[t, x] = total


def window_x_kernel(sources, *refs):
    inputs, (out, down, up) = refs[:-3], refs[-3:]
    planes = out.shape[0]
    for p in range(planes):
        total = None
        for index, offset, first, length in sources:
            k = p - 7 - 8 * offset + 2 - first
            inside = 0 <= p - 7 - 8 * offset + 2 < 12
            if inside and 0 <= k < length:
                value = inputs[index][k]
                total = value if total is None else total + value
        out[p] = total
        down[p] = total[2:10]
        up[p] = total[13:21]
        down[planes + p // 8, p % 8 : p % 8 + 1] = total[10:11]
        up[planes + p // 8, p % 8 : p % 8 + 1] = total[21:22]


def fine_tail_kernel(g1, above, below, out, base, first, second):
    planes, rows1 = g1.shape[0], g1.shape[1]

    for p in range(planes):
        base[0, p] = jnp.zeros(base.shape[2:], F32)
        base[0, p, 4 : 4 + rows1] = g1[p]
        base[0, p, 22:30] = base[0, p, 22:30] + above[p]
        base[0, p, 1:9] = base[0, p, 1:9] + below[p]
        ninth = p % 8
        base[0, p, 30:31] = base[0, p, 30:31] + above[planes + p // 8, ninth : ninth + 1]
        base[0, p, 9:10] = base[0, p, 9:10] + below[planes + p // 8, ninth : ninth + 1]
    seventh = 1.0 / 7.0
    sweep(first, base, 1, planes - 1, base, seventh)
    sweep(second, first, 2, planes - 2, base, seventh)
    sweep(first, second, 3, planes - 3, base, seventh)
    sweep(second, first, 4, planes - 4, base, seventh)
    sweep(first, second, 5, planes - 5, base, seventh)
    for c in range(out.shape[0]):
        out[c] = first[0, 5 + c] * weight(1)


def restrict_lanes(values, width, coarse_width, coarse_tiles):
    out = []
    for s in range(coarse_tiles):
        total = None
        for t, value in enumerate(values):
            matrix = one_hot(
                lambda r, c: ((LANES * t + r) // 2 == lax.rem(LANES * s + c, coarse_width))
                & (LANES * t + r < width)
            )
            term = dot(value, matrix)
            total = term if total is None else total + term
        out.append(total)
    return out


def prolong_lanes(values, width, fine_tiles):
    out = []
    for s in range(fine_tiles):
        total = None
        for t, value in enumerate(values):
            matrix = one_hot(lambda r, c: LANES * t + r == lax.rem(LANES * s + c, width) // 2)
            term = dot(value, matrix)
            total = term if total is None else total + term
        out.append(total)
    return out


def solve(level, width, buffers):
    g, a, b = buffers[level]
    tiles, planes, rows = g.shape[0], g.shape[1], g.shape[2]
    seventh = 1.0 / 7.0
    if level == LEVELS - 1:
        source = [[g[t, p] for t in range(tiles)] for p in range(planes)]

        def step(iteration, carry):
            out = []
            for p in range(planes):
                v = carry[p]
                total = v + carry[(p + 1) % planes] + carry[(p - 1) % planes]
                total = total + (pltpu.roll(v, 1, 0) + pltpu.roll(v, rows - 1, 0))
                total = total + (pltpu.roll(v, 1, 1) + pltpu.roll(v, LANES - 1, 1))
                out.append(source[p][0] + total * seventh)
            return tuple(out)

        start = tuple(source[p][0] for p in range(planes))
        final = lax.fori_loop(0, COARSE_ITERS - 1, step, start)
        for p in range(planes):
            g[0, p] = final[p] * weight(level)
        return
    w = weight(level)
    coarse = buffers[level + 1][0]
    sweep(a, g, 0, planes, None, seventh, planes)
    sweep(b, a, 0, planes, None, seventh, planes)
    for t in range(tiles):
        for p in range(planes):
            g[t, p] = (g[t, p] + a[t, p] + b[t, p]) * w
    sweep(a, b, 0, planes, None, seventh, planes)
    half = rows // 2
    values = []
    for t in range(tiles):
        parts = []
        for c in range(planes // 2):
            total = a[t, 2 * c, pl.ds(0, half, stride=2), :]
            total = total + a[t, 2 * c, pl.ds(1, half, stride=2), :]
            total = total + a[t, 2 * c + 1, pl.ds(0, half, stride=2), :]
            total = total + a[t, 2 * c + 1, pl.ds(1, half, stride=2), :]
            parts.append(total)
        values.append(jnp.concatenate(parts, axis=0))
    values = restrict_lanes(values, width, width // 2, coarse.shape[0])
    for t, value in enumerate(values):
        for c in range(planes // 2):
            coarse[t, c] = value[half * c : half * (c + 1)] * 0.125
    solve(level + 1, width // 2, buffers)
    values = [
        jnp.concatenate([coarse[t, c] for c in range(planes // 2)], axis=0)
        for t in range(coarse.shape[0])
    ]
    values = prolong_lanes(values, width, tiles)
    for t, value in enumerate(values):
        for c in range(planes // 2):
            part = value[half * c : half * (c + 1)]
            for p in (2 * c, 2 * c + 1):
                b[t, p, pl.ds(0, half, stride=2), :] = part
                b[t, p, pl.ds(1, half, stride=2), :] = part
        for p in range(planes):
            b[t, p] = b[t, p] + g[t, p]
    sweep(a, b, 0, planes, None, seventh, planes)
    sweep(b, a, 0, planes, None, seventh, planes)
    sweep(a, b, 0, planes, None, seventh, planes)
    for t in range(tiles):
        for p in range(planes):
            g[t, p] = g[t, p] + a[t, p]


def coarse_kernel(count, *refs):
    shares, out, scratch = refs[:count], refs[count], refs[count + 1 :]
    buffers = {level: scratch[3 * (level - 2) : 3 * (level - 1)] for level in (2, 3, 4)}
    g = buffers[2][0]
    tiles, planes = g.shape[0], g.shape[1]
    for t in range(tiles):
        for p in range(planes):
            for b in range(count):
                value = shares[b][t, p, 0:8] + shares[(b - 1) % count][t, p, 8:16]
                g[t, p, 8 * b : 8 * b + 8] = value
    solve(2, LANES * tiles, buffers)
    for c in range(out.shape[0]):
        out[c] = g[0, (c - 3) % planes, 0:16]


def finish_kernel(field, e2, f1, f0, below, above, out, u1_a, u1_b, u0_a, u0_b, pot):
    share2 = e2.shape[0]
    rows2 = e2.shape[1]
    value = e2[...].reshape(share2 * rows2, LANES)
    value = dot(value, one_hot(lambda r, c: r == c // 2))
    for c in range(share2):
        part = value[rows2 * c : rows2 * (c + 1)]
        for p in (2 * c, 2 * c + 1):
            u1_a[0, p, pl.ds(0, rows2, stride=2), :] = part
            u1_a[0, p, pl.ds(1, rows2, stride=2), :] = part
    count1 = 2 * share2
    sweep(u1_b, u1_a, 1, count1 - 1)
    sweep(u1_a, u1_b, 2, count1 - 2)
    sweep(u1_b, u1_a, 3, count1 - 3)
    share1 = f1.shape[0]
    rows1 = 24
    parts = []
    for c in range(share1):
        parts.append(f1[c, 4 : 4 + rows1] + u1_b[0, 4 + c, 4 : 4 + rows1] * (1.0 / 343.0))
    value = jnp.concatenate(parts, axis=0)
    main = dot(value, one_hot(lambda r, c: r == 32 + c // 2))
    side = dot(value, one_hot(lambda r, c: r == jnp.where(c < 64, 96 + c // 2, c // 2 - 32)))
    for t, value in enumerate((main, side)):
        for c in range(share1):
            part = value[rows1 * c : rows1 * (c + 1)]
            for p in (2 * c, 2 * c + 1):
                u0_a[t, p, pl.ds(0, rows1, stride=2), :] = part
                u0_a[t, p, pl.ds(1, rows1, stride=2), :] = part
    count0 = 2 * share1
    sweep(u0_b, u0_a, 1, count0 - 1)
    sweep(u0_a, u0_b, 2, count0 - 2)
    sweep(u0_b, u0_a, 3, count0 - 3)

    planes, rows = field.shape[1], field.shape[2]
    scale = 1.0 / 343.0
    for i in range(planes + 1):
        value = u0_b[0, 4 + i, ROW0 : ROW0 + rows] * scale + f0[fine_plane(i)]
        if i <= SPILL:
            value = value + below[2 + i]
        if i >= planes - SPILL:
            value = value + above[i - (planes - SPILL)]
        pot[i, 0:rows] = value
        edge = u0_b[0, 4 + i, ROW0 + rows : ROW0 + rows + 1] * scale
        if i < planes:
            edge = edge + f0[6, i + SPILL : i + SPILL + 1]
            if i <= SPILL:
                edge = edge + below[0, i + SPILL + planes : i + SPILL + planes + 1]
            if i >= planes - SPILL:
                edge = edge + above[6, i + SPILL - planes : i + SPILL - planes + 1]
            pot[i, rows : rows + 1] = edge
    column = f0[7] + pltpu.roll(below[1], LANES - planes, 1) + pltpu.roll(above[7], planes, 1)
    lane = iota((rows, LANES), 1)
    for i in range(planes):
        here = pot[i, 0:rows]
        out[0, i] = field[0, i] - (pot[i + 1, 0:rows] - here)
        out[1, i] = field[1, i] - (pot[i, 1 : rows + 1] - here)
        beyond = pltpu.roll(u0_b[1, 4 + i, ROW0 : ROW0 + rows], LANES - 1, 1) * scale
        beyond = beyond + pltpu.roll(column, LANES - 1 - (i + SPILL), 1)
        next_z = jnp.where(lane == LANES - 1, beyond, pltpu.roll(here, LANES - 1, 1))
        out[2, i] = field[2, i] - (next_z - here)


def fine_plane(i):
    return i + SPILL if i <= 0 else i + SPILL + 2


def fine_share_kernel(field, after, main, up, down, base, first, second):
    planes = field.shape[1]
    count = base.shape[1]
    edge = [p for p in range(count) if p < PLANE0 or p > PLANE0 + planes]
    clear_planes(base, edge)
    clear_planes(first, edge)
    clear_planes(second, edge)
    fill_source(field, base)
    low, high = PLANE0, PLANE0 + planes + 1
    seventh = 1.0 / 7.0
    sweep(first, base, low - 1, high + 1, base, seventh)
    sweep(second, first, low - 2, high + 2, base, seventh)
    sweep(first, second, low - 3, high + 3, base, seventh)
    sweep(second, first, low - 4, high + 4, base, seventh)
    sweep(first, second, low - 5, high + 5, base, seventh)
    share, rows = main.shape[0], main.shape[1]

    for p in range(share):
        main[p] = first[0, p + 1] * weight(0)

    def read_up(p):
        return first[1, p + 1]

    def read_down(p):
        lane = iota((rows, LANES), 1)
        turned = pltpu.roll(first[1, p + 1], SPILL, 1)
        return jnp.where(lane == SPILL, pltpu.roll(first[0, p + 1], SPILL, 1), turned)

    for k, packed in enumerate(pack_lanes(read_up, share, 0, 6, 8, rows)):
        up[k] = packed * weight(0)
    for k, packed in enumerate(pack_lanes(read_down, share, 0, 6, 8, rows)):
        down[k] = packed * weight(0)


def fine_z_kernel(main, own, above, below, out, column_out, down, up):
    share, rows = main.shape[0], main.shape[1]
    lane = iota((rows, LANES), 1)
    column = jnp.zeros((rows, LANES), F32)
    for p in range(share):
        tile, k = p // 16, p % 16
        value = main[p] + unpacked(below[tile], k, 8, 0, 6, 0, rows)
        value = value + unpacked(above[tile], k, 8, 0, 5, LANES - 5, rows)
        out[p] = value
        turned = pltpu.roll(own[tile], (p - 8 * k) % LANES, 1)
        turned = turned + pltpu.roll(above[tile], (p - 8 * k - 5) % LANES, 1)
        column = jnp.where(lane == p, turned, column)
        down[p] = value[1:9]
        up[p] = value[40:48]
    column_out[...] = column
    down[share] = column[1:9]
    up[share] = column[40:48]


def fine_y_kernel(main, column, above, below, out, work):
    share = main.shape[0]
    rows = out.shape[1]

    def folded(k, value):
        work[...] = value
        work[33:41] = work[33:41] + above[k]
        work[8:16] = work[8:16] + below[k]

    out[6] = jnp.zeros((rows, LANES), F32)
    for p in range(share):
        folded(p, main[p])
        place = p if p <= SPILL else p + 2
        out[place] = work[ROW0 : ROW0 + rows]
        out[6, p : p + 1] = work[ROW0 + rows : ROW0 + rows + 1]
    folded(share, column[...])
    out[7] = work[ROW0 : ROW0 + rows]


def body(field):
    nx, ny, nz = field.shape[1:]
    size_x, size_y, size_z = lax.axis_size("gx"), lax.axis_size("gy"), lax.axis_size("gz")
    n1 = nx // 2
    share1 = n1 + 4
    rows0 = ny + 16
    rows1 = ny // 2 + 8
    planes0 = nx + 13

    def from_offset(value, axis, offset):
        count = lax.axis_size(axis)
        pairs = [(source, (source - offset) % count) for source in range(count)]
        return lax.ppermute(value, axis, pairs)

    level0 = (2, planes0, rows0, LANES)
    level1 = (1, n1 + 12, ny // 2 + 16, LANES)
    packed = ((n1 // 2 + 6) // 2) * 16
    up, down, far, g1 = call(
        spread_kernel,
        [shape(packed + rows1, LANES), shape(packed + rows1, LANES), shape(packed, LANES),
         shape(share1, rows1, LANES)],
        [level0, level0, level1, level1],
        2.9,
        field,
    )
    received = []
    for o in range(1, size_z):
        message = down if o == 1 else (up if o == size_z - 1 else far)
        received.append(from_offset(message, "gz", o))
    share0 = nx + 11
    main, f_up, f_down = call(
        fine_share_kernel,
        [shape(share0, rows0, LANES), shape(2, rows0, LANES), shape(2, rows0, LANES)],
        [level0, level0, level0],
        5.4,
        field, far,
    )
    f_above = from_offset(f_down, "gz", 1)
    f_below = from_offset(f_up, "gz", -1)

    tiles = size_z * 32 // LANES
    g2, g1 = call(
        functools.partial(gather_z_kernel, size_z),
        [shape(tiles, n1 // 2 + 6, 16, LANES), shape(share1, rows1, LANES)],
        [],
        0.2,
        far, g1, *received,
    )
    shares = [g2] + [from_offset(g2, "gx", o) for o in range(1, size_x)]
    inputs = [g1]
    sources = [(0, 0, 0, share1)]
    spans = {1: (0, 9), -1: (3, 12), 2: (0, 1), -2: (11, 12)}
    residues = {}
    for offset, span in spans.items():
        residues.setdefault(offset % size_x, []).append((offset, span))
    for residue, members in residues.items():
        if residue == 0:
            sources.extend((0, offset, 0, share1) for offset, span in members)
            continue
        first = min(span[0] for offset, span in members)
        last = max(span[1] for offset, span in members)
        inputs.append(from_offset(g1[first:last], "gx", residue))
        sources.extend((len(inputs) - 1, offset, first, last - first) for offset, span in members)
    g2 = call(
        functools.partial(fold_x_kernel, size_x),
        shape(tiles, 4 * size_x, 16, LANES),
        [],
        0.05,
        *shares,
    )
    planes1 = n1 + 14
    extra = -(-planes1 // 8)
    g1, g1_down, g1_up = call(
        functools.partial(window_x_kernel, tuple(sources)),
        [shape(planes1, rows1, LANES), shape(planes1 + extra, 8, LANES),
         shape(planes1 + extra, 8, LANES)],
        [],
        0.05,
        *inputs,
    )
    shares = [g2] + [from_offset(g2, "gy", o) for o in range(1, size_y)]
    g1_above = from_offset(g1_down, "gy", 1)
    g1_below = from_offset(g1_up, "gy", -1)

    main, column, f_down, f_up = call(
        fine_z_kernel,
        [shape(share0, rows0, LANES), shape(rows0, LANES), shape(share0 + 1, 8, LANES),
         shape(share0 + 1, 8, LANES)],
        [],
        0.7,
        main, f_up, f_above, f_below,
    )
    f_above = from_offset(f_down, "gy", 1)
    f_below = from_offset(f_up, "gy", -1)
    f0 = call(
        fine_y_kernel,
        shape(share0 + 2, ny, LANES),
        [(rows0, LANES)],
        0.4,
        main, column, f_above, f_below,
    )
    f_down, f_up = f0[0:8], jnp.concatenate([f0[6:8], f0[share0 + 2 - 6 :]], axis=0)
    if size_x == 2:
        other = from_offset(jnp.concatenate([f_down, f_up[2:]], axis=0), "gx", 1)
        f_above, f_below = other[0:8], jnp.concatenate([other[6:8], other[8:]], axis=0)
    else:
        f_above = from_offset(f_down, "gx", 1)
        f_below = from_offset(f_up, "gx", -1)

    scratch = []
    for level in (2, 3, 4):
        cut = 2 ** (level - 2)
        extent = (max(1, tiles // cut), 4 * size_x // cut, 8 * size_y // cut, LANES)
        scratch.extend([extent] * 3)
    e2 = call(
        functools.partial(coarse_kernel, size_y),
        shape(n1 // 2 + 6, 16, LANES),
        scratch,
        3.5,
        *shares,
    )
    window = (1, planes1, ny // 2 + 16, LANES)
    f1 = call(
        fine_tail_kernel,
        shape(share1, ny // 2 + 16, LANES),
        [window, window, window],
        0.8,
        g1, g1_above, g1_below,
    )
    return call(
        finish_kernel,
        shape(*field.shape),
        [level1, level1, (2, nx + 8, rows0, LANES), (2, nx + 8, rows0, LANES),
         (nx + 1, ny + 8, LANES)],
        3.9,
        field, e2, f1, f0, f_below, f_above,
    )


def solution(mesh):
    in_specs = (P(None, "gx", "gy", "gz"),)
    out_specs = P(None, "gx", "gy", "gz")
    return jax.shard_map(body, mesh=mesh, in_specs=in_specs, out_specs=out_specs, check_vma=False)
```

```python
import functools

import jax
import jax.numpy as jnp
import numpy as np
from jax import lax
from jax.experimental import pallas as pl
from jax.experimental.pallas import tpu as pltpu
from jax.sharding import PartitionSpec as P

LEVELS = 5
SWEEPS = 3
COARSE_ITERS = 24


F32 = jnp.float32
LANES = 128
VMEM_LIMIT = 16 * 1024 * 1024
PEAK_FLOPS_PER_US = 1150000000.0


def weight(level):
    return 4.0**level / 7.0


def shape(*extent):
    return jax.ShapeDtypeStruct(extent, F32)


def call(kernel, outs, scratch, microseconds, *args):
    flops = int(microseconds * PEAK_FLOPS_PER_US)
    return pl.pallas_call(
        kernel,
        out_shape=outs,
        scratch_shapes=[pltpu.VMEM(s, F32) for s in scratch],
        compiler_params=pltpu.CompilerParams(vmem_limit_bytes=VMEM_LIMIT),
        cost_estimate=pl.CostEstimate(flops=flops, bytes_accessed=0, transcendentals=0),
    )(*args)


def iota(extent, dim):
    return lax.broadcasted_iota(jnp.int32, extent, dim)


def one_hot(condition):
    rows = iota((LANES, LANES), 0)
    columns = iota((LANES, LANES), 1)
    return jnp.where(condition(rows, columns), 1.0, 0.0).astype(jnp.bfloat16)


def dot(left, right):
    return lax.dot_general(
        left,
        right,
        (((1,), (0,)), ((), ())),
        precision=lax.Precision.HIGHEST,
        preferred_element_type=F32,
    )


def dot_ones(left, right):
    dims = (((1,), (0,)), ((), ()))
    large = left.astype(jnp.bfloat16)
    small = (left - large.astype(F32)).astype(jnp.bfloat16)
    total = lax.dot_general(large, right, dims, preferred_element_type=F32)
    return total + lax.dot_general(small, right, dims, preferred_element_type=F32)


def seven_sum(source, plane, below, above, wanted=None):
    tiles = source.shape[0]
    rows = source.shape[2]
    center = [source[t, plane] for t in range(tiles)]
    left = [pltpu.roll(v, 1, 1) for v in center]
    right = [pltpu.roll(v, LANES - 1, 1) for v in center]
    if tiles > 1:
        lane = iota((rows, LANES), 1)
        left = [jnp.where(lane == 0, left[t - 1], left[t]) for t in range(tiles)]
        right = [
            jnp.where(lane == LANES - 1, right[(t + 1) % tiles], right[t]) for t in range(tiles)
        ]
    out = []
    for t in range(tiles if wanted is None else wanted):
        v = center[t]
        total = v + (source[t, below] + source[t, above])
        total = total + (pltpu.roll(v, 1, 0) + pltpu.roll(v, rows - 1, 0))
        out.append(total + (left[t] + right[t]))
    return out


def sweep(target, source, low, high, base=None, scale=None, period=None, span=None):
    for plane in range(low, high):
        below, above = plane - 1, plane + 1
        if period is not None:
            below, above = below % period, above % period
        for t, value in enumerate(seven_sum(source, plane, below, above)):
            if scale is not None:
                value = value * scale
            if base is not None and (span is None or span[0] <= plane < span[1]):
                value = value + base[t, plane]
            target[t, plane] = value


PLANE0 = 6
ROW0 = 8
SPILL = 5


def fill_source(field, target):
    planes, rows = field.shape[1], field.shape[2]
    lane = iota((rows, LANES), 1)
    row = iota((rows, LANES), 0)
    row8 = iota((8, LANES), 0)
    zero8 = jnp.zeros((8, LANES), F32)
    zeros = jnp.zeros((rows, LANES), F32)

    def one_plane(i, before):
        along_x, along_y, along_z = field[0, i], field[1, i], field[2, i]
        value = before - along_x - along_y - along_z
        value = value + jnp.where(row == 0, 0.0, pltpu.roll(along_y, 1, 0))
        turned = pltpu.roll(along_z, 1, 1)
        value = value + jnp.where(lane == 0, 0.0, turned)
        p = PLANE0 + i
        target[0, p, 0:ROW0] = zero8
        target[0, p, ROW0 : ROW0 + rows] = value
        last = pltpu.roll(along_y[rows - 8 : rows], 1, 0)
        target[0, p, ROW0 + rows : ROW0 + rows + 8] = jnp.where(row8 == 0, last, 0.0)
        target[1, p, 0:ROW0] = zero8
        target[1, p, ROW0 : ROW0 + rows] = jnp.where(lane == 0, turned, 0.0)
        target[1, p, ROW0 + rows : ROW0 + rows + 8] = zero8

    for i in range(planes):
        one_plane(i, field[0, i - 1] if i else zeros)
    p = PLANE0 + planes
    target[0, p] = jnp.zeros(target.shape[2:], F32)
    target[1, p] = jnp.zeros(target.shape[2:], F32)
    target[0, p, ROW0 : ROW0 + rows] = field[0, planes - 1]


def clear_planes(target, planes):
    for t in range(target.shape[0]):
        for p in planes:
            target[t, p] = jnp.zeros(target.shape[2:], F32)


def pack_lanes(read, count, first, width, spacing, rows):
    lane = iota((rows, LANES), 1)
    per_tile = LANES // spacing
    tiles = []
    for start in range(0, count, per_tile):
        packed = jnp.zeros((rows, LANES), F32)
        for k in range(min(per_tile, count - start)):
            turned = pltpu.roll(read(start + k), (spacing * k - first) % LANES, 1)
            inside = (lane >= spacing * k) & (lane < spacing * k + width)
            packed = jnp.where(inside, turned, packed)
        tiles.append(packed)
    return tiles


def unpacked(packed, k, spacing, offset, width, first, rows):
    lane = iota((rows, LANES), 1)
    turned = pltpu.roll(packed, (first - spacing * k - offset) % LANES, 1)
    inside = (lane >= first) & (lane < first + width)
    return jnp.where(inside, turned, 0.0)


def clear_margin(target, low, high):
    clear_planes(target, (low - 2, low - 1, high, high + 1))


def spread_kernel(field, up, down, far, g1_out, zeroth, first, second, third, g1_a, g1_b):
    planes = field.shape[1]
    fill_source(field, zeroth)
    low, high = PLANE0, PLANE0 + planes + 1
    clear_margin(zeroth, low, high)
    powers = (zeroth, first, second, third)
    for k in (1, 2, 3):
        sweep(powers[k], powers[k - 1], low - k, high + k)
        clear_margin(powers[k], low - k, high + k)

    n1 = planes // 2
    rows1 = first.shape[2] // 2
    pieces = []
    for t in range(2):
        parts = []
        for c in range(-2, n1 + 2):
            p = PLANE0 + 2 * c
            total = third[t, p, pl.ds(0, rows1, stride=2), :]
            total = total + third[t, p, pl.ds(1, rows1, stride=2), :]
            total = total + third[t, p + 1, pl.ds(0, rows1, stride=2), :]
            total = total + third[t, p + 1, pl.ds(1, rows1, stride=2), :]
            parts.append(total)
        pieces.append(jnp.concatenate(parts, axis=0))
    main = one_hot(lambda r, c: c == 32 + r // 2)
    side = one_hot(lambda r, c: c == jnp.where(r < 64, 96 + r // 2, r // 2 - 32))
    g1 = (dot_ones(pieces[0], main) + dot_ones(pieces[1], side)) * (0.125 / 343.0)
    share = n1 + 4
    g1 = g1.reshape(share, rows1, LANES)
    g1_out[...] = g1

    clear_planes(g1_a, range(g1_a.shape[1]))
    clear_planes(g1_b, range(g1_b.shape[1]))
    for c in range(share):
        g1_a[0, 4 + c, 4 : 4 + rows1] = g1[c]
    sweep(g1_b, g1_a, 3, 5 + share)
    sweep(g1_a, g1_b, 2, 6 + share)
    sweep(g1_b, g1_a, 1, 7 + share)
    rows2 = g1_a.shape[2] // 2
    parts = []
    for c in range(g1_a.shape[1] // 2):
        total = g1_b[0, 2 * c, pl.ds(0, rows2, stride=2), :]
        total = total + g1_b[0, 2 * c, pl.ds(1, rows2, stride=2), :]
        total = total + g1_b[0, 2 * c + 1, pl.ds(0, rows2, stride=2), :]
        total = total + g1_b[0, 2 * c + 1, pl.ds(1, rows2, stride=2), :]
        parts.append(total)
    even = jnp.concatenate(parts[0::2], axis=0)
    odd = jnp.concatenate(parts[1::2], axis=0)
    g2 = dot_ones(even, one_hot(lambda r, c: c == r // 2))
    g2 = g2 + dot_ones(odd, one_hot(lambda r, c: c == 64 + r // 2))
    g2 = g2 * (0.125 / 343.0)
    size = g2.shape[0]
    far[...] = g2
    up[0:size] = g2
    down[0:size] = g2
    up[size : size + rows1] = pack_lanes(lambda c: g1[c], share, 89, 9, 10, rows1)[0]
    down[size : size + rows1] = pack_lanes(lambda c: g1[c], share, 30, 9, 10, rows1)[0]
    rows0 = zeroth.shape[2] - ROW0
    lane = iota((rows0, LANES), 1)

    def last_columns(i):
        p = PLANE0 + i
        return jnp.where(lane == 0, zeroth[1, p, ROW0:], zeroth[0, p, ROW0:])

    def first_columns(i):
        return zeroth[0, PLANE0 + i, ROW0:]

    size = size + rows1
    up[size:] = pack_lanes(last_columns, planes + 1, LANES - SPILL, SPILL + 1, 7, rows0)[0]
    down[size:] = pack_lanes(first_columns, planes + 1, 0, SPILL + 1, 7, rows0)[0]


def gather_z_kernel(count, *refs):
    own, g1, up, received = refs[0], refs[1], refs[2], refs[3 : 2 + count]
    g2_out, g1_out, message = refs[2 + count :]
    size = own.shape[0]
    period = 32 * count
    rows2 = 16
    tiles, planes = g2_out.shape[0], g2_out.shape[1]
    lane = iota((size, LANES), 1)
    for parity in range(2):
        totals = [jnp.zeros((size, LANES), F32) for _ in range(tiles)]
        for o in range(count):
            value = own[...] if o == 0 else received[o - 1][0:size]
            shift = (32 * o - 64 * parity) % LANES
            turned = pltpu.roll(value, shift, 1) if shift else value
            position = ((lane - shift) & (LANES - 1)) - 64 * parity
            inside = (position >= 0) & (position < 64)
            for t in range(tiles):
                lands = lax.rem(position + (32 * o + period), period) == lane + LANES * t
                totals[t] = totals[t] + jnp.where(inside & lands, turned, 0.0)
        for t in range(tiles):
            for k in range(planes // 2):
                g2_out[t, 2 * k + parity] = totals[t][rows2 * k : rows2 * (k + 1)]
    rows1 = g1.shape[1]
    above = received[0][size : size + rows1]
    below = received[count - 2][size : size + rows1]
    share = g1.shape[0]
    for c in range(share):
        value = g1[c] + unpacked(below, c, 10, 0, 9, 25, rows1)
        g1_out[c] = value + unpacked(above, c, 10, 0, 9, 94, rows1)
    lane = iota((ROWS_SENT, LANES), 1)
    for q in range(share // 2):
        even, odd = g1_out[2 * q, 2 : 2 + ROWS_SENT], g1_out[2 * q + 1, 2 : 2 + ROWS_SENT]
        value = jnp.where(lane < 64, pltpu.roll(even, LANES - 32, 1), pltpu.roll(odd, 32, 1))
        message[ROWS_SENT * q : ROWS_SENT * (q + 1)] = value
    start = ROWS_SENT * (share // 2)
    for q in range(-(-share // 8)):
        packed = jnp.zeros((ROWS_SENT, LANES), F32)
        for k in range(min(8, share - 8 * q)):
            value = g1_out[8 * q + k, 2 : 2 + ROWS_SENT]
            low = pltpu.roll(value, (16 * k - 24) % LANES, 1)
            high = pltpu.roll(value, (16 * k + 8 - 96) % LANES, 1)
            packed = jnp.where((lane >= 16 * k) & (lane < 16 * k + 8), low, packed)
            packed = jnp.where((lane >= 16 * k + 8) & (lane < 16 * k + 16), high, packed)
        message[start : start + ROWS_SENT] = packed
        start += ROWS_SENT
    rows0 = (message.shape[0] - start) // 3
    for k, strip in enumerate((received[count - 2], received[0], up)):
        message[start + rows0 * k : start + rows0 * (k + 1)] = strip[size + rows1 :]


ROWS_SENT = 20


def plane_sent(message, share, c):
    lane = iota((ROWS_SENT, LANES), 1)
    pair = message[ROWS_SENT * (c // 2) : ROWS_SENT * (c // 2 + 1)]
    inside = (lane >= 32) & (lane < 96)
    value = jnp.where(inside, pltpu.roll(pair, LANES - 32 if c % 2 else 32, 1), 0.0)
    start = ROWS_SENT * (share // 2 + c // 8)
    sides = message[start : start + ROWS_SENT]
    k = c % 8
    low = pltpu.roll(sides, (24 - 16 * k) % LANES, 1)
    high = pltpu.roll(sides, (88 - 16 * k) % LANES, 1)
    value = jnp.where((lane >= 24) & (lane < 32), low, value)
    return jnp.where((lane >= 96) & (lane < 104), high, value)


def fold_x_kernel(count, *refs):
    shares, out = refs[:count], refs[count]
    tiles, period = out.shape[0], out.shape[1]
    for t in range(tiles):
        for x in range(period):
            total = None
            for o in range(count):
                for c in range(10):
                    if (c - 3 + 4 * o) % period == x:
                        value = shares[o][t, c]
                        total = value if total is None else total + value
            out[t, x] = total


def window_x_kernel(sources, *refs):
    own, inputs, (out, down, up, base, first, second) = refs[0], refs[1:-6], refs[-6:]
    planes, share = base.shape[1], out.shape[0]
    read = {}
    for p in range(planes):
        total = None
        for index, offset in sources:
            c = p - 7 - 8 * offset + 2
            if not 0 <= c < share:
                continue
            if (index, c) not in read:
                if index == 0:
                    read[index, c] = own[c, 2 : 2 + ROWS_SENT]
                else:
                    read[index, c] = plane_sent(inputs[index - 1], share, c)
            value = read[index, c]
            total = value if total is None else total + value
        base[0, p, 0:8] = jnp.zeros((8, LANES), F32)
        base[0, p, 24:32] = jnp.zeros((8, LANES), F32)
        base[0, p, 6 : 6 + ROWS_SENT] = total
    seventh = 1.0 / 7.0
    sweep(first, base, 1, planes - 1, base, seventh)
    sweep(second, first, 2, planes - 2, base, seventh)
    sweep(first, second, 3, planes - 3, base, seventh)
    sweep(second, first, 4, planes - 4, base, seventh)
    share = out.shape[0]
    for c in range(share):
        p = 5 + c
        value = (seven_sum(second, p, p - 1, p + 1)[0] * seventh + base[0, p]) * weight(1)
        out[c] = value
        down[c] = value[1:9]
        up[c] = value[22:30]
        down[share + c // 8, c % 8 : c % 8 + 1] = value[9:10]
        up[share + c // 8, c % 8 : c % 8 + 1] = value[30:31]


def restrict_lanes(values, width, coarse_width, coarse_tiles):
    out = []
    for s in range(coarse_tiles):
        total = None
        for t, value in enumerate(values):
            matrix = one_hot(
                lambda r, c: ((LANES * t + r) // 2 == lax.rem(LANES * s + c, coarse_width))
                & (LANES * t + r < width)
            )
            term = dot_ones(value, matrix)
            total = term if total is None else total + term
        out.append(total)
    return out


def prolong_lanes(values, width, fine_tiles):
    out = []
    for s in range(fine_tiles):
        total = None
        for t, value in enumerate(values):
            matrix = one_hot(lambda r, c: LANES * t + r == lax.rem(LANES * s + c, width) // 2)
            term = dot_ones(value, matrix)
            total = term if total is None else total + term
        out.append(total)
    return out


def real_waves(count):
    cells = np.arange(count)
    rows, eigenvalues = [], []
    for k in range(count // 2 + 1):
        angle = 2.0 * np.pi * k / count
        rows.append(np.cos(angle * cells))
        eigenvalues.append(2.0 * np.cos(angle))
        if 0 < k < count / 2:
            rows.append(np.sin(angle * cells))
            eigenvalues.append(2.0 * np.cos(angle))
    basis = np.stack(rows)
    basis = basis / np.sqrt(np.sum(basis * basis, axis=1, keepdims=True))
    return basis, np.array(eigenvalues)


def last_level_matrices(planes, rows, width):
    wave_x, value_x = real_waves(planes)
    wave_y, value_y = real_waves(rows)
    wave_z, value_z = real_waves(width)
    into = np.kron(wave_x, np.repeat(wave_y, 1, axis=1))
    level_values = value_x[:, None, None] + value_y[None, :, None] + value_z[None, None, :]
    factor = (1.0 + level_values) / 7.0
    total = sum(factor**k for k in range(COARSE_ITERS)) * weight(LEVELS - 1) * 0.125
    scale = np.zeros((planes * rows, LANES))
    scale[:, :width] = total.reshape(planes * rows, width)
    fine = 2 * width
    tiles = max(1, fine // LANES)
    lanes = np.arange(LANES * tiles)
    to_waves = np.zeros((LANES * tiles, LANES))
    to_waves[:fine, :width] = wave_z.T[lanes[:fine] // 2]
    from_waves = np.zeros((LANES, LANES * tiles))
    from_waves[:width] = wave_z[:, (lanes % fine) // 2]
    to_waves = to_waves.reshape(tiles, LANES, LANES)
    from_waves = from_waves.reshape(LANES, tiles, LANES).transpose(1, 0, 2)
    arrays = (into, into.T, to_waves, from_waves, scale)
    return [jnp.asarray(np.ascontiguousarray(a), F32) for a in arrays]


def solve_last(values, into, back, to_waves, from_waves, scale):
    total = None
    for t, value in enumerate(values):
        term = dot(dot(into[...], value), to_waves[t])
        total = term if total is None else total + term
    total = dot(back[...], total * scale[...])
    return [dot(total, from_waves[t]) for t in range(len(values))]


def solve(level, width, buffers, spectral):
    g, a, b = buffers[level]
    tiles, planes, rows = g.shape[0], g.shape[1], g.shape[2]
    seventh = 1.0 / 7.0
    w = weight(level)
    sweep(a, g, 0, planes, None, seventh, planes)
    sweep(b, a, 0, planes, None, seventh, planes)
    for t in range(tiles):
        for p in range(planes):
            g[t, p] = (g[t, p] + a[t, p] + b[t, p]) * w
    sweep(a, b, 0, planes, None, seventh, planes)
    half = rows // 2
    values = []
    for t in range(tiles):
        parts = []
        for c in range(planes // 2):
            total = a[t, 2 * c, pl.ds(0, half, stride=2), :]
            total = total + a[t, 2 * c, pl.ds(1, half, stride=2), :]
            total = total + a[t, 2 * c + 1, pl.ds(0, half, stride=2), :]
            total = total + a[t, 2 * c + 1, pl.ds(1, half, stride=2), :]
            parts.append(total)
        values.append(jnp.concatenate(parts, axis=0))
    if level == LEVELS - 2:
        values = solve_last(values, *spectral)
    else:
        coarse = buffers[level + 1][0]
        values = restrict_lanes(values, width, width // 2, coarse.shape[0])
        for t, value in enumerate(values):
            for c in range(planes // 2):
                coarse[t, c] = value[half * c : half * (c + 1)] * 0.125
        solve(level + 1, width // 2, buffers, spectral)
        values = [
            jnp.concatenate([coarse[t, c] for c in range(planes // 2)], axis=0)
            for t in range(coarse.shape[0])
        ]
        values = prolong_lanes(values, width, tiles)
    for t, value in enumerate(values):
        for c in range(planes // 2):
            part = value[half * c : half * (c + 1)]
            for p in (2 * c, 2 * c + 1):
                b[t, p, pl.ds(0, half, stride=2), :] = part
                b[t, p, pl.ds(1, half, stride=2), :] = part
        for p in range(planes):
            b[t, p] = b[t, p] + g[t, p]
    sweep(a, b, 0, planes, None, seventh, planes)
    sweep(b, a, 0, planes, None, seventh, planes)
    sweep(a, b, 0, planes, None, seventh, planes)
    for t in range(tiles):
        for p in range(planes):
            g[t, p] = g[t, p] + a[t, p]


def coarse_kernel(count, *refs):
    shares, spectral = refs[:count], refs[count : count + 5]
    out, scratch = refs[count + 5], refs[count + 6 :]
    buffers = {level: scratch[3 * (level - 2) : 3 * (level - 1)] for level in (2, 3)}
    g = buffers[2][0]
    tiles, planes = g.shape[0], g.shape[1]
    for t in range(tiles):
        for p in range(planes):
            for b in range(count):
                value = shares[b][t, p, 0:8] + shares[(b - 1) % count][t, p, 8:16]
                g[t, p, 8 * b : 8 * b + 8] = value
    solve(2, LANES * tiles, buffers, spectral)
    for c in range(out.shape[0]):
        out[c] = g[0, (c - 3) % planes, 0:16]


def correct_kernel(e2, f1_own, f1_above, f1_below, u0_b, u1_a, u1_b, f1, u0_a):
    share1 = f1_own.shape[0]
    for c in range(share1):
        f1[c] = f1_own[c]
        f1[c, 17:25] = f1[c, 17:25] + f1_above[c]
        f1[c, 6:14] = f1[c, 6:14] + f1_below[c]
        ninth, k = share1 + c // 8, c % 8
        f1[c, 25:26] = f1[c, 25:26] + f1_above[ninth, k : k + 1]
        f1[c, 14:15] = f1[c, 14:15] + f1_below[ninth, k : k + 1]
    share2 = e2.shape[0]
    rows2 = e2.shape[1]
    value = e2[...].reshape(share2 * rows2, LANES)
    value = dot_ones(value, one_hot(lambda r, c: r == c // 2))
    for c in range(share2):
        part = value[rows2 * c : rows2 * (c + 1)]
        for p in (2 * c, 2 * c + 1):
            u1_a[0, p, pl.ds(0, rows2, stride=2), :] = part
            u1_a[0, p, pl.ds(1, rows2, stride=2), :] = part
    count1 = 2 * share2
    sweep(u1_b, u1_a, 1, count1 - 1)
    sweep(u1_a, u1_b, 2, count1 - 2)
    sweep(u1_b, u1_a, 3, count1 - 3)
    rows1 = 24
    parts = []
    for c in range(share1):
        parts.append(f1[c, 4 : 4 + rows1] + u1_b[0, 4 + c, 4 : 4 + rows1] * (1.0 / 343.0))
    value = jnp.concatenate(parts, axis=0)
    main = dot_ones(value, one_hot(lambda r, c: r == 32 + c // 2))
    side = dot_ones(value, one_hot(lambda r, c: r == jnp.where(c < 64, 96 + c // 2, c // 2 - 32)))
    for t, value in enumerate((main, side)):
        for c in range(share1):
            part = value[rows1 * c : rows1 * (c + 1)]
            for p in (2 * c, 2 * c + 1):
                u0_a[t, p, pl.ds(0, rows1, stride=2), :] = part
                u0_a[t, p, pl.ds(1, rows1, stride=2), :] = part
    count0 = 2 * share1
    sweep(u0_b, u0_a, 1, count0 - 1)
    sweep(u0_a, u0_b, 2, count0 - 2)
    sweep(u0_b, u0_a, 3, count0 - 3)


def finish_kernel(field, u0_b, f0, beyond, out, pot):
    planes, rows = field.shape[1], field.shape[2]
    scale = 1.0 / 343.0
    for i in range(planes + 1):
        pot[i, 0:rows] = u0_b[0, 4 + i, ROW0 : ROW0 + rows] * scale + f0[i, 0:rows]
        if i < planes:
            edge = u0_b[0, 4 + i, ROW0 + rows : ROW0 + rows + 1] * scale
            pot[i, rows : rows + 1] = edge + f0[i, rows : rows + 1]
    lane = iota((rows, LANES), 1)
    for i in range(planes):
        here = pot[i, 0:rows]
        out[0, i] = field[0, i] - (pot[i + 1, 0:rows] - here)
        out[1, i] = field[1, i] - (pot[i, 1 : rows + 1] - here)
        last = pltpu.roll(u0_b[1, 4 + i, ROW0 : ROW0 + rows], LANES - 1, 1) * scale + beyond[i]
        next_z = jnp.where(lane == LANES - 1, last, pltpu.roll(here, LANES - 1, 1))
        out[2, i] = field[2, i] - (next_z - here)


def fine_place(p, share):
    if p <= SPILL:
        return p
    return p - share + 13 if p >= share - 6 else p + 7


def fine_own_kernel(zeroth, first, second, third, field, after, main, down, up, field_out, fourth):
    share = main.shape[0]
    field_out[...] = field[...]
    low, high = PLANE0, zeroth.shape[1] - 6
    sweep(fourth, third, low - 4, high + 4)
    clear_margin(fourth, low - 4, high + 4)
    powers = (zeroth, first, second, third, fourth)
    for k in range(share):
        p = low - SPILL + k
        total = seven_sum(fourth, p, p - 1, p + 1, 1)[0] * (weight(0) / 7.0**5)
        for n, power in enumerate(powers):
            if low - n <= p < high + n:
                total = total + power[0, p] * (weight(0) / 7.0**n)
        main[k] = total
        down[k] = total[1:9]
        up[k] = total[40:48]


EDGE = 64
BEYOND = 96


def fine_edge_kernel(start, *refs):
    strips, (out, down, up, base, first, second) = refs[:3], refs[3:]
    share, rows = out.shape[0], out.shape[1]
    planes = share - 1
    inner = rows - ROW0
    lane = iota((inner, LANES), 1)
    sources = [
        [r[start + inner * k : start + inner * (k + 1)] for k in range(3)] for r in strips
    ]
    for k in range(base.shape[1]):
        value = jnp.zeros((inner, LANES), F32)
        for d, offset in ((0, 0), (1, -planes), (2, planes)):
            i = k - SPILL - offset
            if not 0 <= i <= planes:
                continue
            below, above, own = sources[d]
            turned = pltpu.roll(below, (LANES - SPILL - 7 * i) % LANES, 1)
            value = value + jnp.where((lane >= LANES - SPILL) | (lane == 0), turned, 0.0)
            turned = pltpu.roll(above, (EDGE - 7 * i) % LANES, 1)
            value = value + jnp.where((lane >= EDGE) & (lane <= EDGE + SPILL), turned, 0.0)
            turned = pltpu.roll(above, (BEYOND - 7 * i) % LANES, 1)
            value = value + jnp.where((lane >= BEYOND) & (lane <= BEYOND + SPILL), turned, 0.0)
            turned = pltpu.roll(own, (BEYOND - SPILL - 7 * i) % LANES, 1)
            value = value + jnp.where((lane >= BEYOND - SPILL) & (lane <= BEYOND), turned, 0.0)
        base[0, k, 0:ROW0] = jnp.zeros((ROW0, LANES), F32)
        base[0, k, ROW0:] = value
    seventh = 1.0 / 7.0
    high = base.shape[1]
    sweep(first, base, 1, high - 1, base, seventh)
    sweep(second, first, 2, high - 2, base, seventh)
    sweep(first, second, 3, high - 3, base, seventh)
    sweep(second, first, 4, high - 4, base, seventh)
    for i in range(share):
        p = SPILL + i
        value = (seven_sum(second, p, p - 1, p + 1)[0] * seventh + base[0, p]) * weight(0)
        out[i] = value
        down[i] = value[1:9]
        up[i] = value[40:48]


def fine_sum_kernel(f0, below_x, above_x, edge, above, below, out, beyond, work):
    planes, rows = beyond.shape[0], beyond.shape[1]
    lane = iota((rows, LANES), 1)
    lane1 = iota((1, LANES), 1)
    work[:, 0:rows] = edge[:, ROW0 : ROW0 + rows]
    work[:, rows : rows + 8] = edge[:, ROW0 + rows : ROW0 + rows + 8]
    for i in range(planes + 1):
        work[i, 25:33] = work[i, 25:33] + above[i]
        work[i, 0:8] = work[i, 0:8] + below[i]
    for i in range(planes + 1):
        value = f0[fine_place(i + SPILL, planes + 11)]
        if i <= SPILL:
            value = value + below_x[1 + i]
        if i >= planes - SPILL:
            value = value + above_x[i - (planes - SPILL)]
        part = work[i, 0:rows]
        turned = pltpu.roll(part, EDGE, 1)
        value = value + jnp.where(lane <= SPILL, part, 0.0)
        out[i, 0:rows] = value + jnp.where(lane >= LANES - SPILL, turned, 0.0)
        if i < planes:
            beyond[i] = pltpu.roll(part, LANES - 1 - BEYOND, 1)
            row = f0[6, i + SPILL : i + SPILL + 1]
            if i <= SPILL:
                row = row + below_x[0, i + SPILL + planes : i + SPILL + planes + 1]
            if i >= planes - SPILL:
                row = row + above_x[6, i + SPILL - planes : i + SPILL - planes + 1]
            part = work[i, rows : rows + 1]
            row = row + jnp.where(lane1 <= SPILL, part, 0.0)
            row = row + jnp.where(lane1 >= LANES - SPILL, pltpu.roll(part, EDGE, 1), 0.0)
            out[i, rows : rows + 1] = row


def fine_y_kernel(main, above, below, out, work):
    share = main.shape[0]
    rows = out.shape[1]
    out[6] = jnp.zeros((rows, LANES), F32)
    for p in range(share):
        work[p] = main[p]
        work[p, 33:41] = work[p, 33:41] + above[p]
        work[p, 8:16] = work[p, 8:16] + below[p]
        out[fine_place(p, share)] = work[p, ROW0 : ROW0 + rows]
        out[6, p : p + 1] = work[p, ROW0 + rows : ROW0 + rows + 1]


EARLIER = {1: (), -1: (1,), 2: (1, -1), -2: (1, -1, 2)}


def body(field):
    nx, ny, nz = field.shape[1:]
    size_x, size_y, size_z = lax.axis_size("gx"), lax.axis_size("gy"), lax.axis_size("gz")
    n1 = nx // 2
    share1 = n1 + 4
    rows0 = ny + 16
    rows1 = ny // 2 + 8
    planes0 = nx + 13

    def from_offset(value, axis, offset):
        count = lax.axis_size(axis)
        pairs = [(source, (source - offset) % count) for source in range(count)]
        return lax.ppermute(value, axis, pairs)

    level0 = (2, planes0, rows0, LANES)
    level1 = (1, n1 + 12, ny // 2 + 16, LANES)
    packed = ((n1 // 2 + 6) // 2) * 16
    near = packed + rows1 + rows0 - ROW0
    up, down, far, g1, *powers = call(
        spread_kernel,
        [shape(near, LANES), shape(near, LANES), shape(packed, LANES),
         shape(share1, rows1, LANES)] + [shape(*level0)] * 4,
        [level1, level1],
        2.9,
        field,
    )
    received = []
    for o in range(1, size_z):
        message = down if o == 1 else (up if o == size_z - 1 else far)
        received.append(from_offset(message, "gz", o))
    share0 = nx + 11
    main, f_down, f_up, kept = call(
        fine_own_kernel,
        [shape(share0, rows0, LANES), shape(share0, 8, LANES), shape(share0, 8, LANES),
         shape(*field.shape)],
        [level0],
        3.0,
        *powers, field, received[size_z // 2 - 1],
    )
    f_above = from_offset(f_down, "gy", 1)
    f_below = from_offset(f_up, "gy", -1)

    tiles = size_z * 32 // LANES
    inner0 = rows0 - ROW0
    sent1 = ROWS_SENT * (share1 // 2 - (-share1 // 8))
    g2, g1, message = call(
        functools.partial(gather_z_kernel, size_z),
        [shape(tiles, n1 // 2 + 6, 16, LANES), shape(share1, rows1, LANES),
         shape(sent1 + 3 * inner0, LANES)],
        [],
        0.2,
        far, g1, up, *received,
    )
    shares = [g2] + [from_offset(g2, "gx", o) for o in range(1, size_x)]
    messages = {o: from_offset(message, "gx", o) for o in sorted({1, -1, 2, -2}, key=abs)
                if o % size_x and not any(o % size_x == q % size_x for q in EARLIER[o])}
    keys = [0] + list(messages)
    sources = []
    for o in (0, 1, -1, 2, -2):
        index = [k for k, key in enumerate(keys) if key % size_x == o % size_x][0]
        sources.append((index, o))
    g2 = call(
        functools.partial(fold_x_kernel, size_x),
        shape(tiles, 4 * size_x, 16, LANES),
        [],
        0.05,
        *shares,
    )
    window = (1, n1 + 14, ny // 2 + 16, LANES)
    edge1 = share1 + -(-share1 // 8)
    f1, f1_down, f1_up = call(
        functools.partial(window_x_kernel, tuple(sources)),
        [shape(share1, ny // 2 + 16, LANES), shape(edge1, 8, LANES), shape(edge1, 8, LANES)],
        [window, window, window],
        1.0,
        g1, *messages.values(),
    )
    shares = [g2] + [from_offset(g2, "gy", o) for o in range(1, size_y)]
    f1_above = from_offset(f1_down, "gy", 1)
    f1_below = from_offset(f1_up, "gy", -1)

    f0 = call(
        fine_y_kernel,
        shape(share0 + 1, ny, LANES),
        [(share0, rows0, LANES)],
        0.4,
        main, f_above, f_below,
    )
    if size_x == 2:
        other = from_offset(f0[0:13], "gx", 1)
        f_above, f_below = other[0:7], other[6:13]
    else:
        f_above = from_offset(f0[0:7], "gx", 1)
        f_below = from_offset(f0[6:13], "gx", -1)
    edges = (1, nx + 11, rows0, LANES)
    edge, e_down, e_up = call(
        functools.partial(fine_edge_kernel, sent1),
        [shape(nx + 1, rows0, LANES), shape(nx + 1, 8, LANES), shape(nx + 1, 8, LANES)],
        [edges, edges, edges],
        2.0,
        message, messages[-1 if -1 in messages else 1], messages[1],
    )
    e_above = from_offset(e_down, "gy", 1)
    e_below = from_offset(e_up, "gy", -1)
    f0, beyond = call(
        fine_sum_kernel,
        [shape(nx + 1, ny + 8, LANES), shape(nx, ny, LANES)],
        [(nx + 1, ny + 8, LANES)],
        0.4,
        f0, f_below, f_above, edge, e_above, e_below,
    )

    scratch = []
    for level in (2, 3):
        cut = 2 ** (level - 2)
        extent = (max(1, tiles // cut), 4 * size_x // cut, 8 * size_y // cut, LANES)
        scratch.extend([extent] * 3)
    e2 = call(
        functools.partial(coarse_kernel, size_y),
        shape(n1 // 2 + 6, 16, LANES),
        scratch,
        2.2,
        *shares, *last_level_matrices(size_x, 2 * size_y, 8 * size_z),
    )
    fine = (2, nx + 8, rows0, LANES)
    correction = call(
        correct_kernel,
        shape(*fine),
        [level1, level1, (share1, ny // 2 + 16, LANES), fine],
        2.6,
        e2, f1, f1_above, f1_below,
    )
    return call(
        finish_kernel,
        shape(*field.shape),
        [(nx + 1, ny + 8, LANES)],
        0.9,
        kept, correction, f0, beyond,
    )


def solution(mesh):
    in_specs = (P(None, "gx", "gy", "gz"),)
    out_specs = P(None, "gx", "gy", "gz")
    return jax.shard_map(body, mesh=mesh, in_specs=in_specs, out_specs=out_specs, check_vma=False)
```

```python
import functools

import jax
import jax.numpy as jnp
import numpy as np
from jax import lax
from jax.experimental import pallas as pl
from jax.experimental.pallas import tpu as pltpu
from jax.sharding import PartitionSpec as P

LEVELS = 5
SWEEPS = 3
COARSE_ITERS = 24


F32 = jnp.float32
LANES = 128
VMEM_LIMIT = 16 * 1024 * 1024
PEAK_FLOPS_PER_US = 1150000000.0


def weight(level):
    return 4.0**level / 7.0


def shape(*extent):
    return jax.ShapeDtypeStruct(extent, F32)


def call(kernel, outs, scratch, microseconds, *args, after=()):
    flops = int(microseconds * PEAK_FLOPS_PER_US)
    if after:
        inner, first, last = kernel, len(args), len(args) + len(after)

        def kernel(*refs):
            inner(*refs[:first], *refs[last:])

        args = (*args, *after)
    return pl.pallas_call(
        kernel,
        out_shape=outs,
        scratch_shapes=[pltpu.VMEM(s, F32) for s in scratch],
        compiler_params=pltpu.CompilerParams(vmem_limit_bytes=VMEM_LIMIT),
        cost_estimate=pl.CostEstimate(flops=flops, bytes_accessed=0, transcendentals=0),
    )(*args)


def iota(extent, dim):
    return lax.broadcasted_iota(jnp.int32, extent, dim)


def one_hot(condition):
    rows = iota((LANES, LANES), 0)
    columns = iota((LANES, LANES), 1)
    return jnp.where(condition(rows, columns), 1.0, 0.0).astype(jnp.bfloat16)


def dot(left, right):
    return lax.dot_general(
        left,
        right,
        (((1,), (0,)), ((), ())),
        precision=lax.Precision.HIGHEST,
        preferred_element_type=F32,
    )


def dot_ones(left, right):
    large = left.astype(jnp.bfloat16)
    rest = left - large.astype(F32)
    middle = rest.astype(jnp.bfloat16)
    small = (rest - middle.astype(F32)).astype(jnp.bfloat16)
    return lax.dot_general(
        jnp.concatenate([large, middle, small], axis=1),
        jnp.concatenate([right, right, right], axis=0),
        (((1,), (0,)), ((), ())),
        preferred_element_type=F32,
    )


def seven_sum(source, plane, below, above, wanted=None):
    tiles = source.shape[0]
    rows = source.shape[2]
    center = [source[t, plane] for t in range(tiles)]
    left = [pltpu.roll(v, 1, 1) for v in center]
    right = [pltpu.roll(v, LANES - 1, 1) for v in center]
    if tiles > 1:
        lane = iota((rows, LANES), 1)
        left = [jnp.where(lane == 0, left[t - 1], left[t]) for t in range(tiles)]
        right = [
            jnp.where(lane == LANES - 1, right[(t + 1) % tiles], right[t]) for t in range(tiles)
        ]
    out = []
    for t in range(tiles if wanted is None else wanted):
        v = center[t]
        total = v + (source[t, below] + source[t, above])
        total = total + (pltpu.roll(v, 1, 0) + pltpu.roll(v, rows - 1, 0))
        out.append(total + (left[t] + right[t]))
    return out


def sweep(target, source, low, high, base=None, scale=None, period=None, span=None):
    for plane in range(low, high):
        below, above = plane - 1, plane + 1
        if period is not None:
            below, above = below % period, above % period
        for t, value in enumerate(seven_sum(source, plane, below, above)):
            if scale is not None:
                value = value * scale
            if base is not None and (span is None or span[0] <= plane < span[1]):
                value = value + base[t, plane]
            target[t, plane] = value


PLANE0 = 6
ROW0 = 8
SPILL = 5


def fill_source(field, target):
    planes, rows = field.shape[1], field.shape[2]
    lane = iota((rows, LANES), 1)
    row = iota((rows, LANES), 0)
    row8 = iota((8, LANES), 0)
    zero8 = jnp.zeros((8, LANES), F32)
    zeros = jnp.zeros((rows, LANES), F32)

    def one_plane(i, before):
        along_x, along_y, along_z = field[0, i], field[1, i], field[2, i]
        value = before - along_x - along_y - along_z
        value = value + jnp.where(row == 0, 0.0, pltpu.roll(along_y, 1, 0))
        turned = pltpu.roll(along_z, 1, 1)
        value = value + jnp.where(lane == 0, 0.0, turned)
        p = PLANE0 + i
        target[0, p, 0:ROW0] = zero8
        target[0, p, ROW0 : ROW0 + rows] = value
        last = pltpu.roll(along_y[rows - 8 : rows], 1, 0)
        target[0, p, ROW0 + rows : ROW0 + rows + 8] = jnp.where(row8 == 0, last, 0.0)
        target[1, p, 0:ROW0] = zero8
        target[1, p, ROW0 : ROW0 + rows] = jnp.where(lane == 0, turned, 0.0)
        target[1, p, ROW0 + rows : ROW0 + rows + 8] = zero8

    for i in range(planes):
        one_plane(i, field[0, i - 1] if i else zeros)
    p = PLANE0 + planes
    target[0, p] = jnp.zeros(target.shape[2:], F32)
    target[1, p] = jnp.zeros(target.shape[2:], F32)
    target[0, p, ROW0 : ROW0 + rows] = field[0, planes - 1]


def clear_planes(target, planes):
    for t in range(target.shape[0]):
        for p in planes:
            target[t, p] = jnp.zeros(target.shape[2:], F32)


def pack_lanes(read, count, first, width, spacing, rows):
    lane = iota((rows, LANES), 1)
    per_tile = LANES // spacing
    tiles = []
    for start in range(0, count, per_tile):
        packed = jnp.zeros((rows, LANES), F32)
        for k in range(min(per_tile, count - start)):
            turned = pltpu.roll(read(start + k), (spacing * k - first) % LANES, 1)
            inside = (lane >= spacing * k) & (lane < spacing * k + width)
            packed = jnp.where(inside, turned, packed)
        tiles.append(packed)
    return tiles


def unpacked(packed, k, spacing, offset, width, first, rows):
    lane = iota((rows, LANES), 1)
    turned = pltpu.roll(packed, (first - spacing * k - offset) % LANES, 1)
    inside = (lane >= first) & (lane < first + width)
    return jnp.where(inside, turned, 0.0)


def clear_margin(target, low, high):
    clear_planes(target, (low - 2, low - 1, high, high + 1))


def spread_kernel(field, message, g2_out, g1_out, zeroth, first, second, third, g1_a, g1_b):
    planes = field.shape[1]
    fill_source(field, zeroth)
    low, high = PLANE0, PLANE0 + planes + 1
    clear_margin(zeroth, low, high)
    powers = (zeroth, first, second, third)
    for k in (1, 2, 3):
        sweep(powers[k], powers[k - 1], low - k, high + k)
        clear_margin(powers[k], low - k, high + k)

    n1 = planes // 2
    rows1 = first.shape[2] // 2
    pieces = []
    for t in range(2):
        parts = []
        for c in range(-2, n1 + 2):
            p = PLANE0 + 2 * c
            total = third[t, p, pl.ds(0, rows1, stride=2), :]
            total = total + third[t, p, pl.ds(1, rows1, stride=2), :]
            total = total + third[t, p + 1, pl.ds(0, rows1, stride=2), :]
            total = total + third[t, p + 1, pl.ds(1, rows1, stride=2), :]
            parts.append(total)
        pieces.append(jnp.concatenate(parts, axis=0))
    main = one_hot(lambda r, c: c == 32 + r // 2)
    side = one_hot(lambda r, c: c == jnp.where(r < 64, 96 + r // 2, r // 2 - 32))
    g1 = (dot_ones(pieces[0], main) + dot_ones(pieces[1], side)) * (0.125 / 343.0)
    share = n1 + 4
    g1 = g1.reshape(share, rows1, LANES)
    g1_out[...] = g1

    clear_planes(g1_a, range(g1_a.shape[1]))
    clear_planes(g1_b, range(g1_b.shape[1]))
    for c in range(share):
        g1_a[0, 4 + c, 4 : 4 + rows1] = g1[c]
    sweep(g1_b, g1_a, 3, 5 + share)
    sweep(g1_a, g1_b, 2, 6 + share)
    sweep(g1_b, g1_a, 1, 7 + share)
    rows2 = g1_a.shape[2] // 2
    parts = []
    for c in range(g1_a.shape[1] // 2):
        total = g1_b[0, 2 * c, pl.ds(0, rows2, stride=2), :]
        total = total + g1_b[0, 2 * c, pl.ds(1, rows2, stride=2), :]
        total = total + g1_b[0, 2 * c + 1, pl.ds(0, rows2, stride=2), :]
        total = total + g1_b[0, 2 * c + 1, pl.ds(1, rows2, stride=2), :]
        parts.append(total)
    groups = -(-len(parts) // 3)
    parts.extend([jnp.zeros((rows2, LANES), F32)] * (3 * groups - len(parts)))
    g2 = None
    for slot in range(3):
        matrix = one_hot(
            lambda r, c: (c == r // 2 - 13 + 42 * slot) & (r // 2 >= 13) & (r // 2 < 51)
        )
        term = dot_ones(jnp.concatenate(parts[slot::3], axis=0), matrix)
        g2 = term if g2 is None else g2 + term
    g2_out[...] = g2 * (0.125 / 343.0)
    lane = iota((ROWS_SENT, LANES), 1)
    sides = jnp.zeros((ROWS_SENT, LANES), F32)
    for q in range(share // 2):
        even, odd = g1_out[2 * q, 2 : 2 + ROWS_SENT], g1_out[2 * q + 1, 2 : 2 + ROWS_SENT]
        value = jnp.where(lane < 64, pltpu.roll(even, LANES - 32, 1), pltpu.roll(odd, 32, 1))
        message[ROWS_SENT * q : ROWS_SENT * (q + 1)] = value
        for c, value in ((2 * q, even), (2 * q + 1, odd)):
            low = pltpu.roll(value, (8 * c - 28) % LANES, 1)
            high = pltpu.roll(value, (8 * c + 4 - 96) % LANES, 1)
            sides = jnp.where((lane >= 8 * c) & (lane < 8 * c + 4), low, sides)
            sides = jnp.where((lane >= 8 * c + 4) & (lane < 8 * c + 8), high, sides)
    size = ROWS_SENT * (share // 2)
    message[size : size + ROWS_SENT] = sides
    size = size + ROWS_SENT
    rows0 = zeroth.shape[2] - ROW0
    lane = iota((rows0, LANES), 1)

    def last_columns(i):
        p = PLANE0 + i
        return jnp.where(lane == 0, zeroth[1, p, ROW0:], zeroth[0, p, ROW0:])

    def first_columns(i):
        return zeroth[0, PLANE0 + i, ROW0:]

    last = pack_lanes(last_columns, planes + 1, LANES - SPILL, SPILL + 1, 7, rows0)[0]
    message[size : size + rows0] = last
    first = pack_lanes(first_columns, planes + 1, 0, SPILL + 1, 7, rows0)[0]
    message[size + rows0 :] = first


def gather_z_kernel(count, *refs):
    shares, out = refs[:count], refs[count]
    size = shares[0].shape[0]
    period = 32 * count
    rows2 = 16
    tiles, planes = out.shape[0], out.shape[1]
    lane = iota((size, LANES), 1)
    for slot in range(3):
        totals = [jnp.zeros((size, LANES), F32) for _ in range(tiles)]
        for o in range(count):
            shift = (32 * o + 13 - 42 * slot) % LANES
            turned = pltpu.roll(shares[o][...], shift, 1) if shift else shares[o][...]
            position = ((lane - shift) & (LANES - 1)) - 42 * slot
            inside = (position >= 0) & (position < 38)
            for t in range(tiles):
                lands = lax.rem(position + (32 * o + 13 + period), period) == lane + LANES * t
                totals[t] = totals[t] + jnp.where(inside & lands, turned, 0.0)
        for t in range(tiles):
            for c in range(slot, planes, 3):
                out[t, c] = totals[t][rows2 * (c // 3) : rows2 * (c // 3 + 1)]


ROWS_SENT = 20


def plane_sent(message, share, c):
    lane = iota((ROWS_SENT, LANES), 1)
    pair = message[ROWS_SENT * (c // 2) : ROWS_SENT * (c // 2 + 1)]
    inside = (lane >= 32) & (lane < 96)
    value = jnp.where(inside, pltpu.roll(pair, LANES - 32 if c % 2 else 32, 1), 0.0)
    start = ROWS_SENT * (share // 2)
    sides = message[start : start + ROWS_SENT]
    low = pltpu.roll(sides, (28 - 8 * c) % LANES, 1)
    high = pltpu.roll(sides, (92 - 8 * c) % LANES, 1)
    value = jnp.where((lane >= 28) & (lane < 32), low, value)
    return jnp.where((lane >= 96) & (lane < 100), high, value)


def rows_kernel(sources, strips, *refs):
    inputs, (out, up, down) = refs[:-3], refs[-3:]
    own, messages = inputs[0], inputs[1:]
    planes, share = out.shape[0], own.shape[0]
    read = {}
    for p in range(planes):
        total = None
        for index, offset in sources:
            c = p - 7 - 8 * offset + 2
            if not 0 <= c < share:
                continue
            if (index, c) not in read:
                if index == 0:
                    read[index, c] = own[c, 2 : 2 + ROWS_SENT]
                else:
                    read[index, c] = plane_sent(messages[index], share, c)
            value = read[index, c]
            total = value if total is None else total + value
        out[p] = total
        down[9 * p : 9 * p + 9] = total[0:9]
        up[9 * p : 9 * p + 9] = total[11:20]
    start = ROWS_SENT * (share // 2 + 1)
    inner = (messages[0].shape[0] - start) // 2
    place = 9 * planes
    for k in range(strips):
        for part in range(2):
            begin = start + inner * part
            down[place : place + 6] = messages[k][begin : begin + 6]
            last = begin + inner - 8 - SPILL
            up[place : place + 6] = messages[k][last : last + 6]
            place += 6


def columns_kernel(strips, g1, *refs):
    messages, (above, below), (out, up, down) = refs[:-5], refs[-5:-3], refs[-3:]
    planes, rows = out.shape[0], out.shape[1]
    for p in range(planes):
        out[p] = jnp.zeros((rows, LANES), F32)
        out[p, 6 : 6 + ROWS_SENT] = g1[p]
        out[p, 22:31] = out[p, 22:31] + above[9 * p : 9 * p + 9]
        out[p, 1:10] = out[p, 1:10] + below[9 * p : 9 * p + 9]
    share = planes - 10
    start = ROWS_SENT * (share // 2 + 1)
    inner = (messages[0].shape[0] - start) // 2
    for target, first, part in ((up, 89, 0), (down, 30, 1)):
        place = 0
        for packed in pack_lanes(lambda p: out[p], planes, first, 9, 9, rows):
            target[place : place + rows] = packed
            place += rows
        for k in range(strips):
            begin = start + inner * part
            six = 9 * planes + 6 * (2 * k + part)
            target[place : place + ROW0] = jnp.zeros((ROW0, LANES), F32)
            target[place + ROW0 : place + ROW0 + inner] = messages[k][begin : begin + inner]
            at = place + ROW0 - SPILL
            target[at : at + 6] = target[at : at + 6] + below[six : six + 6]
            at = place + ROW0 + inner - 8
            target[at : at + 6] = target[at : at + 6] + above[six : six + 6]
            place += ROW0 + inner


def fold_x_kernel(count, *refs):
    shares, out = refs[:count], refs[count]
    tiles, period = out.shape[0], out.shape[1]
    for t in range(tiles):
        for x in range(period):
            total = None
            for o in range(count):
                for c in range(10):
                    if (c - 3 + 4 * o) % period == x:
                        value = shares[o][t, c]
                        total = value if total is None else total + value
            out[t, x] = total


def window_kernel(g1, above, below, out, base, first, second):
    planes, rows = base.shape[1], base.shape[2]
    for p in range(planes):
        begin = rows * (p // 14)
        lower = below[begin : begin + rows]
        upper = above[begin : begin + rows]
        total = g1[p] + unpacked(lower, p % 14, 9, 0, 9, 25, rows)
        base[0, p] = total + unpacked(upper, p % 14, 9, 0, 9, 94, rows)
    seventh = 1.0 / 7.0
    sweep(first, base, 1, planes - 1, base, seventh)
    sweep(second, first, 2, planes - 2, base, seventh)
    sweep(first, second, 3, planes - 3, base, seventh)
    sweep(second, first, 4, planes - 4, base, seventh)
    for c in range(out.shape[0]):
        p = 5 + c
        out[c] = (seven_sum(second, p, p - 1, p + 1)[0] * seventh + base[0, p]) * weight(1)


def restrict_lanes(values, width, coarse_width, coarse_tiles):
    out = []
    for s in range(coarse_tiles):
        total = None
        for t, value in enumerate(values):
            matrix = one_hot(
                lambda r, c: ((LANES * t + r) // 2 == lax.rem(LANES * s + c, coarse_width))
                & (LANES * t + r < width)
            )
            term = dot_ones(value, matrix)
            total = term if total is None else total + term
        out.append(total)
    return out


def prolong_lanes(values, width, fine_tiles):
    out = []
    for s in range(fine_tiles):
        total = None
        for t, value in enumerate(values):
            matrix = one_hot(lambda r, c: LANES * t + r == lax.rem(LANES * s + c, width) // 2)
            term = dot_ones(value, matrix)
            total = term if total is None else total + term
        out.append(total)
    return out


def real_waves(count):
    cells = np.arange(count)
    rows, eigenvalues = [], []
    for k in range(count // 2 + 1):
        angle = 2.0 * np.pi * k / count
        rows.append(np.cos(angle * cells))
        eigenvalues.append(2.0 * np.cos(angle))
        if 0 < k < count / 2:
            rows.append(np.sin(angle * cells))
            eigenvalues.append(2.0 * np.cos(angle))
    basis = np.stack(rows)
    basis = basis / np.sqrt(np.sum(basis * basis, axis=1, keepdims=True))
    return basis, np.array(eigenvalues)


def last_level_matrices(planes, rows, width):
    wave_x, value_x = real_waves(planes)
    wave_y, value_y = real_waves(rows)
    wave_z, value_z = real_waves(width)
    into = np.kron(wave_x, np.repeat(wave_y, 1, axis=1))
    level_values = value_x[:, None, None] + value_y[None, :, None] + value_z[None, None, :]
    factor = (1.0 + level_values) / 7.0
    total = sum(factor**k for k in range(COARSE_ITERS)) * weight(LEVELS - 1) * 0.125
    scale = np.zeros((planes * rows, LANES))
    scale[:, :width] = total.reshape(planes * rows, width)
    fine = 2 * width
    tiles = max(1, fine // LANES)
    lanes = np.arange(LANES * tiles)
    to_waves = np.zeros((LANES * tiles, LANES))
    to_waves[:fine, :width] = wave_z.T[lanes[:fine] // 2]
    from_waves = np.zeros((LANES, LANES * tiles))
    from_waves[:width] = wave_z[:, (lanes % fine) // 2]
    to_waves = to_waves.reshape(tiles, LANES, LANES)
    from_waves = from_waves.reshape(LANES, tiles, LANES).transpose(1, 0, 2)
    arrays = (into, into.T, to_waves, from_waves, scale)
    return [jnp.asarray(np.ascontiguousarray(a), F32) for a in arrays]


def solve_last(values, into, back, to_waves, from_waves, scale):
    total = None
    for t, value in enumerate(values):
        term = dot(dot(into[...], value), to_waves[t])
        total = term if total is None else total + term
    total = dot(back[...], total * scale[...])
    return [dot(total, from_waves[t]) for t in range(len(values))]


def solve(level, width, buffers, spectral):
    g, a, b = buffers[level]
    tiles, planes, rows = g.shape[0], g.shape[1], g.shape[2]
    seventh = 1.0 / 7.0
    w = weight(level)
    sweep(a, g, 0, planes, None, seventh, planes)
    sweep(b, a, 0, planes, None, seventh, planes)
    for t in range(tiles):
        for p in range(planes):
            g[t, p] = (g[t, p] + a[t, p] + b[t, p]) * w
    sweep(a, b, 0, planes, None, seventh, planes)
    half = rows // 2
    values = []
    for t in range(tiles):
        parts = []
        for c in range(planes // 2):
            total = a[t, 2 * c, pl.ds(0, half, stride=2), :]
            total = total + a[t, 2 * c, pl.ds(1, half, stride=2), :]
            total = total + a[t, 2 * c + 1, pl.ds(0, half, stride=2), :]
            total = total + a[t, 2 * c + 1, pl.ds(1, half, stride=2), :]
            parts.append(total)
        values.append(jnp.concatenate(parts, axis=0))
    if level == LEVELS - 2:
        values = solve_last(values, *spectral)
    else:
        coarse = buffers[level + 1][0]
        values = restrict_lanes(values, width, width // 2, coarse.shape[0])
        for t, value in enumerate(values):
            for c in range(planes // 2):
                coarse[t, c] = value[half * c : half * (c + 1)] * 0.125
        solve(level + 1, width // 2, buffers, spectral)
        values = [
            jnp.concatenate([coarse[t, c] for c in range(planes // 2)], axis=0)
            for t in range(coarse.shape[0])
        ]
        values = prolong_lanes(values, width, tiles)
    for t, value in enumerate(values):
        for c in range(planes // 2):
            part = value[half * c : half * (c + 1)]
            for p in (2 * c, 2 * c + 1):
                b[t, p, pl.ds(0, half, stride=2), :] = part
                b[t, p, pl.ds(1, half, stride=2), :] = part
        for p in range(planes):
            b[t, p] = b[t, p] + g[t, p]
    sweep(a, b, 0, planes, None, seventh, planes)
    sweep(b, a, 0, planes, None, seventh, planes)
    sweep(a, b, 0, planes, None, seventh, planes)
    for t in range(tiles):
        for p in range(planes):
            g[t, p] = g[t, p] + a[t, p]


def coarse_kernel(count, *refs):
    shares, spectral = refs[:count], refs[count : count + 5]
    out, scratch = refs[count + 5], refs[count + 6 :]
    buffers = {level: scratch[3 * (level - 2) : 3 * (level - 1)] for level in (2, 3)}
    g = buffers[2][0]
    tiles, planes = g.shape[0], g.shape[1]
    for t in range(tiles):
        for p in range(planes):
            for b in range(count):
                value = shares[b][t, p, 0:8] + shares[(b - 1) % count][t, p, 8:16]
                g[t, p, 8 * b : 8 * b + 8] = value
    solve(2, LANES * tiles, buffers, spectral)
    for c in range(out.shape[0]):
        out[c] = g[0, (c - 3) % planes, 0:16]


def correct_kernel(e2, f1, u0_b, u1_a, u1_b, u0_a):
    share1 = f1.shape[0]
    share2 = e2.shape[0]
    rows2 = e2.shape[1]
    value = e2[...].reshape(share2 * rows2, LANES)
    value = dot_ones(value, one_hot(lambda r, c: r == c // 2))
    for c in range(share2):
        part = value[rows2 * c : rows2 * (c + 1)]
        for p in (2 * c, 2 * c + 1):
            u1_a[0, p, pl.ds(0, rows2, stride=2), :] = part
            u1_a[0, p, pl.ds(1, rows2, stride=2), :] = part
    count1 = 2 * share2
    sweep(u1_b, u1_a, 1, count1 - 1)
    sweep(u1_a, u1_b, 2, count1 - 2)
    sweep(u1_b, u1_a, 3, count1 - 3)
    rows1, sent = 24, 20
    parts = []
    for c in range(share1):
        parts.append(f1[c, 6 : 6 + rows1] + u1_b[0, 4 + c, 6 : 6 + rows1] * (1.0 / 343.0))
    value = jnp.concatenate(parts, axis=0)
    main = dot_ones(value, one_hot(lambda r, c: r == 32 + c // 2))
    side = dot_ones(value, one_hot(lambda r, c: r == jnp.where(c < 64, 96 + c // 2, c // 2 - 32)))
    for t, value in enumerate((main, side)):
        for c in range(share1):
            part = value[rows1 * c : rows1 * c + sent]
            for p in (2 * c, 2 * c + 1):
                u0_a[t, p, pl.ds(0, sent, stride=2), :] = part
                u0_a[t, p, pl.ds(1, sent, stride=2), :] = part
    count0 = 2 * share1
    sweep(u0_b, u0_a, 1, count0 - 1)
    sweep(u0_a, u0_b, 2, count0 - 2)
    sweep(u0_b, u0_a, 3, count0 - 3)


def finish_kernel(field, u0_b, f0, beyond, out, pot):
    planes, rows = field.shape[1], field.shape[2]
    scale = 1.0 / 343.0
    for i in range(planes + 1):
        pot[i, 0:rows] = u0_b[0, 4 + i, 4 : 4 + rows] * scale + f0[i, 0:rows]
        if i < planes:
            edge = u0_b[0, 4 + i, 4 + rows : 5 + rows] * scale
            pot[i, rows : rows + 1] = edge + f0[i, rows : rows + 1]
    lane = iota((rows, LANES), 1)
    for i in range(planes):
        here = pot[i, 0:rows]
        out[0, i] = field[0, i] - (pot[i + 1, 0:rows] - here)
        out[1, i] = field[1, i] - (pot[i, 1 : rows + 1] - here)
        last = pltpu.roll(u0_b[1, 4 + i, 4 : 4 + rows], LANES - 1, 1) * scale + beyond[i]
        next_z = jnp.where(lane == LANES - 1, last, pltpu.roll(here, LANES - 1, 1))
        out[2, i] = field[2, i] - (next_z - here)


def fine_place(p, share):
    if p <= SPILL:
        return p
    return p - share + 13 if p >= share - 6 else p + 7


def fine_own_kernel(zeroth, first, second, third, field, main, down, up, field_out, fourth):
    share = main.shape[0]
    field_out[...] = field[...]
    low, high = PLANE0, zeroth.shape[1] - 6
    sweep(fourth, third, low - 4, high + 4)
    clear_margin(fourth, low - 4, high + 4)
    powers = (zeroth, first, second, third, fourth)
    for k in range(share):
        p = low - SPILL + k
        total = seven_sum(fourth, p, p - 1, p + 1, 1)[0] * (weight(0) / 7.0**5)
        for n, power in enumerate(powers):
            if low - n <= p < high + n:
                total = total + power[0, p] * (weight(0) / 7.0**n)
        main[k] = total
        down[k] = total[1:9]
        up[k] = total[40:48]


EDGE = 64
BEYOND = 96


def fine_edge_kernel(sources, above, below, own, out, base, first, second):
    planes, rows = out.shape[0] - 1, base.shape[2]
    lane = iota((rows, LANES), 1)
    strips = 1 + max(index for index, offset in sources)
    start = above.shape[0] - rows * strips
    for k in range(base.shape[1]):
        value = jnp.zeros((rows, LANES), F32)
        for index, offset in sources:
            i = k - SPILL - offset * planes
            if not 0 <= i <= planes:
                continue
            begin = start + rows * index
            turned = pltpu.roll(below[begin : begin + rows], (LANES - SPILL - 7 * i) % LANES, 1)
            value = value + jnp.where((lane >= LANES - SPILL) | (lane == 0), turned, 0.0)
            turned = pltpu.roll(above[begin : begin + rows], (EDGE - 7 * i) % LANES, 1)
            value = value + jnp.where((lane >= EDGE) & (lane <= EDGE + SPILL), turned, 0.0)
            turned = pltpu.roll(own[begin : begin + rows], (BEYOND - SPILL - 7 * i) % LANES, 1)
            value = value + jnp.where((lane >= BEYOND - SPILL) & (lane <= BEYOND), turned, 0.0)
        base[0, k] = value
    seventh = 1.0 / 7.0
    high = base.shape[1]
    sweep(first, base, 1, high - 1, base, seventh)
    sweep(second, first, 2, high - 2, base, seventh)
    sweep(first, second, 3, high - 3, base, seventh)
    sweep(second, first, 4, high - 4, base, seventh)
    kept = out.shape[1]
    for i in range(planes + 1):
        p = SPILL + i
        value = (seven_sum(second, p, p - 1, p + 1)[0] * seventh + base[0, p]) * weight(0)
        out[i] = value[ROW0 : ROW0 + kept]


def turned_to_last(value, lane):
    return pltpu.roll(value, LANES - 1 - lane, 1)


def fine_sum_kernel(f0, below_x, above_x, work, out, beyond):
    planes, rows = beyond.shape[0], beyond.shape[1]
    lane = iota((rows, LANES), 1)
    lane1 = iota((1, LANES), 1)
    for i in range(planes + 1):
        value = f0[fine_place(i + SPILL, planes + 11)]
        if i <= SPILL:
            value = value + below_x[1 + i]
        if i >= planes - SPILL:
            value = value + above_x[i - (planes - SPILL)]
        part = work[i, 0:rows]
        turned = pltpu.roll(part, EDGE, 1)
        value = value + jnp.where(lane <= SPILL, part, 0.0)
        out[i, 0:rows] = value + jnp.where(lane >= LANES - SPILL, turned, 0.0)
        if i < planes:
            beyond[i] = turned_to_last(part, EDGE) + turned_to_last(part, BEYOND)
            row = f0[6, i + SPILL : i + SPILL + 1]
            if i <= SPILL:
                row = row + below_x[0, i + SPILL + planes : i + SPILL + planes + 1]
            if i >= planes - SPILL:
                row = row + above_x[6, i + SPILL - planes : i + SPILL - planes + 1]
            part = work[i, rows : rows + 1]
            row = row + jnp.where(lane1 <= SPILL, part, 0.0)
            row = row + jnp.where(lane1 >= LANES - SPILL, pltpu.roll(part, EDGE, 1), 0.0)
            out[i, rows : rows + 1] = row


def fine_y_kernel(main, above, below, out, work):
    share = main.shape[0]
    rows = out.shape[1]
    out[6] = jnp.zeros((rows, LANES), F32)
    for p in range(share):
        work[p] = main[p]
        work[p, 33:41] = work[p, 33:41] + above[p]
        work[p, 8:16] = work[p, 8:16] + below[p]
        out[fine_place(p, share)] = work[p, ROW0 : ROW0 + rows]
        out[6, p : p + 1] = work[p, ROW0 + rows : ROW0 + rows + 1]


def body(field):
    nx, ny, nz = field.shape[1:]
    size_x, size_y, size_z = lax.axis_size("gx"), lax.axis_size("gy"), lax.axis_size("gz")
    n1 = nx // 2
    share1 = n1 + 4
    rows0 = ny + 16
    rows1 = ny // 2 + 8
    planes0 = nx + 13

    def from_offset(value, axis, offset):
        count = lax.axis_size(axis)
        pairs = [(source, (source - offset) % count) for source in range(count)]
        return lax.ppermute(value, axis, pairs)

    level0 = (2, planes0, rows0, LANES)
    level1 = (1, n1 + 12, ny // 2 + 16, LANES)
    packed = -(-(n1 // 2 + 6) // 3) * 16
    inner0 = rows0 - ROW0
    sent1 = ROWS_SENT * (share1 // 2 + 1)
    message, g2, g1, *powers = call(
        spread_kernel,
        [shape(sent1 + 2 * inner0, LANES), shape(packed, LANES),
         shape(share1, rows1, LANES)] + [shape(*level0)] * 4,
        [level1, level1],
        2.9,
        field,
    )
    shares = [g2] + [from_offset(g2, "gz", o) for o in range(1, size_z)]
    messages = {0: message}
    sources = []
    for o in (0, 1, -1, 2, -2):
        key = [k for k in messages if k % size_x == o % size_x]
        if not key:
            messages[o] = from_offset(message, "gx", o)
            key = [o]
        sources.append((list(messages).index(key[0]), o))
    messages = list(messages.values())
    strips = min(3, size_x)
    planes1 = n1 + 14
    sent_y = 9 * planes1 + 12 * strips
    rows_g1, up, down = call(
        functools.partial(rows_kernel, tuple(sources), strips),
        [shape(planes1, ROWS_SENT, LANES), shape(sent_y, LANES), shape(sent_y, LANES)],
        [],
        0.2,
        g1, *messages,
    )
    window = (1, planes1, ny // 2 + 16, LANES)
    sent_z = window[2] * -(-planes1 // 14) + rows0 * strips
    window_g1, up, down = call(
        functools.partial(columns_kernel, strips),
        [shape(*window[1:]), shape(sent_z, LANES), shape(sent_z, LANES)],
        [],
        0.3,
        rows_g1, *messages[:strips], from_offset(down, "gy", 1), from_offset(up, "gy", -1),
    )
    above = from_offset(down, "gz", 1)
    below = from_offset(up, "gz", -1)
    f1 = call(
        window_kernel,
        shape(share1, *window[2:]),
        [window, window, window],
        0.9,
        window_g1, above, below,
    )
    share0 = nx + 11
    main, f_down, f_up, kept = call(
        fine_own_kernel,
        [shape(share0, rows0, LANES), shape(share0, 8, LANES), shape(share0, 8, LANES),
         shape(*field.shape)],
        [level0],
        3.0,
        *powers, field,
        after=(messages[1],),
    )
    f_above = from_offset(f_down, "gy", 1)
    f_below = from_offset(f_up, "gy", -1)

    tiles = size_z * 32 // LANES
    g2 = call(
        functools.partial(gather_z_kernel, size_z),
        shape(tiles, n1 // 2 + 6, 16, LANES),
        [],
        0.15,
        *shares,
        after=(rows_g1, main,),
    )
    shares = [g2] + [from_offset(g2, "gx", o) for o in range(1, size_x)]
    g2 = call(
        functools.partial(fold_x_kernel, size_x),
        shape(tiles, 4 * size_x, 16, LANES),
        [],
        0.05,
        *shares,
        after=(window_g1,),
    )
    shares = [g2] + [from_offset(g2, "gy", o) for o in range(1, size_y)]

    f0 = call(
        fine_y_kernel,
        shape(share0 + 1, ny, LANES),
        [(share0, rows0, LANES)],
        0.4,
        main, f_above, f_below,
    )
    if size_x == 2:
        other = from_offset(f0[0:13], "gx", 1)
        f_above, f_below = other[0:7], other[6:13]
    else:
        f_above = from_offset(f0[0:7], "gx", 1)
        f_below = from_offset(f0[6:13], "gx", -1)
    edges = (1, nx + 11, rows0, LANES)
    edge = call(
        functools.partial(fine_edge_kernel, tuple(sources[:3])),
        shape(nx + 1, ny + 8, LANES),
        [edges, edges, edges],
        1.9,
        above, below, up,
    )
    f0, beyond = call(
        fine_sum_kernel,
        [shape(nx + 1, ny + 8, LANES), shape(nx, ny, LANES)],
        [],
        0.3,
        f0, f_below, f_above, edge,
    )

    scratch = []
    for level in (2, 3):
        cut = 2 ** (level - 2)
        extent = (max(1, tiles // cut), 4 * size_x // cut, 8 * size_y // cut, LANES)
        scratch.extend([extent] * 3)
    e2 = call(
        functools.partial(coarse_kernel, size_y),
        shape(n1 // 2 + 6, 16, LANES),
        scratch,
        2.2,
        *shares, *last_level_matrices(size_x, 2 * size_y, 8 * size_z),
        after=(f1,),
    )
    fine = (2, nx + 8, ny + 8, LANES)
    correction = call(
        correct_kernel,
        shape(*fine),
        [level1, level1, fine],
        2.2,
        e2, f1,
    )
    return call(
        finish_kernel,
        shape(*field.shape),
        [(nx + 1, ny + 8, LANES)],
        0.9,
        kept, correction, f0, beyond,
    )


def solution(mesh):
    in_specs = (P(None, "gx", "gy", "gz"),)
    out_specs = P(None, "gx", "gy", "gz")
    return jax.shard_map(body, mesh=mesh, in_specs=in_specs, out_specs=out_specs, check_vma=False)
```

```python
import functools

import jax
import jax.numpy as jnp
import numpy as np
from jax import lax
from jax.experimental import pallas as pl
from jax.experimental.pallas import tpu as pltpu
from jax.sharding import PartitionSpec as P

LEVELS = 5
SWEEPS = 3
COARSE_ITERS = 24


F32 = jnp.float32
LANES = 128
VMEM_LIMIT = 16 * 1024 * 1024
PEAK_FLOPS_PER_US = 1150000000.0


def weight(level):
    return 4.0**level / 7.0


def shape(*extent):
    return jax.ShapeDtypeStruct(extent, F32)


def call(kernel, outs, scratch, microseconds, *args, after=()):
    flops = int(microseconds * PEAK_FLOPS_PER_US)
    if after:
        inner, first, last = kernel, len(args), len(args) + len(after)

        def kernel(*refs):
            inner(*refs[:first], *refs[last:])

        args = (*args, *after)
    return pl.pallas_call(
        kernel,
        out_shape=outs,
        scratch_shapes=[pltpu.VMEM(s, F32) for s in scratch],
        compiler_params=pltpu.CompilerParams(vmem_limit_bytes=VMEM_LIMIT),
        cost_estimate=pl.CostEstimate(flops=flops, bytes_accessed=0, transcendentals=0),
    )(*args)


def iota(extent, dim):
    return lax.broadcasted_iota(jnp.int32, extent, dim)


def one_hot(condition):
    rows = iota((LANES, LANES), 0)
    columns = iota((LANES, LANES), 1)
    return jnp.where(condition(rows, columns), 1.0, 0.0).astype(jnp.bfloat16)


def dot(left, right):
    return lax.dot_general(
        left,
        right,
        (((1,), (0,)), ((), ())),
        precision=lax.Precision.HIGHEST,
        preferred_element_type=F32,
    )


def dot_ones(left, right):
    large = left.astype(jnp.bfloat16)
    rest = left - large.astype(F32)
    middle = rest.astype(jnp.bfloat16)
    small = (rest - middle.astype(F32)).astype(jnp.bfloat16)
    return lax.dot_general(
        jnp.concatenate([large, middle, small], axis=1),
        jnp.concatenate([right, right, right], axis=0),
        (((1,), (0,)), ((), ())),
        preferred_element_type=F32,
    )


def seven_sum(source, plane, below, above, wanted=None):
    tiles = source.shape[0]
    rows = source.shape[2]
    center = [source[t, plane] for t in range(tiles)]
    left = [pltpu.roll(v, 1, 1) for v in center]
    right = [pltpu.roll(v, LANES - 1, 1) for v in center]
    if tiles > 1:
        lane = iota((rows, LANES), 1)
        left = [jnp.where(lane == 0, left[t - 1], left[t]) for t in range(tiles)]
        right = [
            jnp.where(lane == LANES - 1, right[(t + 1) % tiles], right[t]) for t in range(tiles)
        ]
    out = []
    for t in range(tiles if wanted is None else wanted):
        v = center[t]
        total = v + (source[t, below] + source[t, above])
        total = total + (pltpu.roll(v, 1, 0) + pltpu.roll(v, rows - 1, 0))
        out.append(total + (left[t] + right[t]))
    return out


def sweep(target, source, low, high, base=None, scale=None, period=None, span=None):
    for plane in range(low, high):
        below, above = plane - 1, plane + 1
        if period is not None:
            below, above = below % period, above % period
        for t, value in enumerate(seven_sum(source, plane, below, above)):
            if scale is not None:
                value = value * scale
            if base is not None and (span is None or span[0] <= plane < span[1]):
                value = value + base[t, plane]
            target[t, plane] = value


PLANE0 = 6
ROW0 = 8
SPILL = 5


def fill_source(field, target):
    planes, rows = field.shape[1], field.shape[2]
    lane = iota((rows, LANES), 1)
    row = iota((rows, LANES), 0)
    row8 = iota((8, LANES), 0)
    zero8 = jnp.zeros((8, LANES), F32)
    zeros = jnp.zeros((rows, LANES), F32)

    def one_plane(i, before):
        along_x, along_y, along_z = field[0, i], field[1, i], field[2, i]
        value = before - along_x - along_y - along_z
        value = value + jnp.where(row == 0, 0.0, pltpu.roll(along_y, 1, 0))
        turned = pltpu.roll(along_z, 1, 1)
        value = value + jnp.where(lane == 0, 0.0, turned)
        p = PLANE0 + i
        target[0, p, 0:ROW0] = zero8
        target[0, p, ROW0 : ROW0 + rows] = value
        last = pltpu.roll(along_y[rows - 8 : rows], 1, 0)
        target[0, p, ROW0 + rows : ROW0 + rows + 8] = jnp.where(row8 == 0, last, 0.0)
        target[1, p, 0:ROW0] = zero8
        target[1, p, ROW0 : ROW0 + rows] = jnp.where(lane == 0, turned, 0.0)
        target[1, p, ROW0 + rows : ROW0 + rows + 8] = zero8

    for i in range(planes):
        one_plane(i, field[0, i - 1] if i else zeros)
    p = PLANE0 + planes
    target[0, p] = jnp.zeros(target.shape[2:], F32)
    target[1, p] = jnp.zeros(target.shape[2:], F32)
    target[0, p, ROW0 : ROW0 + rows] = field[0, planes - 1]


def clear_planes(target, planes):
    for t in range(target.shape[0]):
        for p in planes:
            target[t, p] = jnp.zeros(target.shape[2:], F32)


def pack_lanes(read, count, first, width, spacing, rows):
    lane = iota((rows, LANES), 1)
    per_tile = LANES // spacing
    tiles = []
    for start in range(0, count, per_tile):
        packed = jnp.zeros((rows, LANES), F32)
        for k in range(min(per_tile, count - start)):
            turned = pltpu.roll(read(start + k), (spacing * k - first) % LANES, 1)
            inside = (lane >= spacing * k) & (lane < spacing * k + width)
            packed = jnp.where(inside, turned, packed)
        tiles.append(packed)
    return tiles


def unpacked(packed, k, spacing, offset, width, first, rows):
    lane = iota((rows, LANES), 1)
    turned = pltpu.roll(packed, (first - spacing * k - offset) % LANES, 1)
    inside = (lane >= first) & (lane < first + width)
    return jnp.where(inside, turned, 0.0)


def clear_margin(target, low, high):
    clear_planes(target, (low - 2, low - 1, high, high + 1))


def spread_kernel(field, message, g2_out, g1_out, zeroth, first, second, third, g1_a, g1_b):
    planes = field.shape[1]
    fill_source(field, zeroth)
    low, high = PLANE0, PLANE0 + planes + 1
    clear_margin(zeroth, low, high)
    powers = (zeroth, first, second, third)
    for k in (1, 2, 3):
        sweep(powers[k], powers[k - 1], low - k, high + k)
        clear_margin(powers[k], low - k, high + k)

    n1 = planes // 2
    rows1 = first.shape[2] // 2
    pieces = []
    for t in range(2):
        parts = []
        for c in range(-2, n1 + 2):
            p = PLANE0 + 2 * c
            total = third[t, p, pl.ds(0, rows1, stride=2), :]
            total = total + third[t, p, pl.ds(1, rows1, stride=2), :]
            total = total + third[t, p + 1, pl.ds(0, rows1, stride=2), :]
            total = total + third[t, p + 1, pl.ds(1, rows1, stride=2), :]
            parts.append(total)
        pieces.append(jnp.concatenate(parts, axis=0))
    main = one_hot(lambda r, c: c == 32 + r // 2)
    side = one_hot(lambda r, c: c == jnp.where(r < 64, 96 + r // 2, r // 2 - 32))
    g1 = (dot_ones(pieces[0], main) + dot_ones(pieces[1], side)) * (0.125 / 343.0)
    share = n1 + 4
    g1 = g1.reshape(share, rows1, LANES)
    g1_out[...] = g1

    clear_planes(g1_a, range(g1_a.shape[1]))
    clear_planes(g1_b, range(g1_b.shape[1]))
    for c in range(share):
        g1_a[0, 4 + c, 4 : 4 + rows1] = g1[c]
    sweep(g1_b, g1_a, 3, 5 + share)
    sweep(g1_a, g1_b, 2, 6 + share)
    sweep(g1_b, g1_a, 1, 7 + share)
    rows2 = g1_a.shape[2] // 2
    parts = []
    for c in range(g1_a.shape[1] // 2):
        total = g1_b[0, 2 * c, pl.ds(0, rows2, stride=2), :]
        total = total + g1_b[0, 2 * c, pl.ds(1, rows2, stride=2), :]
        total = total + g1_b[0, 2 * c + 1, pl.ds(0, rows2, stride=2), :]
        total = total + g1_b[0, 2 * c + 1, pl.ds(1, rows2, stride=2), :]
        parts.append(total)
    groups = -(-len(parts) // 3)
    parts.extend([jnp.zeros((rows2, LANES), F32)] * (3 * groups - len(parts)))
    g2 = None
    for slot in range(3):
        matrix = one_hot(
            lambda r, c: (c == r // 2 - 13 + 42 * slot) & (r // 2 >= 13) & (r // 2 < 51)
        )
        term = dot_ones(jnp.concatenate(parts[slot::3], axis=0), matrix)
        g2 = term if g2 is None else g2 + term
    g2_out[...] = g2 * (0.125 / 343.0)
    lane = iota((ROWS_SENT, LANES), 1)
    sides = jnp.zeros((ROWS_SENT, LANES), F32)
    for q in range(share // 2):
        even, odd = g1_out[2 * q, 2 : 2 + ROWS_SENT], g1_out[2 * q + 1, 2 : 2 + ROWS_SENT]
        value = jnp.where(lane < 64, pltpu.roll(even, LANES - 32, 1), pltpu.roll(odd, 32, 1))
        message[ROWS_SENT * q : ROWS_SENT * (q + 1)] = value
        for c, value in ((2 * q, even), (2 * q + 1, odd)):
            low = pltpu.roll(value, (8 * c - 28) % LANES, 1)
            high = pltpu.roll(value, (8 * c + 4 - 96) % LANES, 1)
            sides = jnp.where((lane >= 8 * c) & (lane < 8 * c + 4), low, sides)
            sides = jnp.where((lane >= 8 * c + 4) & (lane < 8 * c + 8), high, sides)
    size = ROWS_SENT * (share // 2)
    message[size : size + ROWS_SENT] = sides
    size = size + ROWS_SENT
    rows0 = zeroth.shape[2] - ROW0
    lane = iota((rows0, LANES), 1)

    def last_columns(i):
        p = PLANE0 + i
        return jnp.where(lane == 0, zeroth[1, p, ROW0:], zeroth[0, p, ROW0:])

    def first_columns(i):
        return zeroth[0, PLANE0 + i, ROW0:]

    last = pack_lanes(last_columns, planes + 1, LANES - SPILL, SPILL + 1, 7, rows0)[0]
    message[size : size + rows0] = last
    first = pack_lanes(first_columns, planes + 1, 0, SPILL + 1, 7, rows0)[0]
    message[size + rows0 :] = first


def gather_z_kernel(count, *refs):
    shares, out = refs[:count], refs[count]
    size = shares[0].shape[0]
    period = 32 * count
    rows2 = 16
    tiles, planes = out.shape[0], out.shape[1]
    lane = iota((size, LANES), 1)
    for slot in range(3):
        totals = [jnp.zeros((size, LANES), F32) for _ in range(tiles)]
        for o in range(count):
            shift = (32 * o + 13 - 42 * slot) % LANES
            turned = pltpu.roll(shares[o][...], shift, 1) if shift else shares[o][...]
            position = ((lane - shift) & (LANES - 1)) - 42 * slot
            inside = (position >= 0) & (position < 38)
            for t in range(tiles):
                lands = lax.rem(position + (32 * o + 13 + period), period) == lane + LANES * t
                totals[t] = totals[t] + jnp.where(inside & lands, turned, 0.0)
        for t in range(tiles):
            for c in range(slot, planes, 3):
                out[t, c] = totals[t][rows2 * (c // 3) : rows2 * (c // 3 + 1)]


ROWS_SENT = 20


def plane_sent(message, share, c):
    lane = iota((ROWS_SENT, LANES), 1)
    pair = message[ROWS_SENT * (c // 2) : ROWS_SENT * (c // 2 + 1)]
    inside = (lane >= 32) & (lane < 96)
    value = jnp.where(inside, pltpu.roll(pair, LANES - 32 if c % 2 else 32, 1), 0.0)
    start = ROWS_SENT * (share // 2)
    sides = message[start : start + ROWS_SENT]
    low = pltpu.roll(sides, (28 - 8 * c) % LANES, 1)
    high = pltpu.roll(sides, (92 - 8 * c) % LANES, 1)
    value = jnp.where((lane >= 28) & (lane < 32), low, value)
    return jnp.where((lane >= 96) & (lane < 100), high, value)


def rows_kernel(sources, strips, *refs):
    inputs, (out, up, down) = refs[:-3], refs[-3:]
    own, messages = inputs[0], inputs[1:]
    planes, share = out.shape[0], own.shape[0]
    read = {}
    for p in range(planes):
        total = None
        for index, offset in sources:
            c = p - 7 - 8 * offset + 2
            if not 0 <= c < share:
                continue
            if (index, c) not in read:
                if index == 0:
                    read[index, c] = own[c, 2 : 2 + ROWS_SENT]
                else:
                    read[index, c] = plane_sent(messages[index], share, c)
            value = read[index, c]
            total = value if total is None else total + value
        out[p] = total
        down[9 * p : 9 * p + 9] = total[0:9]
        up[9 * p : 9 * p + 9] = total[11:20]
    start = ROWS_SENT * (share // 2 + 1)
    inner = (messages[0].shape[0] - start) // 2
    place = 9 * planes
    for k in range(strips):
        for part in range(2):
            begin = start + inner * part
            down[place : place + 6] = messages[k][begin : begin + 6]
            last = begin + inner - 8 - SPILL
            up[place : place + 6] = messages[k][last : last + 6]
            place += 6


def columns_kernel(strips, g1, *refs):
    messages, (above, below), (out, up, down) = refs[:-5], refs[-5:-3], refs[-3:]
    planes, rows = out.shape[0], out.shape[1]
    for p in range(planes):
        out[p] = jnp.zeros((rows, LANES), F32)
        out[p, 6 : 6 + ROWS_SENT] = g1[p]
        out[p, 22:31] = out[p, 22:31] + above[9 * p : 9 * p + 9]
        out[p, 1:10] = out[p, 1:10] + below[9 * p : 9 * p + 9]
    share = planes - 10
    start = ROWS_SENT * (share // 2 + 1)
    inner = (messages[0].shape[0] - start) // 2
    for target, first, part in ((up, 89, 0), (down, 30, 1)):
        place = 0
        for packed in pack_lanes(lambda p: out[p], planes, first, 9, 9, rows):
            target[place : place + rows] = packed
            place += rows
        for k in range(strips):
            begin = start + inner * part
            six = 9 * planes + 6 * (2 * k + part)
            target[place : place + ROW0] = jnp.zeros((ROW0, LANES), F32)
            target[place + ROW0 : place + ROW0 + inner] = messages[k][begin : begin + inner]
            at = place + ROW0 - SPILL
            target[at : at + 6] = target[at : at + 6] + below[six : six + 6]
            at = place + ROW0 + inner - 8
            target[at : at + 6] = target[at : at + 6] + above[six : six + 6]
            place += ROW0 + inner


def fold_x_kernel(count, *refs):
    shares, out = refs[:count], refs[count]
    tiles, period = out.shape[0], out.shape[1]
    for t in range(tiles):
        for x in range(period):
            total = None
            for o in range(count):
                for c in range(10):
                    if (c - 3 + 4 * o) % period == x:
                        value = shares[o][t, c]
                        total = value if total is None else total + value
            out[t, x] = total


def window_kernel(g1, above, below, out, base, first, second):
    planes, rows = base.shape[1], base.shape[2]
    lane = iota((rows, LANES), 1)
    kept_lanes = ((lane >= 25) & (lane < 34)) | ((lane >= 94) & (lane < 103))
    turned = []
    for begin in range(0, rows * -(-planes // 14), rows):
        turned.append((pltpu.roll(below[begin : begin + rows], 25, 1),
                       pltpu.roll(above[begin : begin + rows], 94, 1)))
    for p in range(planes):
        lower, upper = turned[p // 14]
        shift = 9 * (p % 14)
        term = jnp.where(((lane - shift) & (LANES - 1)) < 64, lower, upper)
        term = pltpu.roll(term, (LANES - shift) % LANES, 1) if shift else term
        base[0, p] = g1[p] + jnp.where(kept_lanes, term, 0.0)
    seventh = 1.0 / 7.0
    sweep(first, base, 1, planes - 1, base, seventh)
    sweep(second, first, 2, planes - 2, base, seventh)
    sweep(first, second, 3, planes - 3, base, seventh)
    sweep(second, first, 4, planes - 4, base, seventh)
    for c in range(out.shape[0]):
        p = 5 + c
        out[c] = (seven_sum(second, p, p - 1, p + 1)[0] * seventh + base[0, p]) * weight(1)


def restrict_lanes(values, width, coarse_width, coarse_tiles):
    out = []
    for s in range(coarse_tiles):
        total = None
        for t, value in enumerate(values):
            matrix = one_hot(
                lambda r, c: ((LANES * t + r) // 2 == lax.rem(LANES * s + c, coarse_width))
                & (LANES * t + r < width)
            )
            term = dot_ones(value, matrix)
            total = term if total is None else total + term
        out.append(total)
    return out


def prolong_lanes(values, width, fine_tiles):
    out = []
    for s in range(fine_tiles):
        total = None
        for t, value in enumerate(values):
            matrix = one_hot(lambda r, c: LANES * t + r == lax.rem(LANES * s + c, width) // 2)
            term = dot_ones(value, matrix)
            total = term if total is None else total + term
        out.append(total)
    return out


def swept(values):
    rows = values[0].shape[0]
    out = []
    for p, v in enumerate(values):
        total = v + (values[p - 1] + values[(p + 1) % len(values)])
        total = total + (pltpu.roll(v, 1, 0) + pltpu.roll(v, rows - 1, 0))
        out.append((total + (pltpu.roll(v, 1, 1) + pltpu.roll(v, LANES - 1, 1))) * (1.0 / 7.0))
    return out


def real_waves(count):
    cells = np.arange(count)
    rows, eigenvalues = [], []
    for k in range(count // 2 + 1):
        angle = 2.0 * np.pi * k / count
        rows.append(np.cos(angle * cells))
        eigenvalues.append(2.0 * np.cos(angle))
        if 0 < k < count / 2:
            rows.append(np.sin(angle * cells))
            eigenvalues.append(2.0 * np.cos(angle))
    basis = np.stack(rows)
    basis = basis / np.sqrt(np.sum(basis * basis, axis=1, keepdims=True))
    return basis, np.array(eigenvalues)


def last_level_matrices(planes, rows, width):
    wave_x, value_x = real_waves(planes)
    wave_y, value_y = real_waves(rows)
    wave_z, value_z = real_waves(width)
    into = np.kron(np.repeat(wave_x, 2, axis=1), np.repeat(wave_y, 2, axis=1))
    level_values = value_x[:, None, None] + value_y[None, :, None] + value_z[None, None, :]
    factor = (1.0 + level_values) / 7.0
    total = sum(factor**k for k in range(COARSE_ITERS)) * weight(LEVELS - 1) * 0.125
    scale = np.zeros((planes * rows, LANES))
    scale[:, :width] = total.reshape(planes * rows, width)
    fine = 2 * width
    tiles = max(1, fine // LANES)
    lanes = np.arange(LANES * tiles)
    to_waves = np.zeros((LANES * tiles, LANES))
    to_waves[:fine, :width] = wave_z.T[lanes[:fine] // 2]
    from_waves = np.zeros((LANES, LANES * tiles))
    from_waves[:width] = wave_z[:, (lanes % fine) // 2]
    to_waves = to_waves.reshape(tiles, LANES, LANES)
    from_waves = from_waves.reshape(LANES, tiles, LANES).transpose(1, 0, 2)
    arrays = (into, into.T, to_waves, from_waves, scale)
    return [jnp.asarray(np.ascontiguousarray(a), F32) for a in arrays]


def solve_last(values, into, back, to_waves, from_waves, scale):
    waves = dot(dot(into[...], values), to_waves[0])
    return dot(dot(back[...], waves * scale[...]), from_waves[0])


def solve(level, width, buffers, spectral):
    g, a, b = buffers[level]
    tiles, planes, rows = g.shape[0], g.shape[1], g.shape[2]
    seventh = 1.0 / 7.0
    w = weight(level)
    if level == LEVELS - 2:
        source = [g[0, p] for p in range(planes)]
        first = swept(source)
        second = swept(first)
        third = swept(second)
        before = [(x + y + z) * w for x, y, z in zip(source, first, second)]
        values = solve_last(jnp.concatenate(third, axis=0), *spectral)
        error = [before[p] + values[rows * p : rows * (p + 1)] for p in range(planes)]
        error = swept(swept(swept(error)))
        for p in range(planes):
            g[0, p] = before[p] + error[p]
        return
    sweep(a, g, 0, planes, None, seventh, planes)
    sweep(b, a, 0, planes, None, seventh, planes)
    for t in range(tiles):
        for p in range(planes):
            g[t, p] = (g[t, p] + a[t, p] + b[t, p]) * w
    sweep(a, b, 0, planes, None, seventh, planes)
    half = rows // 2
    values = []
    for t in range(tiles):
        parts = []
        for c in range(planes // 2):
            total = a[t, 2 * c, pl.ds(0, half, stride=2), :]
            total = total + a[t, 2 * c, pl.ds(1, half, stride=2), :]
            total = total + a[t, 2 * c + 1, pl.ds(0, half, stride=2), :]
            total = total + a[t, 2 * c + 1, pl.ds(1, half, stride=2), :]
            parts.append(total)
        values.append(jnp.concatenate(parts, axis=0))
    coarse = buffers[level + 1][0]
    values = restrict_lanes(values, width, width // 2, coarse.shape[0])
    for t, value in enumerate(values):
        for c in range(planes // 2):
            coarse[t, c] = value[half * c : half * (c + 1)] * 0.125
    solve(level + 1, width // 2, buffers, spectral)
    values = [
        jnp.concatenate([coarse[t, c] for c in range(planes // 2)], axis=0)
        for t in range(coarse.shape[0])
    ]
    values = prolong_lanes(values, width, tiles)
    for t, value in enumerate(values):
        for c in range(planes // 2):
            part = value[half * c : half * (c + 1)]
            for p in (2 * c, 2 * c + 1):
                b[t, p, pl.ds(0, half, stride=2), :] = part
                b[t, p, pl.ds(1, half, stride=2), :] = part
        for p in range(planes):
            b[t, p] = b[t, p] + g[t, p]
    sweep(a, b, 0, planes, None, seventh, planes)
    sweep(b, a, 0, planes, None, seventh, planes)
    sweep(a, b, 0, planes, None, seventh, planes)
    for t in range(tiles):
        for p in range(planes):
            g[t, p] = g[t, p] + a[t, p]


def coarse_kernel(count, *refs):
    shares, spectral = refs[:count], refs[count : count + 5]
    out, scratch = refs[count + 5], refs[count + 6 :]
    buffers = {level: scratch[3 * (level - 2) : 3 * (level - 1)] for level in (2, 3)}
    g = buffers[2][0]
    tiles, planes = g.shape[0], g.shape[1]
    for t in range(tiles):
        for p in range(planes):
            for b in range(count):
                value = shares[b][t, p, 0:8] + shares[(b - 1) % count][t, p, 8:16]
                g[t, p, 8 * b : 8 * b + 8] = value
    solve(2, LANES * tiles, buffers, spectral)
    for c in range(out.shape[0]):
        out[c] = g[0, (c - 3) % planes, 0:16]


def correct_kernel(e2, f1, u0_b, u1_a, u1_b, u0_a):
    share1 = f1.shape[0]
    share2 = e2.shape[0]
    rows2 = e2.shape[1]
    value = e2[...].reshape(share2 * rows2, LANES)
    value = dot_ones(value, one_hot(lambda r, c: r == c // 2))
    for c in range(share2):
        part = value[rows2 * c : rows2 * (c + 1)]
        for p in (2 * c, 2 * c + 1):
            u1_a[0, p, pl.ds(0, rows2, stride=2), :] = part
            u1_a[0, p, pl.ds(1, rows2, stride=2), :] = part
    count1 = 2 * share2
    sweep(u1_b, u1_a, 1, count1 - 1)
    sweep(u1_a, u1_b, 2, count1 - 2)
    sweep(u1_b, u1_a, 3, count1 - 3)
    rows1, sent = 24, 20
    parts = []
    for c in range(share1):
        parts.append(f1[c, 6 : 6 + rows1] + u1_b[0, 4 + c, 6 : 6 + rows1] * (1.0 / 343.0))
    value = jnp.concatenate(parts, axis=0)
    main = dot_ones(value, one_hot(lambda r, c: r == 32 + c // 2))
    side = dot_ones(value, one_hot(lambda r, c: r == jnp.where(c < 64, 96 + c // 2, c // 2 - 32)))
    for t, value in enumerate((main, side)):
        for c in range(share1):
            part = value[rows1 * c : rows1 * c + sent]
            for p in (2 * c, 2 * c + 1):
                u0_a[t, p, pl.ds(0, sent, stride=2), :] = part
                u0_a[t, p, pl.ds(1, sent, stride=2), :] = part
    count0 = 2 * share1
    sweep(u0_b, u0_a, 1, count0 - 1)
    sweep(u0_a, u0_b, 2, count0 - 2)
    sweep(u0_b, u0_a, 3, count0 - 3)


def finish_kernel(field, u0_b, f0, beyond, out, pot):
    planes, rows = field.shape[1], field.shape[2]
    scale = 1.0 / 343.0
    for i in range(planes + 1):
        pot[i, 0:rows] = u0_b[0, 4 + i, 4 : 4 + rows] * scale + f0[i, 0:rows]
        if i < planes:
            edge = u0_b[0, 4 + i, 4 + rows : 5 + rows] * scale
            pot[i, rows : rows + 1] = edge + f0[i, rows : rows + 1]
    lane = iota((rows, LANES), 1)
    for i in range(planes):
        here = pot[i, 0:rows]
        out[0, i] = field[0, i] - (pot[i + 1, 0:rows] - here)
        out[1, i] = field[1, i] - (pot[i, 1 : rows + 1] - here)
        last = pltpu.roll(u0_b[1, 4 + i, 4 : 4 + rows], LANES - 1, 1) * scale + beyond[i]
        next_z = jnp.where(lane == LANES - 1, last, pltpu.roll(here, LANES - 1, 1))
        out[2, i] = field[2, i] - (next_z - here)


def fine_place(p, share):
    if p <= SPILL:
        return p
    return p - share + 13 if p >= share - 6 else p + 7


def fine_own_kernel(zeroth, first, second, third, field, main, down, up, field_out, fourth):
    share = main.shape[0]
    field_out[...] = field[...]
    low, high = PLANE0, zeroth.shape[1] - 6
    sweep(fourth, third, low - 4, high + 4)
    clear_margin(fourth, low - 4, high + 4)
    powers = (zeroth, first, second, third, fourth)
    for k in range(share):
        p = low - SPILL + k
        total = seven_sum(fourth, p, p - 1, p + 1, 1)[0] * (weight(0) / 7.0**5)
        for n, power in enumerate(powers):
            if low - n <= p < high + n:
                total = total + power[0, p] * (weight(0) / 7.0**n)
        main[k] = total
        down[k] = total[1:9]
        up[k] = total[40:48]


GROUPS = 3
GROUP_LANES = 42
LOW_END, HIGH_AT, OWN_AT = 5, 16, 22


def fine_edge_kernel(sources, planes, above, below, own, out, base, first, second):
    rows = base.shape[2]
    size = out.shape[0]
    lane = iota((rows, LANES), 1)
    strips = 1 + max(index for index, offset in sources)
    start = above.shape[0] - rows * strips
    turned = []
    for index in range(strips):
        begin = start + rows * index
        turned.append((below[begin : begin + rows],
                       pltpu.roll(above[begin : begin + rows], HIGH_AT, 1),
                       pltpu.roll(own[begin : begin + rows], OWN_AT, 1)))
    spread = SPILL + 1
    for j in range(base.shape[1]):
        value = jnp.zeros((rows, LANES), F32)
        for q in range(GROUPS):
            total = None
            for index, offset in sources:
                i = size * q + j - SPILL - offset * planes
                if not 0 <= i <= planes:
                    continue
                low, high, last = turned[index]
                place = (lane - 7 * i) & (LANES - 1)
                term = jnp.where(place < OWN_AT, jnp.where(place < HIGH_AT, low, high), last)
                shift = (GROUP_LANES * q - 7 * i) % LANES
                term = pltpu.roll(term, shift, 1) if shift else term
                total = term if total is None else total + term
            if total is None:
                continue
            place = lane - GROUP_LANES * q
            inside = (place >= 0) & (place < OWN_AT + spread)
            inside = inside & ((place < spread) | (place >= HIGH_AT))
            value = jnp.where(inside, total, value)
        base[0, j] = value
    seventh = 1.0 / 7.0
    high = base.shape[1]
    sweep(first, base, 1, high - 1, base, seventh)
    sweep(second, first, 2, high - 2, base, seventh)
    sweep(first, second, 3, high - 3, base, seventh)
    sweep(second, first, 4, high - 4, base, seventh)
    kept = out.shape[1]
    for i in range(size):
        p = SPILL + i
        value = (seven_sum(second, p, p - 1, p + 1)[0] * seventh + base[0, p]) * weight(0)
        out[i] = value[ROW0 : ROW0 + kept]


def edge_sides(part, q):
    lane = iota(part.shape, 1)
    low = pltpu.roll(part, (-GROUP_LANES * q - LOW_END) % LANES, 1)
    high = pltpu.roll(part, (LANES - SPILL - GROUP_LANES * q - LOW_END - 6) % LANES, 1)
    return jnp.where(lane <= SPILL, low, jnp.where(lane >= LANES - SPILL, high, 0.0))


def turned_to_last(value, lane):
    return pltpu.roll(value, (LANES - 1 - lane) % LANES, 1)


def fine_sum_kernel(f0, below_x, above_x, work, out, beyond):
    planes, rows = beyond.shape[0], beyond.shape[1]
    lane = iota((rows, LANES), 1)
    lane1 = iota((1, LANES), 1)
    for i in range(planes + 1):
        value = f0[fine_place(i + SPILL, planes + 11)]
        if i <= SPILL:
            value = value + below_x[1 + i]
        if i >= planes - SPILL:
            value = value + above_x[i - (planes - SPILL)]
        q, m = i // work.shape[0], i % work.shape[0]
        part = work[m, 0:rows]
        out[i, 0:rows] = value + edge_sides(part, q)
        if i < planes:
            first = GROUP_LANES * q
            last = turned_to_last(part, first + HIGH_AT)
            beyond[i] = last + turned_to_last(part, first + OWN_AT + SPILL)
            row = f0[6, i + SPILL : i + SPILL + 1]
            if i <= SPILL:
                row = row + below_x[0, i + SPILL + planes : i + SPILL + planes + 1]
            if i >= planes - SPILL:
                row = row + above_x[6, i + SPILL - planes : i + SPILL - planes + 1]
            row = row + edge_sides(work[m, rows : rows + 1], q)
            out[i, rows : rows + 1] = row


def fine_y_kernel(main, above, below, out, work):
    share = main.shape[0]
    rows = out.shape[1]
    out[6] = jnp.zeros((rows, LANES), F32)
    for p in range(share):
        work[p] = main[p]
        work[p, 33:41] = work[p, 33:41] + above[p]
        work[p, 8:16] = work[p, 8:16] + below[p]
        out[fine_place(p, share)] = work[p, ROW0 : ROW0 + rows]
        out[6, p : p + 1] = work[p, ROW0 + rows : ROW0 + rows + 1]


def body(field):
    nx, ny, nz = field.shape[1:]
    size_x, size_y, size_z = lax.axis_size("gx"), lax.axis_size("gy"), lax.axis_size("gz")
    n1 = nx // 2
    share1 = n1 + 4
    rows0 = ny + 16
    rows1 = ny // 2 + 8
    planes0 = nx + 13

    def from_offset(value, axis, offset):
        count = lax.axis_size(axis)
        pairs = [(source, (source - offset) % count) for source in range(count)]
        return lax.ppermute(value, axis, pairs)

    level0 = (2, planes0, rows0, LANES)
    level1 = (1, n1 + 12, ny // 2 + 16, LANES)
    packed = -(-(n1 // 2 + 6) // 3) * 16
    inner0 = rows0 - ROW0
    sent1 = ROWS_SENT * (share1 // 2 + 1)
    message, g2, g1, *powers = call(
        spread_kernel,
        [shape(sent1 + 2 * inner0, LANES), shape(packed, LANES),
         shape(share1, rows1, LANES)] + [shape(*level0)] * 4,
        [level1, level1],
        2.9,
        field,
    )
    shares = [g2] + [from_offset(g2, "gz", o) for o in range(1, size_z)]
    messages = {0: message}
    sources = []
    for o in (0, 1, -1, 2, -2):
        key = [k for k in messages if k % size_x == o % size_x]
        if not key:
            messages[o] = from_offset(message, "gx", o)
            key = [o]
        sources.append((list(messages).index(key[0]), o))
    messages = list(messages.values())
    strips = min(3, size_x)
    planes1 = n1 + 14
    sent_y = 9 * planes1 + 12 * strips
    rows_g1, up, down = call(
        functools.partial(rows_kernel, tuple(sources), strips),
        [shape(planes1, ROWS_SENT, LANES), shape(sent_y, LANES), shape(sent_y, LANES)],
        [],
        0.2,
        g1, *messages,
    )
    window = (1, planes1, ny // 2 + 16, LANES)
    sent_z = window[2] * -(-planes1 // 14) + rows0 * strips
    window_g1, up, down = call(
        functools.partial(columns_kernel, strips),
        [shape(*window[1:]), shape(sent_z, LANES), shape(sent_z, LANES)],
        [],
        0.3,
        rows_g1, *messages[:strips], from_offset(down, "gy", 1), from_offset(up, "gy", -1),
    )
    above = from_offset(down, "gz", 1)
    below = from_offset(up, "gz", -1)
    f1 = call(
        window_kernel,
        shape(share1, *window[2:]),
        [window, window, window],
        0.9,
        window_g1, above, below,
    )
    share0 = nx + 11
    main, f_down, f_up, kept = call(
        fine_own_kernel,
        [shape(share0, rows0, LANES), shape(share0, 8, LANES), shape(share0, 8, LANES),
         shape(*field.shape)],
        [level0],
        3.0,
        *powers, field,
        after=(messages[1],),
    )
    f_above = from_offset(f_down, "gy", 1)
    f_below = from_offset(f_up, "gy", -1)

    tiles = size_z * 32 // LANES
    g2 = call(
        functools.partial(gather_z_kernel, size_z),
        shape(tiles, n1 // 2 + 6, 16, LANES),
        [],
        0.15,
        *shares,
        after=(rows_g1, main,),
    )
    shares = [g2] + [from_offset(g2, "gx", o) for o in range(1, size_x)]
    g2 = call(
        functools.partial(fold_x_kernel, size_x),
        shape(tiles, 4 * size_x, 16, LANES),
        [],
        0.05,
        *shares,
        after=(window_g1,),
    )
    shares = [g2] + [from_offset(g2, "gy", o) for o in range(1, size_y)]

    f0 = call(
        fine_y_kernel,
        shape(share0 + 1, ny, LANES),
        [(share0, rows0, LANES)],
        0.4,
        main, f_above, f_below,
        after=(g2,),
    )
    if size_x == 2:
        other = from_offset(f0[0:13], "gx", 1)
        f_above, f_below = other[0:7], other[6:13]
    else:
        f_above = from_offset(f0[0:7], "gx", 1)
        f_below = from_offset(f0[6:13], "gx", -1)
    group = -(-(nx + 1) // GROUPS)
    edges = (1, group + 2 * SPILL, rows0, LANES)
    edge = call(
        functools.partial(fine_edge_kernel, tuple(sources[:3]), nx),
        shape(group, ny + 8, LANES),
        [edges, edges, edges],
        1.9,
        above, below, up,
    )
    f0, beyond = call(
        fine_sum_kernel,
        [shape(nx + 1, ny + 8, LANES), shape(nx, ny, LANES)],
        [],
        0.3,
        f0, f_below, f_above, edge,
    )

    scratch = []
    for level in (2, 3):
        cut = 2 ** (level - 2)
        extent = (max(1, tiles // cut), 4 * size_x // cut, 8 * size_y // cut, LANES)
        scratch.extend([extent] * 3)
    e2 = call(
        functools.partial(coarse_kernel, size_y),
        shape(n1 // 2 + 6, 16, LANES),
        scratch,
        2.2,
        *shares, *last_level_matrices(size_x, 2 * size_y, 8 * size_z),
        after=(f1,),
    )
    fine = (2, nx + 8, ny + 8, LANES)
    correction = call(
        correct_kernel,
        shape(*fine),
        [level1, level1, fine],
        2.2,
        e2, f1,
    )
    return call(
        finish_kernel,
        shape(*field.shape),
        [(nx + 1, ny + 8, LANES)],
        0.9,
        kept, correction, f0, beyond,
    )


def solution(mesh):
    in_specs = (P(None, "gx", "gy", "gz"),)
    out_specs = P(None, "gx", "gy", "gz")
    return jax.shard_map(body, mesh=mesh, in_specs=in_specs, out_specs=out_specs, check_vma=False)
```

```python
import functools

import jax
import jax.numpy as jnp
import numpy as np
from jax import lax
from jax.experimental import pallas as pl
from jax.experimental.pallas import tpu as pltpu
from jax.sharding import PartitionSpec as P

LEVELS = 5
SWEEPS = 3
COARSE_ITERS = 24


F32 = jnp.float32
LANES = 128
VMEM_LIMIT = 16 * 1024 * 1024
PEAK_FLOPS_PER_US = 1150000000.0


def weight(level):
    return 4.0**level / 7.0


def shape(*extent):
    return jax.ShapeDtypeStruct(extent, F32)


def call(kernel, outs, scratch, microseconds, *args, after=()):
    flops = int(microseconds * PEAK_FLOPS_PER_US)
    if after:
        inner, first, last = kernel, len(args), len(args) + len(after)

        def kernel(*refs):
            inner(*refs[:first], *refs[last:])

        args = (*args, *after)
    return pl.pallas_call(
        kernel,
        out_shape=outs,
        scratch_shapes=[pltpu.VMEM(s, F32) for s in scratch],
        compiler_params=pltpu.CompilerParams(vmem_limit_bytes=VMEM_LIMIT),
        cost_estimate=pl.CostEstimate(flops=flops, bytes_accessed=0, transcendentals=0),
    )(*args)


def iota(extent, dim):
    return lax.broadcasted_iota(jnp.int32, extent, dim)


def one_hot(condition):
    rows = iota((LANES, LANES), 0)
    columns = iota((LANES, LANES), 1)
    return jnp.where(condition(rows, columns), 1.0, 0.0).astype(jnp.bfloat16)


def dot(left, right):
    return lax.dot_general(
        left,
        right,
        (((1,), (0,)), ((), ())),
        precision=lax.Precision.HIGHEST,
        preferred_element_type=F32,
    )


def dot_ones(left, right):
    large = left.astype(jnp.bfloat16)
    rest = left - large.astype(F32)
    middle = rest.astype(jnp.bfloat16)
    small = (rest - middle.astype(F32)).astype(jnp.bfloat16)
    return lax.dot_general(
        jnp.concatenate([large, middle, small], axis=1),
        jnp.concatenate([right, right, right], axis=0),
        (((1,), (0,)), ((), ())),
        preferred_element_type=F32,
    )


def seven_sum(source, plane, below, above, wanted=None):
    tiles = source.shape[0]
    rows = source.shape[2]
    center = [source[t, plane] for t in range(tiles)]
    left = [pltpu.roll(v, 1, 1) for v in center]
    right = [pltpu.roll(v, LANES - 1, 1) for v in center]
    if tiles > 1:
        lane = iota((rows, LANES), 1)
        left = [jnp.where(lane == 0, left[t - 1], left[t]) for t in range(tiles)]
        right = [
            jnp.where(lane == LANES - 1, right[(t + 1) % tiles], right[t]) for t in range(tiles)
        ]
    out = []
    for t in range(tiles if wanted is None else wanted):
        v = center[t]
        total = v + (source[t, below] + source[t, above])
        total = total + (pltpu.roll(v, 1, 0) + pltpu.roll(v, rows - 1, 0))
        out.append(total + (left[t] + right[t]))
    return out


def sweep(*args, **options):
    for _ in sweep_steps(*args, **options):
        pass


def together(*runs):
    waiting = list(runs)
    while waiting:
        for run in list(waiting):
            if next(run, "end") == "end":
                waiting.remove(run)


def sweep_steps(target, source, low, high, base=None, scale=None, period=None, span=None):
    for plane in range(low, high):
        below, above = plane - 1, plane + 1
        if period is not None:
            below, above = below % period, above % period
        for t, value in enumerate(seven_sum(source, plane, below, above)):
            if scale is not None:
                value = value * scale
            if base is not None and (span is None or span[0] <= plane < span[1]):
                value = value + base[t, plane]
            target[t, plane] = value
        yield


PLANE0 = 6
ROW0 = 8
SPILL = 5


def fill_source(field, target):
    planes, rows = field.shape[1], field.shape[2]
    lane = iota((rows, LANES), 1)
    row = iota((rows, LANES), 0)
    row8 = iota((8, LANES), 0)
    zero8 = jnp.zeros((8, LANES), F32)
    zeros = jnp.zeros((rows, LANES), F32)

    def one_plane(i, before):
        along_x, along_y, along_z = field[0, i], field[1, i], field[2, i]
        value = before - along_x - along_y - along_z
        value = value + jnp.where(row == 0, 0.0, pltpu.roll(along_y, 1, 0))
        turned = pltpu.roll(along_z, 1, 1)
        value = value + jnp.where(lane == 0, 0.0, turned)
        p = PLANE0 + i
        target[0, p, 0:ROW0] = zero8
        target[0, p, ROW0 : ROW0 + rows] = value
        last = pltpu.roll(along_y[rows - 8 : rows], 1, 0)
        target[0, p, ROW0 + rows : ROW0 + rows + 8] = jnp.where(row8 == 0, last, 0.0)
        target[1, p, 0:ROW0] = zero8
        target[1, p, ROW0 : ROW0 + rows] = jnp.where(lane == 0, turned, 0.0)
        target[1, p, ROW0 + rows : ROW0 + rows + 8] = zero8

    for i in range(planes):
        one_plane(i, field[0, i - 1] if i else zeros)
    p = PLANE0 + planes
    target[0, p] = jnp.zeros(target.shape[2:], F32)
    target[1, p] = jnp.zeros(target.shape[2:], F32)
    target[0, p, ROW0 : ROW0 + rows] = field[0, planes - 1]


def clear_planes(target, planes):
    for t in range(target.shape[0]):
        for p in planes:
            target[t, p] = jnp.zeros(target.shape[2:], F32)


def pack_lanes(read, count, first, width, spacing, rows):
    lane = iota((rows, LANES), 1)
    per_tile = LANES // spacing
    tiles = []
    for start in range(0, count, per_tile):
        packed = jnp.zeros((rows, LANES), F32)
        for k in range(min(per_tile, count - start)):
            turned = pltpu.roll(read(start + k), (spacing * k - first) % LANES, 1)
            inside = (lane >= spacing * k) & (lane < spacing * k + width)
            packed = jnp.where(inside, turned, packed)
        tiles.append(packed)
    return tiles


def unpacked(packed, k, spacing, offset, width, first, rows):
    lane = iota((rows, LANES), 1)
    turned = pltpu.roll(packed, (first - spacing * k - offset) % LANES, 1)
    inside = (lane >= first) & (lane < first + width)
    return jnp.where(inside, turned, 0.0)


def clear_margin(target, low, high):
    clear_planes(target, (low - 2, low - 1, high, high + 1))


def spread_kernel(field, message, g2_out, g1_out, zeroth, first, second, third, g1_a, g1_b):
    planes = field.shape[1]
    fill_source(field, zeroth)
    low, high = PLANE0, PLANE0 + planes + 1
    clear_margin(zeroth, low, high)
    powers = (zeroth, first, second, third)
    for k in (1, 2, 3):
        sweep(powers[k], powers[k - 1], low - k, high + k)
        clear_margin(powers[k], low - k, high + k)

    n1 = planes // 2
    rows1 = first.shape[2] // 2
    pieces = []
    for t in range(2):
        parts = []
        for c in range(-2, n1 + 2):
            p = PLANE0 + 2 * c
            total = third[t, p, pl.ds(0, rows1, stride=2), :]
            total = total + third[t, p, pl.ds(1, rows1, stride=2), :]
            total = total + third[t, p + 1, pl.ds(0, rows1, stride=2), :]
            total = total + third[t, p + 1, pl.ds(1, rows1, stride=2), :]
            parts.append(total)
        pieces.append(jnp.concatenate(parts, axis=0))
    main = one_hot(lambda r, c: c == 32 + r // 2)
    side = one_hot(lambda r, c: c == jnp.where(r < 64, 96 + r // 2, r // 2 - 32))
    g1 = (dot_ones(pieces[0], main) + dot_ones(pieces[1], side)) * (0.125 / 343.0)
    share = n1 + 4
    g1 = g1.reshape(share, rows1, LANES)
    g1_out[...] = g1

    clear_planes(g1_a, range(g1_a.shape[1]))
    clear_planes(g1_b, range(g1_b.shape[1]))
    for c in range(share):
        g1_a[0, 4 + c, 4 : 4 + rows1] = g1[c]
    sweep(g1_b, g1_a, 3, 5 + share)
    sweep(g1_a, g1_b, 2, 6 + share)
    sweep(g1_b, g1_a, 1, 7 + share)
    rows2 = g1_a.shape[2] // 2
    parts = []
    for c in range(g1_a.shape[1] // 2):
        total = g1_b[0, 2 * c, pl.ds(0, rows2, stride=2), :]
        total = total + g1_b[0, 2 * c, pl.ds(1, rows2, stride=2), :]
        total = total + g1_b[0, 2 * c + 1, pl.ds(0, rows2, stride=2), :]
        total = total + g1_b[0, 2 * c + 1, pl.ds(1, rows2, stride=2), :]
        parts.append(total)
    groups = -(-len(parts) // 3)
    parts.extend([jnp.zeros((rows2, LANES), F32)] * (3 * groups - len(parts)))
    g2 = None
    for slot in range(3):
        matrix = one_hot(
            lambda r, c: (c == r // 2 - 13 + 42 * slot) & (r // 2 >= 13) & (r // 2 < 51)
        )
        term = dot_ones(jnp.concatenate(parts[slot::3], axis=0), matrix)
        g2 = term if g2 is None else g2 + term
    g2_out[...] = g2 * (0.125 / 343.0)
    lane = iota((ROWS_SENT, LANES), 1)
    sides = jnp.zeros((ROWS_SENT, LANES), F32)
    for q in range(share // 2):
        even, odd = g1_out[2 * q, 2 : 2 + ROWS_SENT], g1_out[2 * q + 1, 2 : 2 + ROWS_SENT]
        value = jnp.where(lane < 64, pltpu.roll(even, LANES - 32, 1), pltpu.roll(odd, 32, 1))
        message[ROWS_SENT * q : ROWS_SENT * (q + 1)] = value
        for c, value in ((2 * q, even), (2 * q + 1, odd)):
            low = pltpu.roll(value, (8 * c - 28) % LANES, 1)
            high = pltpu.roll(value, (8 * c + 4 - 96) % LANES, 1)
            sides = jnp.where((lane >= 8 * c) & (lane < 8 * c + 4), low, sides)
            sides = jnp.where((lane >= 8 * c + 4) & (lane < 8 * c + 8), high, sides)
    size = ROWS_SENT * (share // 2)
    message[size : size + ROWS_SENT] = sides
    size = size + ROWS_SENT
    rows0 = zeroth.shape[2] - ROW0
    lane = iota((rows0, LANES), 1)

    def last_columns(i):
        p = PLANE0 + i
        return jnp.where(lane == 0, zeroth[1, p, ROW0:], zeroth[0, p, ROW0:])

    def first_columns(i):
        return zeroth[0, PLANE0 + i, ROW0:]

    last = pack_lanes(last_columns, planes + 1, LANES - SPILL, SPILL + 1, 7, rows0)[0]
    message[size : size + rows0] = last
    first = pack_lanes(first_columns, planes + 1, 0, SPILL + 1, 7, rows0)[0]
    message[size + rows0 :] = first


def gather_z_kernel(count, *refs):
    shares, out = refs[:count], refs[count]
    size = shares[0].shape[0]
    period = 32 * count
    rows2 = 16
    tiles, planes = out.shape[0], out.shape[1]
    lane = iota((size, LANES), 1)
    for slot in range(3):
        totals = [jnp.zeros((size, LANES), F32) for _ in range(tiles)]
        for o in range(count):
            shift = (32 * o + 13 - 42 * slot) % LANES
            turned = pltpu.roll(shares[o][...], shift, 1) if shift else shares[o][...]
            position = ((lane - shift) & (LANES - 1)) - 42 * slot
            inside = (position >= 0) & (position < 38)
            for t in range(tiles):
                lands = lax.rem(position + (32 * o + 13 + period), period) == lane + LANES * t
                totals[t] = totals[t] + jnp.where(inside & lands, turned, 0.0)
        for t in range(tiles):
            for c in range(slot, planes, 3):
                out[t, c] = totals[t][rows2 * (c // 3) : rows2 * (c // 3 + 1)]


ROWS_SENT = 20


def plane_sent(message, share, c):
    lane = iota((ROWS_SENT, LANES), 1)
    pair = message[ROWS_SENT * (c // 2) : ROWS_SENT * (c // 2 + 1)]
    inside = (lane >= 32) & (lane < 96)
    value = jnp.where(inside, pltpu.roll(pair, LANES - 32 if c % 2 else 32, 1), 0.0)
    start = ROWS_SENT * (share // 2)
    sides = message[start : start + ROWS_SENT]
    low = pltpu.roll(sides, (28 - 8 * c) % LANES, 1)
    high = pltpu.roll(sides, (92 - 8 * c) % LANES, 1)
    value = jnp.where((lane >= 28) & (lane < 32), low, value)
    return jnp.where((lane >= 96) & (lane < 100), high, value)


def rows_kernel(sources, strips, *refs):
    inputs, (out, up, down) = refs[:-3], refs[-3:]
    own, messages = inputs[0], inputs[1:]
    planes, share = out.shape[0], own.shape[0]
    read = {}
    for p in range(planes):
        total = None
        for index, offset in sources:
            c = p - 7 - 8 * offset + 2
            if not 0 <= c < share:
                continue
            if (index, c) not in read:
                if index == 0:
                    read[index, c] = own[c, 2 : 2 + ROWS_SENT]
                else:
                    read[index, c] = plane_sent(messages[index], share, c)
            value = read[index, c]
            total = value if total is None else total + value
        out[p] = total
        down[9 * p : 9 * p + 9] = total[0:9]
        up[9 * p : 9 * p + 9] = total[11:20]
    start = ROWS_SENT * (share // 2 + 1)
    inner = (messages[0].shape[0] - start) // 2
    place = 9 * planes
    for k in range(strips):
        for part in range(2):
            begin = start + inner * part
            down[place : place + 6] = messages[k][begin : begin + 6]
            last = begin + inner - 8 - SPILL
            up[place : place + 6] = messages[k][last : last + 6]
            place += 6


def columns_kernel(strips, g1, *refs):
    messages, (above, below), (out, up, down) = refs[:-5], refs[-5:-3], refs[-3:]
    planes, rows = out.shape[0], out.shape[1]
    for p in range(planes):
        out[p] = jnp.zeros((rows, LANES), F32)
        out[p, 6 : 6 + ROWS_SENT] = g1[p]
        out[p, 22:31] = out[p, 22:31] + above[9 * p : 9 * p + 9]
        out[p, 1:10] = out[p, 1:10] + below[9 * p : 9 * p + 9]
    share = planes - 10
    start = ROWS_SENT * (share // 2 + 1)
    inner = (messages[0].shape[0] - start) // 2
    for target, first, part in ((up, 89, 0), (down, 30, 1)):
        place = 0
        for packed in pack_lanes(lambda p: out[p], planes, first, 9, 9, rows):
            target[place : place + rows] = packed
            place += rows
        for k in range(strips):
            begin = start + inner * part
            six = 9 * planes + 6 * (2 * k + part)
            target[place : place + ROW0] = jnp.zeros((ROW0, LANES), F32)
            target[place + ROW0 : place + ROW0 + inner] = messages[k][begin : begin + inner]
            at = place + ROW0 - SPILL
            target[at : at + 6] = target[at : at + 6] + below[six : six + 6]
            at = place + ROW0 + inner - 8
            target[at : at + 6] = target[at : at + 6] + above[six : six + 6]
            place += ROW0 + inner


def fold_x_kernel(count, *refs):
    shares, out = refs[:count], refs[count]
    tiles, period = out.shape[0], out.shape[1]
    for t in range(tiles):
        for x in range(period):
            total = None
            for o in range(count):
                for c in range(10):
                    if (c - 3 + 4 * o) % period == x:
                        value = shares[o][t, c]
                        total = value if total is None else total + value
            out[t, x] = total


def fine_sweeps(base, first, second):
    seventh = 1.0 / 7.0
    planes = base.shape[1]
    yield from sweep_steps(first, base, 1, planes - 1, base, seventh)
    yield from sweep_steps(second, first, 2, planes - 2, base, seventh)
    yield from sweep_steps(first, second, 3, planes - 3, base, seventh)
    yield from sweep_steps(second, first, 4, planes - 4, base, seventh)


def window_kernel(g1, out, base, first, second):
    for p in range(base.shape[1]):
        base[0, p] = g1[p]
    together(fine_sweeps(base, first, second))
    for c in range(out.shape[0]):
        p = 5 + c
        out[c] = (seven_sum(second, p, p - 1, p + 1)[0] * (1.0 / 7.0) + base[0, p]) * weight(1)


WINDOW_LANES = 28


def window_edge_steps(f1, above, below, out, base, first, second):
    rows = base.shape[2]
    share = out.shape[0]
    size = share // 4
    planes = share + 10
    lane = iota((rows, LANES), 1)
    turned = []
    for begin in range(0, rows * -(-planes // 14), rows):
        turned.append((below[begin : begin + rows],
                       pltpu.roll(above[begin : begin + rows], 19, 1)))
    for j in range(base.shape[1]):
        value = jnp.zeros((rows, LANES), F32)
        for q in range(4):
            p = size * q + j
            lower, upper = turned[p // 14]
            shift = 9 * (p % 14)
            term = jnp.where(((lane - shift) & (LANES - 1)) < 14, lower, upper)
            shift = (WINDOW_LANES * q - shift) % LANES
            term = pltpu.roll(term, shift, 1) if shift else term
            place = lane - WINDOW_LANES * q
            inside = (place >= 0) & (place < WINDOW_LANES) & ((place < 9) | (place >= 19))
            value = jnp.where(inside, term, value)
        base[0, j] = value
        yield
    yield from fine_sweeps(base, first, second)
    for m in range(size):
        p = 5 + m
        value = seven_sum(second, p, p - 1, p + 1)[0] * (1.0 / 7.0) + base[0, p]
        value = value * weight(1)
        for q in range(4):
            c = size * q + m
            low = pltpu.roll(value, (25 - WINDOW_LANES * q) % LANES, 1)
            high = pltpu.roll(value, (75 - WINDOW_LANES * q) % LANES, 1)
            part = jnp.where((lane >= 89) & (lane < 98), high, 0.0)
            out[c] = f1[c] + jnp.where((lane >= 30) & (lane < 39), low, part)
        yield


def restrict_lanes(values, width, coarse_width, coarse_tiles):
    out = []
    for s in range(coarse_tiles):
        total = None
        for t, value in enumerate(values):
            matrix = one_hot(
                lambda r, c: ((LANES * t + r) // 2 == lax.rem(LANES * s + c, coarse_width))
                & (LANES * t + r < width)
            )
            term = dot_ones(value, matrix)
            total = term if total is None else total + term
        out.append(total)
    return out


def prolong_lanes(values, width, fine_tiles):
    out = []
    for s in range(fine_tiles):
        total = None
        for t, value in enumerate(values):
            matrix = one_hot(lambda r, c: LANES * t + r == lax.rem(LANES * s + c, width) // 2)
            term = dot_ones(value, matrix)
            total = term if total is None else total + term
        out.append(total)
    return out


def swept(values):
    rows = values[0].shape[0]
    out = []
    for p, v in enumerate(values):
        total = v + (values[p - 1] + values[(p + 1) % len(values)])
        total = total + (pltpu.roll(v, 1, 0) + pltpu.roll(v, rows - 1, 0))
        out.append((total + (pltpu.roll(v, 1, 1) + pltpu.roll(v, LANES - 1, 1))) * (1.0 / 7.0))
    return out


def real_waves(count):
    cells = np.arange(count)
    rows, eigenvalues = [], []
    for k in range(count // 2 + 1):
        angle = 2.0 * np.pi * k / count
        rows.append(np.cos(angle * cells))
        eigenvalues.append(2.0 * np.cos(angle))
        if 0 < k < count / 2:
            rows.append(np.sin(angle * cells))
            eigenvalues.append(2.0 * np.cos(angle))
    basis = np.stack(rows)
    basis = basis / np.sqrt(np.sum(basis * basis, axis=1, keepdims=True))
    return basis, np.array(eigenvalues)


def last_level_matrices(planes, rows, width):
    wave_x, value_x = real_waves(planes)
    wave_y, value_y = real_waves(rows)
    wave_z, value_z = real_waves(width)
    into = np.kron(np.repeat(wave_x, 2, axis=1), np.repeat(wave_y, 2, axis=1))
    level_values = value_x[:, None, None] + value_y[None, :, None] + value_z[None, None, :]
    factor = (1.0 + level_values) / 7.0
    total = sum(factor**k for k in range(COARSE_ITERS)) * weight(LEVELS - 1) * 0.125
    scale = np.zeros((planes * rows, LANES))
    scale[:, :width] = total.reshape(planes * rows, width)
    fine = 2 * width
    tiles = max(1, fine // LANES)
    lanes = np.arange(LANES * tiles)
    to_waves = np.zeros((LANES * tiles, LANES))
    to_waves[:fine, :width] = wave_z.T[lanes[:fine] // 2]
    from_waves = np.zeros((LANES, LANES * tiles))
    from_waves[:width] = wave_z[:, (lanes % fine) // 2]
    to_waves = to_waves.reshape(tiles, LANES, LANES)
    from_waves = from_waves.reshape(LANES, tiles, LANES).transpose(1, 0, 2)
    arrays = (into, into.T, to_waves, from_waves, scale)
    return [jnp.asarray(np.ascontiguousarray(a), F32) for a in arrays]


def solve_last(values, into, back, to_waves, from_waves, scale):
    values = dot(into[...], values)
    yield
    values = dot(values, to_waves[0]) * scale[...]
    yield
    values = dot(back[...], values)
    yield
    return dot(values, from_waves[0])


def solve(level, width, buffers, spectral):
    g, a, b = buffers[level]
    tiles, planes, rows = g.shape[0], g.shape[1], g.shape[2]
    seventh = 1.0 / 7.0
    w = weight(level)
    if level == LEVELS - 2:
        source = [g[0, p] for p in range(planes)]
        first = swept(source)
        yield
        second = swept(first)
        yield
        third = swept(second)
        yield
        before = [(x + y + z) * w for x, y, z in zip(source, first, second)]
        values = yield from solve_last(jnp.concatenate(third, axis=0), *spectral)
        error = [before[p] + values[rows * p : rows * (p + 1)] for p in range(planes)]
        yield
        for _ in range(SWEEPS):
            error = swept(error)
            yield
        for p in range(planes):
            g[0, p] = before[p] + error[p]
        return
    yield from sweep_steps(a, g, 0, planes, None, seventh, planes)
    yield from sweep_steps(b, a, 0, planes, None, seventh, planes)
    for t in range(tiles):
        for p in range(planes):
            g[t, p] = (g[t, p] + a[t, p] + b[t, p]) * w
    yield from sweep_steps(a, b, 0, planes, None, seventh, planes)
    half = rows // 2
    values = []
    for t in range(tiles):
        parts = []
        for c in range(planes // 2):
            total = a[t, 2 * c, pl.ds(0, half, stride=2), :]
            total = total + a[t, 2 * c, pl.ds(1, half, stride=2), :]
            total = total + a[t, 2 * c + 1, pl.ds(0, half, stride=2), :]
            total = total + a[t, 2 * c + 1, pl.ds(1, half, stride=2), :]
            parts.append(total)
        values.append(jnp.concatenate(parts, axis=0))
    coarse = buffers[level + 1][0]
    values = restrict_lanes(values, width, width // 2, coarse.shape[0])
    for t, value in enumerate(values):
        for c in range(planes // 2):
            coarse[t, c] = value[half * c : half * (c + 1)] * 0.125
    yield from solve(level + 1, width // 2, buffers, spectral)
    values = [
        jnp.concatenate([coarse[t, c] for c in range(planes // 2)], axis=0)
        for t in range(coarse.shape[0])
    ]
    values = prolong_lanes(values, width, tiles)
    for t, value in enumerate(values):
        for c in range(planes // 2):
            part = value[half * c : half * (c + 1)]
            for p in (2 * c, 2 * c + 1):
                b[t, p, pl.ds(0, half, stride=2), :] = part
                b[t, p, pl.ds(1, half, stride=2), :] = part
        for p in range(planes):
            b[t, p] = b[t, p] + g[t, p]
    yield from sweep_steps(a, b, 0, planes, None, seventh, planes)
    yield from sweep_steps(b, a, 0, planes, None, seventh, planes)
    yield from sweep_steps(a, b, 0, planes, None, seventh, planes)
    for t in range(tiles):
        for p in range(planes):
            g[t, p] = g[t, p] + a[t, p]


def coarse_steps(count, *refs):
    shares, spectral = refs[:count], refs[count : count + 5]
    out, scratch = refs[count + 5], refs[count + 6 :]
    buffers = {level: scratch[3 * (level - 2) : 3 * (level - 1)] for level in (2, 3)}
    g = buffers[2][0]
    tiles, planes = g.shape[0], g.shape[1]
    for t in range(tiles):
        for p in range(planes):
            for b in range(count):
                value = shares[b][t, p, 0:8] + shares[(b - 1) % count][t, p, 8:16]
                g[t, p, 8 * b : 8 * b + 8] = value
    yield from solve(2, LANES * tiles, buffers, spectral)
    for c in range(out.shape[0]):
        out[c] = g[0, (c - 3) % planes, 0:16]


def arrived_kernel(above, below, out):
    out[...] = jnp.zeros(out.shape, F32)


def late_kernel(count, sources, planes, *refs):
    shares, rest = refs[: count + 5], refs[count + 5 :]
    f1, above, below, own, e2_out, f1_out, edge_out = rest[:7]
    scratch = rest[7:]
    together(
        coarse_steps(count, *shares, e2_out, *scratch[:6]),
        window_edge_steps(f1, above, below, f1_out, *scratch[6:9]),
        fine_edge_steps(sources, planes, above, below, own, edge_out, *scratch[9:12]),
    )


def correct_kernel(e2, f1, u0_b, u1_a, u1_b, u0_a):
    share1 = f1.shape[0]
    share2 = e2.shape[0]
    rows2 = e2.shape[1]
    value = e2[...].reshape(share2 * rows2, LANES)
    value = dot_ones(value, one_hot(lambda r, c: r == c // 2))
    for c in range(share2):
        part = value[rows2 * c : rows2 * (c + 1)]
        for p in (2 * c, 2 * c + 1):
            u1_a[0, p, pl.ds(0, rows2, stride=2), :] = part
            u1_a[0, p, pl.ds(1, rows2, stride=2), :] = part
    count1 = 2 * share2
    sweep(u1_b, u1_a, 1, count1 - 1)
    sweep(u1_a, u1_b, 2, count1 - 2)
    sweep(u1_b, u1_a, 3, count1 - 3)
    rows1, sent = 24, 20
    parts = []
    for c in range(share1):
        parts.append(f1[c, 6 : 6 + rows1] + u1_b[0, 4 + c, 6 : 6 + rows1] * (1.0 / 343.0))
    value = jnp.concatenate(parts, axis=0)
    main = dot_ones(value, one_hot(lambda r, c: r == 32 + c // 2))
    side = dot_ones(value, one_hot(lambda r, c: r == jnp.where(c < 64, 96 + c // 2, c // 2 - 32)))
    for t, value in enumerate((main, side)):
        for c in range(share1):
            part = value[rows1 * c : rows1 * c + sent]
            for p in (2 * c, 2 * c + 1):
                u0_a[t, p, pl.ds(0, sent, stride=2), :] = part
                u0_a[t, p, pl.ds(1, sent, stride=2), :] = part
    count0 = 2 * share1
    sweep(u0_b, u0_a, 1, count0 - 1)
    sweep(u0_a, u0_b, 2, count0 - 2)
    sweep(u0_b, u0_a, 3, count0 - 3)


def finish_kernel(field, u0_b, f0, beyond, out, pot):
    planes, rows = field.shape[1], field.shape[2]
    scale = 1.0 / 343.0
    for i in range(planes + 1):
        pot[i, 0:rows] = u0_b[0, 4 + i, 4 : 4 + rows] * scale + f0[i, 0:rows]
        if i < planes:
            edge = u0_b[0, 4 + i, 4 + rows : 5 + rows] * scale
            pot[i, rows : rows + 1] = edge + f0[i, rows : rows + 1]
    lane = iota((rows, LANES), 1)
    for i in range(planes):
        here = pot[i, 0:rows]
        out[0, i] = field[0, i] - (pot[i + 1, 0:rows] - here)
        out[1, i] = field[1, i] - (pot[i, 1 : rows + 1] - here)
        last = pltpu.roll(u0_b[1, 4 + i, 4 : 4 + rows], LANES - 1, 1) * scale + beyond[i]
        next_z = jnp.where(lane == LANES - 1, last, pltpu.roll(here, LANES - 1, 1))
        out[2, i] = field[2, i] - (next_z - here)


def fine_place(p, share):
    if p <= SPILL:
        return p
    return p - share + 13 if p >= share - 6 else p + 7


def fine_own_kernel(zeroth, first, second, third, field, main, down, up, field_out, fourth):
    share = main.shape[0]
    field_out[...] = field[...]
    low, high = PLANE0, zeroth.shape[1] - 6
    sweep(fourth, third, low - 4, high + 4)
    clear_margin(fourth, low - 4, high + 4)
    powers = (zeroth, first, second, third, fourth)
    for k in range(share):
        p = low - SPILL + k
        total = seven_sum(fourth, p, p - 1, p + 1, 1)[0] * (weight(0) / 7.0**5)
        for n, power in enumerate(powers):
            if low - n <= p < high + n:
                total = total + power[0, p] * (weight(0) / 7.0**n)
        main[k] = total
        down[k] = total[1:9]
        up[k] = total[40:48]


GROUPS = 3
GROUP_LANES = 42
LOW_END, HIGH_AT, OWN_AT = 5, 16, 22


def fine_edge_steps(sources, planes, above, below, own, out, base, first, second):
    rows = base.shape[2]
    size = out.shape[0]
    lane = iota((rows, LANES), 1)
    strips = 1 + max(index for index, offset in sources)
    start = above.shape[0] - rows * strips
    turned = []
    for index in range(strips):
        begin = start + rows * index
        turned.append((below[begin : begin + rows],
                       pltpu.roll(above[begin : begin + rows], HIGH_AT, 1),
                       pltpu.roll(own[begin : begin + rows], OWN_AT, 1)))
    spread = SPILL + 1
    for j in range(base.shape[1]):
        value = jnp.zeros((rows, LANES), F32)
        for q in range(GROUPS):
            total = None
            for index, offset in sources:
                i = size * q + j - SPILL - offset * planes
                if not 0 <= i <= planes:
                    continue
                low, high, last = turned[index]
                place = (lane - 7 * i) & (LANES - 1)
                term = jnp.where(place < OWN_AT, jnp.where(place < HIGH_AT, low, high), last)
                shift = (GROUP_LANES * q - 7 * i) % LANES
                term = pltpu.roll(term, shift, 1) if shift else term
                total = term if total is None else total + term
            if total is None:
                continue
            place = lane - GROUP_LANES * q
            inside = (place >= 0) & (place < OWN_AT + spread)
            inside = inside & ((place < spread) | (place >= HIGH_AT))
            value = jnp.where(inside, total, value)
        base[0, j] = value
        yield
    seventh = 1.0 / 7.0
    yield from fine_sweeps(base, first, second)
    kept = out.shape[1]
    for i in range(size):
        p = SPILL + i
        value = (seven_sum(second, p, p - 1, p + 1)[0] * seventh + base[0, p]) * weight(0)
        out[i] = value[ROW0 : ROW0 + kept]
        yield


def edge_sides(part, q):
    lane = iota(part.shape, 1)
    low = pltpu.roll(part, (-GROUP_LANES * q - LOW_END) % LANES, 1)
    high = pltpu.roll(part, (LANES - SPILL - GROUP_LANES * q - LOW_END - 6) % LANES, 1)
    return jnp.where(lane <= SPILL, low, jnp.where(lane >= LANES - SPILL, high, 0.0))


def turned_to_last(value, lane):
    return pltpu.roll(value, (LANES - 1 - lane) % LANES, 1)


def fine_sum_kernel(f0, below_x, above_x, work, out, beyond):
    planes, rows = beyond.shape[0], beyond.shape[1]
    lane = iota((rows, LANES), 1)
    lane1 = iota((1, LANES), 1)
    for i in range(planes + 1):
        value = f0[fine_place(i + SPILL, planes + 11)]
        if i <= SPILL:
            value = value + below_x[1 + i]
        if i >= planes - SPILL:
            value = value + above_x[i - (planes - SPILL)]
        q, m = i // work.shape[0], i % work.shape[0]
        part = work[m, 0:rows]
        out[i, 0:rows] = value + edge_sides(part, q)
        if i < planes:
            first = GROUP_LANES * q
            last = turned_to_last(part, first + HIGH_AT)
            beyond[i] = last + turned_to_last(part, first + OWN_AT + SPILL)
            row = f0[6, i + SPILL : i + SPILL + 1]
            if i <= SPILL:
                row = row + below_x[0, i + SPILL + planes : i + SPILL + planes + 1]
            if i >= planes - SPILL:
                row = row + above_x[6, i + SPILL - planes : i + SPILL - planes + 1]
            row = row + edge_sides(work[m, rows : rows + 1], q)
            out[i, rows : rows + 1] = row


def fine_y_kernel(main, above, below, out, work):
    share = main.shape[0]
    rows = out.shape[1]
    out[6] = jnp.zeros((rows, LANES), F32)
    for p in range(share):
        work[p] = main[p]
        work[p, 33:41] = work[p, 33:41] + above[p]
        work[p, 8:16] = work[p, 8:16] + below[p]
        out[fine_place(p, share)] = work[p, ROW0 : ROW0 + rows]
        out[6, p : p + 1] = work[p, ROW0 + rows : ROW0 + rows + 1]


def body(field):
    nx, ny, nz = field.shape[1:]
    size_x, size_y, size_z = lax.axis_size("gx"), lax.axis_size("gy"), lax.axis_size("gz")
    n1 = nx // 2
    share1 = n1 + 4
    rows0 = ny + 16
    rows1 = ny // 2 + 8
    planes0 = nx + 13

    def from_offset(value, axis, offset):
        count = lax.axis_size(axis)
        pairs = [(source, (source - offset) % count) for source in range(count)]
        return lax.ppermute(value, axis, pairs)

    level0 = (2, planes0, rows0, LANES)
    level1 = (1, n1 + 12, ny // 2 + 16, LANES)
    packed = -(-(n1 // 2 + 6) // 3) * 16
    inner0 = rows0 - ROW0
    sent1 = ROWS_SENT * (share1 // 2 + 1)
    message, g2, g1, *powers = call(
        spread_kernel,
        [shape(sent1 + 2 * inner0, LANES), shape(packed, LANES),
         shape(share1, rows1, LANES)] + [shape(*level0)] * 4,
        [level1, level1],
        2.9,
        field,
    )
    shares = [g2] + [from_offset(g2, "gz", o) for o in range(1, size_z)]
    messages = {0: message}
    sources = []
    for o in (0, 1, -1, 2, -2):
        key = [k for k in messages if k % size_x == o % size_x]
        if not key:
            messages[o] = from_offset(message, "gx", o)
            key = [o]
        sources.append((list(messages).index(key[0]), o))
    messages = list(messages.values())
    strips = min(3, size_x)
    planes1 = n1 + 14
    sent_y = 9 * planes1 + 12 * strips
    rows_g1, up, down = call(
        functools.partial(rows_kernel, tuple(sources), strips),
        [shape(planes1, ROWS_SENT, LANES), shape(sent_y, LANES), shape(sent_y, LANES)],
        [],
        0.2,
        g1, *messages,
    )
    window = (1, planes1, ny // 2 + 16, LANES)
    sent_z = window[2] * -(-planes1 // 14) + rows0 * strips
    window_g1, up, down = call(
        functools.partial(columns_kernel, strips),
        [shape(*window[1:]), shape(sent_z, LANES), shape(sent_z, LANES)],
        [],
        0.3,
        rows_g1, *messages[:strips], from_offset(down, "gy", 1), from_offset(up, "gy", -1),
    )
    above = from_offset(down, "gz", 1)
    below = from_offset(up, "gz", -1)
    f1 = call(
        window_kernel,
        shape(share1, *window[2:]),
        [window, window, window],
        0.01,
        window_g1,
    )
    packed = (1, share1 // 4 + 10, *window[2:])
    share0 = nx + 11
    main, f_down, f_up, kept = call(
        fine_own_kernel,
        [shape(share0, rows0, LANES), shape(share0, 8, LANES), shape(share0, 8, LANES),
         shape(*field.shape)],
        [level0],
        3.0,
        *powers, field,
        after=(messages[1],),
    )
    f_above = from_offset(f_down, "gy", 1)
    f_below = from_offset(f_up, "gy", -1)

    tiles = size_z * 32 // LANES
    g2 = call(
        functools.partial(gather_z_kernel, size_z),
        shape(tiles, n1 // 2 + 6, 16, LANES),
        [],
        0.15,
        *shares,
        after=(rows_g1, main,),
    )
    shares = [g2] + [from_offset(g2, "gx", o) for o in range(1, size_x)]
    g2 = call(
        functools.partial(fold_x_kernel, size_x),
        shape(tiles, 4 * size_x, 16, LANES),
        [],
        0.05,
        *shares,
        after=(window_g1,),
    )
    shares = [g2] + [from_offset(g2, "gy", o) for o in range(1, size_y)]

    f0 = call(
        fine_y_kernel,
        shape(share0 + 1, ny, LANES),
        [(share0, rows0, LANES)],
        0.01,
        main, f_above, f_below,
        after=(g2,),
    )
    if size_x == 2:
        other = from_offset(f0[0:13], "gx", 1)
        f_above, f_below = other[0:7], other[6:13]
    else:
        f_above = from_offset(f0[0:7], "gx", 1)
        f_below = from_offset(f0[6:13], "gx", -1)
    group = -(-(nx + 1) // GROUPS)
    edges = (1, group + 2 * SPILL, rows0, LANES)
    scratch = []
    for level in (2, 3):
        cut = 2 ** (level - 2)
        extent = (max(1, tiles // cut), 4 * size_x // cut, 8 * size_y // cut, LANES)
        scratch.extend([extent] * 3)
    arrived = call(arrived_kernel, shape(8, LANES), [], 2.0, above, below)
    e2, f1, edge = call(
        functools.partial(late_kernel, size_y, tuple(sources[:3]), nx),
        [shape(n1 // 2 + 6, 16, LANES), shape(share1, *window[2:]), shape(group, ny + 8, LANES)],
        scratch + [packed] * 3 + [edges] * 3,
        3.0,
        *shares, *last_level_matrices(size_x, 2 * size_y, 8 * size_z), f1, above, below, up,
        after=(arrived,),
    )
    f0, beyond = call(
        fine_sum_kernel,
        [shape(nx + 1, ny + 8, LANES), shape(nx, ny, LANES)],
        [],
        0.3,
        f0, f_below, f_above, edge,
    )

    fine = (2, nx + 8, ny + 8, LANES)
    correction = call(
        correct_kernel,
        shape(*fine),
        [level1, level1, fine],
        2.2,
        e2, f1,
    )
    return call(
        finish_kernel,
        shape(*field.shape),
        [(nx + 1, ny + 8, LANES)],
        0.9,
        kept, correction, f0, beyond,
    )


def solution(mesh):
    in_specs = (P(None, "gx", "gy", "gz"),)
    out_specs = P(None, "gx", "gy", "gz")
    return jax.shard_map(body, mesh=mesh, in_specs=in_specs, out_specs=out_specs, check_vma=False)
```

```python
import functools

import jax
import jax.numpy as jnp
import numpy as np
from jax import lax
from jax.experimental import pallas as pl
from jax.experimental.pallas import tpu as pltpu
from jax.sharding import PartitionSpec as P

LEVELS = 5
SWEEPS = 3
COARSE_ITERS = 24


F32 = jnp.float32
LANES = 128
VMEM_LIMIT = 16 * 1024 * 1024
PEAK_FLOPS_PER_US = 1150000000.0


def weight(level):
    return 4.0**level / 7.0


def shape(*extent):
    return jax.ShapeDtypeStruct(extent, F32)


def call(kernel, outs, scratch, microseconds, *args, after=(), **specs):
    flops = int(microseconds * PEAK_FLOPS_PER_US)
    if after:
        inner, first, last = kernel, len(args), len(args) + len(after)

        def kernel(*refs):
            inner(*refs[:first], *refs[last:])

        args = (*args, *after)
    return pl.pallas_call(
        kernel,
        out_shape=outs,
        scratch_shapes=[pltpu.VMEM(s, F32) if isinstance(s, tuple) else s for s in scratch],
        compiler_params=pltpu.CompilerParams(vmem_limit_bytes=VMEM_LIMIT),
        **specs,
        cost_estimate=pl.CostEstimate(flops=flops, bytes_accessed=0, transcendentals=0),
    )(*args)


def iota(extent, dim):
    return lax.broadcasted_iota(jnp.int32, extent, dim)


def one_hot(condition):
    rows = iota((LANES, LANES), 0)
    columns = iota((LANES, LANES), 1)
    return jnp.where(condition(rows, columns), 1.0, 0.0).astype(jnp.bfloat16)


def dot(left, right):
    return lax.dot_general(
        left,
        right,
        (((1,), (0,)), ((), ())),
        precision=lax.Precision.HIGHEST,
        preferred_element_type=F32,
    )


def dot_ones(left, right):
    large = left.astype(jnp.bfloat16)
    rest = left - large.astype(F32)
    middle = rest.astype(jnp.bfloat16)
    small = (rest - middle.astype(F32)).astype(jnp.bfloat16)
    return lax.dot_general(
        jnp.concatenate([large, middle, small], axis=1),
        jnp.concatenate([right, right, right], axis=0),
        (((1,), (0,)), ((), ())),
        preferred_element_type=F32,
    )


def seven_sum(source, plane, below, above, wanted=None):
    tiles = source.shape[0]
    rows = source.shape[2]
    center = [source[t, plane] for t in range(tiles)]
    left = [pltpu.roll(v, 1, 1) for v in center]
    right = [pltpu.roll(v, LANES - 1, 1) for v in center]
    if tiles > 1:
        lane = iota((rows, LANES), 1)
        left = [jnp.where(lane == 0, left[t - 1], left[t]) for t in range(tiles)]
        right = [
            jnp.where(lane == LANES - 1, right[(t + 1) % tiles], right[t]) for t in range(tiles)
        ]
    out = []
    for t in range(tiles if wanted is None else wanted):
        v = center[t]
        total = v + (source[t, below] + source[t, above])
        total = total + (pltpu.roll(v, 1, 0) + pltpu.roll(v, rows - 1, 0))
        out.append(total + (left[t] + right[t]))
    return out


def sweep(*args, **options):
    for _ in sweep_steps(*args, **options):
        pass


def together(*runs):
    waiting = list(runs)
    while waiting:
        for run in list(waiting):
            if next(run, "end") == "end":
                waiting.remove(run)


def sweep_steps(target, source, low, high, base=None, scale=None, period=None, span=None):
    for plane in range(low, high):
        below, above = plane - 1, plane + 1
        if period is not None:
            below, above = below % period, above % period
        for t, value in enumerate(seven_sum(source, plane, below, above)):
            if scale is not None:
                value = value * scale
            if base is not None and (span is None or span[0] <= plane < span[1]):
                value = value + base[t, plane]
            target[t, plane] = value
        yield


PLANE0 = 6
ROW0 = 8
SPILL = 5


def fill_source(field, target):
    planes, rows = field.shape[1], field.shape[2]
    lane = iota((rows, LANES), 1)
    row = iota((rows, LANES), 0)
    row8 = iota((8, LANES), 0)
    zero8 = jnp.zeros((8, LANES), F32)
    zeros = jnp.zeros((rows, LANES), F32)

    def one_plane(i, before):
        along_x, along_y, along_z = field[0, i], field[1, i], field[2, i]
        value = before - along_x - along_y - along_z
        value = value + jnp.where(row == 0, 0.0, pltpu.roll(along_y, 1, 0))
        turned = pltpu.roll(along_z, 1, 1)
        value = value + jnp.where(lane == 0, 0.0, turned)
        p = PLANE0 + i
        target[0, p, 0:ROW0] = zero8
        target[0, p, ROW0 : ROW0 + rows] = value
        last = pltpu.roll(along_y[rows - 8 : rows], 1, 0)
        target[0, p, ROW0 + rows : ROW0 + rows + 8] = jnp.where(row8 == 0, last, 0.0)
        target[1, p, 0:ROW0] = zero8
        target[1, p, ROW0 : ROW0 + rows] = jnp.where(lane == 0, turned, 0.0)
        target[1, p, ROW0 + rows : ROW0 + rows + 8] = zero8

    for i in range(planes):
        one_plane(i, field[0, i - 1] if i else zeros)
    p = PLANE0 + planes
    target[0, p] = jnp.zeros(target.shape[2:], F32)
    target[1, p] = jnp.zeros(target.shape[2:], F32)
    target[0, p, ROW0 : ROW0 + rows] = field[0, planes - 1]


def clear_planes(target, planes):
    for t in range(target.shape[0]):
        for p in planes:
            target[t, p] = jnp.zeros(target.shape[2:], F32)


def pack_lanes(read, count, first, width, spacing, rows):
    lane = iota((rows, LANES), 1)
    per_tile = LANES // spacing
    tiles = []
    for start in range(0, count, per_tile):
        packed = jnp.zeros((rows, LANES), F32)
        for k in range(min(per_tile, count - start)):
            turned = pltpu.roll(read(start + k), (spacing * k - first) % LANES, 1)
            inside = (lane >= spacing * k) & (lane < spacing * k + width)
            packed = jnp.where(inside, turned, packed)
        tiles.append(packed)
    return tiles


def unpacked(packed, k, spacing, offset, width, first, rows):
    lane = iota((rows, LANES), 1)
    turned = pltpu.roll(packed, (first - spacing * k - offset) % LANES, 1)
    inside = (lane >= first) & (lane < first + width)
    return jnp.where(inside, turned, 0.0)


def clear_margin(target, low, high):
    clear_planes(target, (low - 2, low - 1, high, high + 1))


def spread_kernel(field, message, g2_out, g1_out, zeroth, first, second, third, g1_a, g1_b):
    planes = field.shape[1]
    fill_source(field, zeroth)
    low, high = PLANE0, PLANE0 + planes + 1
    clear_margin(zeroth, low, high)
    powers = (zeroth, first, second, third)
    for k in (1, 2, 3):
        sweep(powers[k], powers[k - 1], low - k, high + k)
        clear_margin(powers[k], low - k, high + k)

    n1 = planes // 2
    rows1 = first.shape[2] // 2
    pieces = []
    for t in range(2):
        parts = []
        for c in range(-2, n1 + 2):
            p = PLANE0 + 2 * c
            total = third[t, p, pl.ds(0, rows1, stride=2), :]
            total = total + third[t, p, pl.ds(1, rows1, stride=2), :]
            total = total + third[t, p + 1, pl.ds(0, rows1, stride=2), :]
            total = total + third[t, p + 1, pl.ds(1, rows1, stride=2), :]
            parts.append(total)
        pieces.append(jnp.concatenate(parts, axis=0))
    main = one_hot(lambda r, c: c == 32 + r // 2)
    side = one_hot(lambda r, c: c == jnp.where(r < 64, 96 + r // 2, r // 2 - 32))
    g1 = (dot_ones(pieces[0], main) + dot_ones(pieces[1], side)) * (0.125 / 343.0)
    share = n1 + 4
    g1 = g1.reshape(share, rows1, LANES)
    g1_out[...] = g1

    clear_planes(g1_a, range(g1_a.shape[1]))
    clear_planes(g1_b, range(g1_b.shape[1]))
    for c in range(share):
        g1_a[0, 4 + c, 4 : 4 + rows1] = g1[c]
    sweep(g1_b, g1_a, 3, 5 + share)
    sweep(g1_a, g1_b, 2, 6 + share)
    sweep(g1_b, g1_a, 1, 7 + share)
    rows2 = g1_a.shape[2] // 2
    parts = []
    for c in range(g1_a.shape[1] // 2):
        total = g1_b[0, 2 * c, pl.ds(0, rows2, stride=2), :]
        total = total + g1_b[0, 2 * c, pl.ds(1, rows2, stride=2), :]
        total = total + g1_b[0, 2 * c + 1, pl.ds(0, rows2, stride=2), :]
        total = total + g1_b[0, 2 * c + 1, pl.ds(1, rows2, stride=2), :]
        parts.append(total)
    groups = -(-len(parts) // 3)
    parts.extend([jnp.zeros((rows2, LANES), F32)] * (3 * groups - len(parts)))
    g2 = None
    for slot in range(3):
        matrix = one_hot(
            lambda r, c: (c == r // 2 - 13 + 42 * slot) & (r // 2 >= 13) & (r // 2 < 51)
        )
        term = dot_ones(jnp.concatenate(parts[slot::3], axis=0), matrix)
        g2 = term if g2 is None else g2 + term
    g2_out[...] = g2 * (0.125 / 343.0)
    lane = iota((ROWS_SENT, LANES), 1)
    sides = jnp.zeros((ROWS_SENT, LANES), F32)
    for q in range(share // 2):
        even, odd = g1_out[2 * q, 2 : 2 + ROWS_SENT], g1_out[2 * q + 1, 2 : 2 + ROWS_SENT]
        value = jnp.where(lane < 64, pltpu.roll(even, LANES - 32, 1), pltpu.roll(odd, 32, 1))
        message[ROWS_SENT * q : ROWS_SENT * (q + 1)] = value
        for c, value in ((2 * q, even), (2 * q + 1, odd)):
            low = pltpu.roll(value, (8 * c - 28) % LANES, 1)
            high = pltpu.roll(value, (8 * c + 4 - 96) % LANES, 1)
            sides = jnp.where((lane >= 8 * c) & (lane < 8 * c + 4), low, sides)
            sides = jnp.where((lane >= 8 * c + 4) & (lane < 8 * c + 8), high, sides)
    size = ROWS_SENT * (share // 2)
    message[size : size + ROWS_SENT] = sides
    size = size + ROWS_SENT
    rows0 = zeroth.shape[2] - ROW0
    lane = iota((rows0, LANES), 1)

    def last_columns(i):
        p = PLANE0 + i
        return jnp.where(lane == 0, zeroth[1, p, ROW0:], zeroth[0, p, ROW0:])

    def first_columns(i):
        return zeroth[0, PLANE0 + i, ROW0:]

    last = pack_lanes(last_columns, planes + 1, LANES - SPILL, SPILL + 1, 7, rows0)[0]
    message[size : size + rows0] = last
    first = pack_lanes(first_columns, planes + 1, 0, SPILL + 1, 7, rows0)[0]
    message[size + rows0 :] = first


def gather_z_kernel(count, *refs):
    shares, out = refs[:count], refs[count]
    size = shares[0].shape[0]
    period = 32 * count
    rows2 = 16
    tiles, planes = out.shape[0], out.shape[1]
    lane = iota((size, LANES), 1)
    for slot in range(3):
        totals = [jnp.zeros((size, LANES), F32) for _ in range(tiles)]
        for o in range(count):
            shift = (32 * o + 13 - 42 * slot) % LANES
            turned = pltpu.roll(shares[o][...], shift, 1) if shift else shares[o][...]
            position = ((lane - shift) & (LANES - 1)) - 42 * slot
            inside = (position >= 0) & (position < 38)
            for t in range(tiles):
                lands = lax.rem(position + (32 * o + 13 + period), period) == lane + LANES * t
                totals[t] = totals[t] + jnp.where(inside & lands, turned, 0.0)
        for t in range(tiles):
            for c in range(slot, planes, 3):
                out[t, c] = totals[t][rows2 * (c // 3) : rows2 * (c // 3 + 1)]


ROWS_SENT = 20


def plane_sent(message, share, c):
    lane = iota((ROWS_SENT, LANES), 1)
    pair = message[ROWS_SENT * (c // 2) : ROWS_SENT * (c // 2 + 1)]
    inside = (lane >= 32) & (lane < 96)
    value = jnp.where(inside, pltpu.roll(pair, LANES - 32 if c % 2 else 32, 1), 0.0)
    start = ROWS_SENT * (share // 2)
    sides = message[start : start + ROWS_SENT]
    low = pltpu.roll(sides, (28 - 8 * c) % LANES, 1)
    high = pltpu.roll(sides, (92 - 8 * c) % LANES, 1)
    value = jnp.where((lane >= 28) & (lane < 32), low, value)
    return jnp.where((lane >= 96) & (lane < 100), high, value)


def rows_kernel(sources, strips, *refs):
    inputs, (out, up, down) = refs[:-3], refs[-3:]
    own, messages = inputs[0], inputs[1:]
    planes, share = out.shape[0], own.shape[0]
    read = {}
    for p in range(planes):
        total = None
        for index, offset in sources:
            c = p - 7 - 8 * offset + 2
            if not 0 <= c < share:
                continue
            if (index, c) not in read:
                if index == 0:
                    read[index, c] = own[c, 2 : 2 + ROWS_SENT]
                else:
                    read[index, c] = plane_sent(messages[index], share, c)
            value = read[index, c]
            total = value if total is None else total + value
        out[p] = total
        down[9 * p : 9 * p + 9] = total[0:9]
        up[9 * p : 9 * p + 9] = total[11:20]
    start = ROWS_SENT * (share // 2 + 1)
    inner = (messages[0].shape[0] - start) // 2
    place = 9 * planes
    for k in range(strips):
        for part in range(2):
            begin = start + inner * part
            down[place : place + 6] = messages[k][begin : begin + 6]
            last = begin + inner - 8 - SPILL
            up[place : place + 6] = messages[k][last : last + 6]
            place += 6


def columns_kernel(strips, g1, *refs):
    messages, (above, below), (out, up, down) = refs[:-5], refs[-5:-3], refs[-3:]
    planes, rows = out.shape[0], out.shape[1]
    for p in range(planes):
        out[p] = jnp.zeros((rows, LANES), F32)
        out[p, 6 : 6 + ROWS_SENT] = g1[p]
        out[p, 22:31] = out[p, 22:31] + above[9 * p : 9 * p + 9]
        out[p, 1:10] = out[p, 1:10] + below[9 * p : 9 * p + 9]
    share = planes - 10
    start = ROWS_SENT * (share // 2 + 1)
    inner = (messages[0].shape[0] - start) // 2
    for target, first, part in ((up, 89, 0), (down, 30, 1)):
        place = 0
        for packed in pack_lanes(lambda p: out[p], planes, first, 9, 9, rows):
            target[place : place + rows] = packed
            place += rows
        for k in range(strips):
            begin = start + inner * part
            six = 9 * planes + 6 * (2 * k + part)
            target[place : place + ROW0] = jnp.zeros((ROW0, LANES), F32)
            target[place + ROW0 : place + ROW0 + inner] = messages[k][begin : begin + inner]
            at = place + ROW0 - SPILL
            target[at : at + 6] = target[at : at + 6] + below[six : six + 6]
            at = place + ROW0 + inner - 8
            target[at : at + 6] = target[at : at + 6] + above[six : six + 6]
            place += ROW0 + inner


def fold_x_kernel(count, *refs):
    shares, out = refs[:count], refs[count]
    tiles, period = out.shape[0], out.shape[1]
    for t in range(tiles):
        for x in range(period):
            total = None
            for o in range(count):
                for c in range(10):
                    if (c - 3 + 4 * o) % period == x:
                        value = shares[o][t, c]
                        total = value if total is None else total + value
            out[t, x] = total


def fine_sweeps(base, first, second):
    seventh = 1.0 / 7.0
    planes = base.shape[1]
    yield from sweep_steps(first, base, 1, planes - 1, base, seventh)
    yield from sweep_steps(second, first, 2, planes - 2, base, seventh)
    yield from sweep_steps(first, second, 3, planes - 3, base, seventh)
    yield from sweep_steps(second, first, 4, planes - 4, base, seventh)


def window_kernel(g1, out, base, first, second):
    for p in range(base.shape[1]):
        base[0, p] = g1[p]
    together(fine_sweeps(base, first, second))
    for c in range(out.shape[0]):
        p = 5 + c
        out[c] = (seven_sum(second, p, p - 1, p + 1)[0] * (1.0 / 7.0) + base[0, p]) * weight(1)


WINDOW_LANES = 28


def window_edge_steps(f1, above, below, out, base, first, second):
    rows = base.shape[2]
    share = out.shape[0]
    size = share // 4
    planes = share + 10
    lane = iota((rows, LANES), 1)
    turned = []
    for begin in range(0, rows * -(-planes // 14), rows):
        turned.append((below[begin : begin + rows],
                       pltpu.roll(above[begin : begin + rows], 19, 1)))
    for j in range(base.shape[1]):
        value = jnp.zeros((rows, LANES), F32)
        for q in range(4):
            p = size * q + j
            lower, upper = turned[p // 14]
            shift = 9 * (p % 14)
            term = jnp.where(((lane - shift) & (LANES - 1)) < 14, lower, upper)
            shift = (WINDOW_LANES * q - shift) % LANES
            term = pltpu.roll(term, shift, 1) if shift else term
            place = lane - WINDOW_LANES * q
            inside = (place >= 0) & (place < WINDOW_LANES) & ((place < 9) | (place >= 19))
            value = jnp.where(inside, term, value)
        base[0, j] = value
        yield
    yield from fine_sweeps(base, first, second)
    for m in range(size):
        p = 5 + m
        value = seven_sum(second, p, p - 1, p + 1)[0] * (1.0 / 7.0) + base[0, p]
        value = value * weight(1)
        for q in range(4):
            c = size * q + m
            low = pltpu.roll(value, (25 - WINDOW_LANES * q) % LANES, 1)
            high = pltpu.roll(value, (75 - WINDOW_LANES * q) % LANES, 1)
            part = jnp.where((lane >= 89) & (lane < 98), high, 0.0)
            out[c] = f1[c] + jnp.where((lane >= 30) & (lane < 39), low, part)
        yield


def restrict_lanes(values, width, coarse_width, coarse_tiles):
    out = []
    for s in range(coarse_tiles):
        total = None
        for t, value in enumerate(values):
            matrix = one_hot(
                lambda r, c: ((LANES * t + r) // 2 == lax.rem(LANES * s + c, coarse_width))
                & (LANES * t + r < width)
            )
            term = dot_ones(value, matrix)
            total = term if total is None else total + term
        out.append(total)
    return out


def prolong_lanes(values, width, fine_tiles):
    out = []
    for s in range(fine_tiles):
        total = None
        for t, value in enumerate(values):
            matrix = one_hot(lambda r, c: LANES * t + r == lax.rem(LANES * s + c, width) // 2)
            term = dot_ones(value, matrix)
            total = term if total is None else total + term
        out.append(total)
    return out


def swept(values):
    rows = values[0].shape[0]
    out = []
    for p, v in enumerate(values):
        total = v + (values[p - 1] + values[(p + 1) % len(values)])
        total = total + (pltpu.roll(v, 1, 0) + pltpu.roll(v, rows - 1, 0))
        out.append((total + (pltpu.roll(v, 1, 1) + pltpu.roll(v, LANES - 1, 1))) * (1.0 / 7.0))
    return out


def real_waves(count):
    cells = np.arange(count)
    rows, eigenvalues = [], []
    for k in range(count // 2 + 1):
        angle = 2.0 * np.pi * k / count
        rows.append(np.cos(angle * cells))
        eigenvalues.append(2.0 * np.cos(angle))
        if 0 < k < count / 2:
            rows.append(np.sin(angle * cells))
            eigenvalues.append(2.0 * np.cos(angle))
    basis = np.stack(rows)
    basis = basis / np.sqrt(np.sum(basis * basis, axis=1, keepdims=True))
    return basis, np.array(eigenvalues)


def last_level_matrices(planes, rows, width):
    wave_x, value_x = real_waves(planes)
    wave_y, value_y = real_waves(rows)
    wave_z, value_z = real_waves(width)
    into = np.kron(np.repeat(wave_x, 2, axis=1), np.repeat(wave_y, 2, axis=1))
    level_values = value_x[:, None, None] + value_y[None, :, None] + value_z[None, None, :]
    factor = (1.0 + level_values) / 7.0
    total = sum(factor**k for k in range(COARSE_ITERS)) * weight(LEVELS - 1) * 0.125
    scale = np.zeros((planes * rows, LANES))
    scale[:, :width] = total.reshape(planes * rows, width)
    fine = 2 * width
    tiles = max(1, fine // LANES)
    lanes = np.arange(LANES * tiles)
    to_waves = np.zeros((LANES * tiles, LANES))
    to_waves[:fine, :width] = wave_z.T[lanes[:fine] // 2]
    from_waves = np.zeros((LANES, LANES * tiles))
    from_waves[:width] = wave_z[:, (lanes % fine) // 2]
    to_waves = to_waves.reshape(tiles, LANES, LANES)
    from_waves = from_waves.reshape(LANES, tiles, LANES).transpose(1, 0, 2)
    arrays = (into, into.T, to_waves, from_waves, scale)
    return [jnp.asarray(np.ascontiguousarray(a), F32) for a in arrays]


def solve_last(values, into, back, to_waves, from_waves, scale):
    values = dot(into[...], values)
    yield
    values = dot(values, to_waves[0]) * scale[...]
    yield
    values = dot(back[...], values)
    yield
    return dot(values, from_waves[0])


def solve(level, width, buffers, spectral):
    g, a, b = buffers[level]
    tiles, planes, rows = g.shape[0], g.shape[1], g.shape[2]
    seventh = 1.0 / 7.0
    w = weight(level)
    if level == LEVELS - 2:
        source = [g[0, p] for p in range(planes)]
        first = swept(source)
        yield
        second = swept(first)
        yield
        third = swept(second)
        yield
        before = [(x + y + z) * w for x, y, z in zip(source, first, second)]
        values = yield from solve_last(jnp.concatenate(third, axis=0), *spectral)
        error = [before[p] + values[rows * p : rows * (p + 1)] for p in range(planes)]
        yield
        for _ in range(SWEEPS):
            error = swept(error)
            yield
        for p in range(planes):
            g[0, p] = before[p] + error[p]
        return
    yield from sweep_steps(a, g, 0, planes, None, seventh, planes)
    yield from sweep_steps(b, a, 0, planes, None, seventh, planes)
    for t in range(tiles):
        for p in range(planes):
            g[t, p] = (g[t, p] + a[t, p] + b[t, p]) * w
    yield from sweep_steps(a, b, 0, planes, None, seventh, planes)
    half = rows // 2
    values = []
    for t in range(tiles):
        parts = []
        for c in range(planes // 2):
            total = a[t, 2 * c, pl.ds(0, half, stride=2), :]
            total = total + a[t, 2 * c, pl.ds(1, half, stride=2), :]
            total = total + a[t, 2 * c + 1, pl.ds(0, half, stride=2), :]
            total = total + a[t, 2 * c + 1, pl.ds(1, half, stride=2), :]
            parts.append(total)
        values.append(jnp.concatenate(parts, axis=0))
    coarse = buffers[level + 1][0]
    values = restrict_lanes(values, width, width // 2, coarse.shape[0])
    for t, value in enumerate(values):
        for c in range(planes // 2):
            coarse[t, c] = value[half * c : half * (c + 1)] * 0.125
    yield from solve(level + 1, width // 2, buffers, spectral)
    values = [
        jnp.concatenate([coarse[t, c] for c in range(planes // 2)], axis=0)
        for t in range(coarse.shape[0])
    ]
    values = prolong_lanes(values, width, tiles)
    for t, value in enumerate(values):
        for c in range(planes // 2):
            part = value[half * c : half * (c + 1)]
            for p in (2 * c, 2 * c + 1):
                b[t, p, pl.ds(0, half, stride=2), :] = part
                b[t, p, pl.ds(1, half, stride=2), :] = part
        for p in range(planes):
            b[t, p] = b[t, p] + g[t, p]
    yield from sweep_steps(a, b, 0, planes, None, seventh, planes)
    yield from sweep_steps(b, a, 0, planes, None, seventh, planes)
    yield from sweep_steps(a, b, 0, planes, None, seventh, planes)
    for t in range(tiles):
        for p in range(planes):
            g[t, p] = g[t, p] + a[t, p]


def coarse_steps(count, *refs):
    shares, spectral = refs[:count], refs[count : count + 5]
    out, scratch = refs[count + 5], refs[count + 6 :]
    buffers = {level: scratch[3 * (level - 2) : 3 * (level - 1)] for level in (2, 3)}
    g = buffers[2][0]
    tiles, planes = g.shape[0], g.shape[1]
    for t in range(tiles):
        for p in range(planes):
            for b in range(count):
                value = shares[b][t, p, 0:8] + shares[(b - 1) % count][t, p, 8:16]
                g[t, p, 8 * b : 8 * b + 8] = value
    yield from solve(2, LANES * tiles, buffers, spectral)
    for c in range(out.shape[0]):
        out[c] = g[0, (c - 3) % planes, 0:16]


def arrived_kernel(above, below, out):
    out[...] = jnp.zeros(out.shape, F32)


def late_kernel(count, sources, planes, *refs):
    shares, rest = refs[: count + 5], refs[count + 5 :]
    f1, above, below, own, e2_out, f1_out, edge_out = rest[:7]
    scratch = rest[7:]
    together(
        coarse_steps(count, *shares, e2_out, *scratch[:6]),
        window_edge_steps(f1, above, below, f1_out, *scratch[6:9]),
        fine_edge_steps(sources, planes, above, below, own, edge_out, *scratch[9:12]),
    )


def correct_kernel(e2, f1, u0_b, u1_a, u1_b, u0_a):
    share1 = f1.shape[0]
    share2 = e2.shape[0]
    rows2 = e2.shape[1]
    value = e2[...].reshape(share2 * rows2, LANES)
    value = dot_ones(value, one_hot(lambda r, c: r == c // 2))
    for c in range(share2):
        part = value[rows2 * c : rows2 * (c + 1)]
        for p in (2 * c, 2 * c + 1):
            u1_a[0, p, pl.ds(0, rows2, stride=2), :] = part
            u1_a[0, p, pl.ds(1, rows2, stride=2), :] = part
    count1 = 2 * share2
    sweep(u1_b, u1_a, 1, count1 - 1)
    sweep(u1_a, u1_b, 2, count1 - 2)
    sweep(u1_b, u1_a, 3, count1 - 3)
    rows1, sent = 24, 20
    parts = []
    for c in range(share1):
        parts.append(f1[c, 6 : 6 + rows1] + u1_b[0, 4 + c, 6 : 6 + rows1] * (1.0 / 343.0))
    value = jnp.concatenate(parts, axis=0)
    main = dot_ones(value, one_hot(lambda r, c: r == 32 + c // 2))
    side = dot_ones(value, one_hot(lambda r, c: r == jnp.where(c < 64, 96 + c // 2, c // 2 - 32)))
    for t, value in enumerate((main, side)):
        for c in range(share1):
            part = value[rows1 * c : rows1 * c + sent]
            for p in (2 * c, 2 * c + 1):
                u0_a[t, p, pl.ds(0, sent, stride=2), :] = part
                u0_a[t, p, pl.ds(1, sent, stride=2), :] = part
    count0 = 2 * share1
    sweep(u0_b, u0_a, 1, count0 - 1)
    sweep(u0_a, u0_b, 2, count0 - 2)
    sweep(u0_b, u0_a, 3, count0 - 3)


def plane_copies(source, target, semaphores):
    step = source.shape[1] // semaphores.shape[0]
    copies = []
    for k in range(semaphores.shape[0]):
        planes = pl.ds(step * k, step)
        copies.append(
            pltpu.make_async_copy(source.at[:, planes], target.at[:, planes], semaphores.at[k])
        )
    return copies


def finish_kernel(field, u0_b, f0, below_x, above_x, edge, result, out, finished):
    planes, rows = field.shape[1], field.shape[2]
    scale = 1.0 / 343.0
    lane = iota((rows, LANES), 1)
    row = iota((rows, LANES), 0)
    copies = plane_copies(out, result, finished)
    step = planes // len(copies)

    def potential(i):
        q, m = i // edge.shape[0], i % edge.shape[0]
        value = u0_b[0, 4 + i, 4 : 4 + rows] * scale + f0[fine_place(i + SPILL, planes + 11)]
        if i <= SPILL:
            value = value + below_x[1 + i]
        if i >= planes - SPILL:
            value = value + above_x[i - (planes - SPILL)]
        return value + edge_sides(edge[m, 0:rows], q)

    here = potential(0)
    for i in range(planes):
        above = potential(i + 1)
        out[0, i] = field[0, i] - (above - here)
        q, m = i // edge.shape[0], i % edge.shape[0]
        end = u0_b[0, 4 + i, 4 + rows : 5 + rows] * scale + f0[6, i + SPILL : i + SPILL + 1]
        if i <= SPILL:
            end = end + below_x[0, i + SPILL + planes : i + SPILL + planes + 1]
        if i >= planes - SPILL:
            end = end + above_x[6, i + SPILL - planes : i + SPILL - planes + 1]
        end = end + edge_sides(edge[m, rows : rows + 1], q)
        end = jnp.broadcast_to(end, (rows, LANES))
        next_y = jnp.where(row == rows - 1, end, pltpu.roll(here, rows - 1, 0))
        out[1, i] = field[1, i] - (next_y - here)
        part = edge[m, 0:rows]
        last = pltpu.roll(u0_b[1, 4 + i, 4 : 4 + rows], LANES - 1, 1) * scale
        last = last + turned_to_last(part, GROUP_LANES * q + HIGH_AT)
        last = last + turned_to_last(part, GROUP_LANES * q + OWN_AT + SPILL)
        next_z = jnp.where(lane == LANES - 1, last, pltpu.roll(here, LANES - 1, 1))
        out[2, i] = field[2, i] - (next_z - here)
        if i % step == step - 1:
            copies[i // step].start()
        here = above
    for copy in copies:
        copy.wait()


def fine_place(p, share):
    if p <= SPILL:
        return p
    return p - share + 13 if p >= share - 6 else p + 7


def fine_own_kernel(zeroth, first, second, third, field, main, down, up, field_out, fourth):
    share = main.shape[0]
    field_out[...] = field[...]
    low, high = PLANE0, zeroth.shape[1] - 6
    sweep(fourth, third, low - 4, high + 4)
    clear_margin(fourth, low - 4, high + 4)
    powers = (zeroth, first, second, third, fourth)
    for k in range(share):
        p = low - SPILL + k
        total = seven_sum(fourth, p, p - 1, p + 1, 1)[0] * (weight(0) / 7.0**5)
        for n, power in enumerate(powers):
            if low - n <= p < high + n:
                total = total + power[0, p] * (weight(0) / 7.0**n)
        main[k] = total
        down[k] = total[1:9]
        up[k] = total[40:48]


GROUPS = 3
GROUP_LANES = 42
LOW_END, HIGH_AT, OWN_AT = 5, 16, 22


def fine_edge_steps(sources, planes, above, below, own, out, base, first, second):
    rows = base.shape[2]
    size = out.shape[0]
    lane = iota((rows, LANES), 1)
    strips = 1 + max(index for index, offset in sources)
    start = above.shape[0] - rows * strips
    turned = []
    for index in range(strips):
        begin = start + rows * index
        turned.append((below[begin : begin + rows],
                       pltpu.roll(above[begin : begin + rows], HIGH_AT, 1),
                       pltpu.roll(own[begin : begin + rows], OWN_AT, 1)))
    spread = SPILL + 1
    for j in range(base.shape[1]):
        value = jnp.zeros((rows, LANES), F32)
        for q in range(GROUPS):
            total = None
            for index, offset in sources:
                i = size * q + j - SPILL - offset * planes
                if not 0 <= i <= planes:
                    continue
                low, high, last = turned[index]
                place = (lane - 7 * i) & (LANES - 1)
                term = jnp.where(place < OWN_AT, jnp.where(place < HIGH_AT, low, high), last)
                shift = (GROUP_LANES * q - 7 * i) % LANES
                term = pltpu.roll(term, shift, 1) if shift else term
                total = term if total is None else total + term
            if total is None:
                continue
            place = lane - GROUP_LANES * q
            inside = (place >= 0) & (place < OWN_AT + spread)
            inside = inside & ((place < spread) | (place >= HIGH_AT))
            value = jnp.where(inside, total, value)
        base[0, j] = value
        yield
    seventh = 1.0 / 7.0
    yield from fine_sweeps(base, first, second)
    kept = out.shape[1]
    for i in range(size):
        p = SPILL + i
        value = (seven_sum(second, p, p - 1, p + 1)[0] * seventh + base[0, p]) * weight(0)
        out[i] = value[ROW0 : ROW0 + kept]
        yield


def edge_sides(part, q):
    lane = iota(part.shape, 1)
    low = pltpu.roll(part, (-GROUP_LANES * q - LOW_END) % LANES, 1)
    high = pltpu.roll(part, (LANES - SPILL - GROUP_LANES * q - LOW_END - 6) % LANES, 1)
    return jnp.where(lane <= SPILL, low, jnp.where(lane >= LANES - SPILL, high, 0.0))


def turned_to_last(value, lane):
    return pltpu.roll(value, (LANES - 1 - lane) % LANES, 1)


def fine_y_kernel(main, above, below, out, work):
    share = main.shape[0]
    rows = out.shape[1]
    out[6] = jnp.zeros((rows, LANES), F32)
    for p in range(share):
        work[p] = main[p]
        work[p, 33:41] = work[p, 33:41] + above[p]
        work[p, 8:16] = work[p, 8:16] + below[p]
        out[fine_place(p, share)] = work[p, ROW0 : ROW0 + rows]
        out[6, p : p + 1] = work[p, ROW0 + rows : ROW0 + rows + 1]


def body(field):
    nx, ny, nz = field.shape[1:]
    size_x, size_y, size_z = lax.axis_size("gx"), lax.axis_size("gy"), lax.axis_size("gz")
    n1 = nx // 2
    share1 = n1 + 4
    rows0 = ny + 16
    rows1 = ny // 2 + 8
    planes0 = nx + 13

    def from_offset(value, axis, offset):
        count = lax.axis_size(axis)
        pairs = [(source, (source - offset) % count) for source in range(count)]
        return lax.ppermute(value, axis, pairs)

    level0 = (2, planes0, rows0, LANES)
    level1 = (1, n1 + 12, ny // 2 + 16, LANES)
    packed = -(-(n1 // 2 + 6) // 3) * 16
    inner0 = rows0 - ROW0
    sent1 = ROWS_SENT * (share1 // 2 + 1)
    message, g2, g1, *powers = call(
        spread_kernel,
        [shape(sent1 + 2 * inner0, LANES), shape(packed, LANES),
         shape(share1, rows1, LANES)] + [shape(*level0)] * 4,
        [level1, level1],
        2.9,
        field,
    )
    shares = [g2] + [from_offset(g2, "gz", o) for o in range(1, size_z)]
    messages = {0: message}
    sources = []
    for o in (0, 1, -1, 2, -2):
        key = [k for k in messages if k % size_x == o % size_x]
        if not key:
            messages[o] = from_offset(message, "gx", o)
            key = [o]
        sources.append((list(messages).index(key[0]), o))
    messages = list(messages.values())
    strips = min(3, size_x)
    planes1 = n1 + 14
    sent_y = 9 * planes1 + 12 * strips
    rows_g1, up, down = call(
        functools.partial(rows_kernel, tuple(sources), strips),
        [shape(planes1, ROWS_SENT, LANES), shape(sent_y, LANES), shape(sent_y, LANES)],
        [],
        0.2,
        g1, *messages,
    )
    window = (1, planes1, ny // 2 + 16, LANES)
    sent_z = window[2] * -(-planes1 // 14) + rows0 * strips
    window_g1, up, down = call(
        functools.partial(columns_kernel, strips),
        [shape(*window[1:]), shape(sent_z, LANES), shape(sent_z, LANES)],
        [],
        0.3,
        rows_g1, *messages[:strips], from_offset(down, "gy", 1), from_offset(up, "gy", -1),
    )
    above = from_offset(down, "gz", 1)
    below = from_offset(up, "gz", -1)
    f1 = call(
        window_kernel,
        shape(share1, *window[2:]),
        [window, window, window],
        0.01,
        window_g1,
    )
    packed = (1, share1 // 4 + 10, *window[2:])
    share0 = nx + 11
    main, f_down, f_up, kept = call(
        fine_own_kernel,
        [shape(share0, rows0, LANES), shape(share0, 8, LANES), shape(share0, 8, LANES),
         shape(*field.shape)],
        [level0],
        3.0,
        *powers, field,
        after=(messages[1],),
    )
    f_above = from_offset(f_down, "gy", 1)
    f_below = from_offset(f_up, "gy", -1)

    tiles = size_z * 32 // LANES
    g2 = call(
        functools.partial(gather_z_kernel, size_z),
        shape(tiles, n1 // 2 + 6, 16, LANES),
        [],
        0.15,
        *shares,
        after=(rows_g1, main,),
    )
    shares = [g2] + [from_offset(g2, "gx", o) for o in range(1, size_x)]
    g2 = call(
        functools.partial(fold_x_kernel, size_x),
        shape(tiles, 4 * size_x, 16, LANES),
        [],
        0.05,
        *shares,
        after=(window_g1,),
    )
    shares = [g2] + [from_offset(g2, "gy", o) for o in range(1, size_y)]

    f0 = call(
        fine_y_kernel,
        shape(share0 + 1, ny, LANES),
        [(share0, rows0, LANES)],
        0.01,
        main, f_above, f_below,
        after=(g2,),
    )
    if size_x == 2:
        other = from_offset(f0[0:13], "gx", 1)
        f_above, f_below = other[0:7], other[6:13]
    else:
        f_above = from_offset(f0[0:7], "gx", 1)
        f_below = from_offset(f0[6:13], "gx", -1)
    group = -(-(nx + 1) // GROUPS)
    edges = (1, group + 2 * SPILL, rows0, LANES)
    scratch = []
    for level in (2, 3):
        cut = 2 ** (level - 2)
        extent = (max(1, tiles // cut), 4 * size_x // cut, 8 * size_y // cut, LANES)
        scratch.extend([extent] * 3)
    arrived = call(arrived_kernel, shape(8, LANES), [], 2.0, above, below)
    e2, f1, edge = call(
        functools.partial(late_kernel, size_y, tuple(sources[:3]), nx),
        [shape(n1 // 2 + 6, 16, LANES), shape(share1, *window[2:]), shape(group, ny + 8, LANES)],
        scratch + [packed] * 3 + [edges] * 3,
        3.0,
        *shares, *last_level_matrices(size_x, 2 * size_y, 8 * size_z), f1, above, below, up,
        after=(arrived,),
    )
    fine = (2, nx + 8, ny + 8, LANES)
    correction = call(
        correct_kernel,
        shape(*fine),
        [level1, level1, fine],
        2.2,
        e2, f1,
    )
    return call(
        finish_kernel,
        shape(*field.shape),
        [field.shape, pltpu.SemaphoreType.DMA((4,))],
        1.2,
        kept, correction, f0, f_below, f_above, edge,
        out_specs=pl.BlockSpec(memory_space=pltpu.HBM),
    )


def solution(mesh):
    in_specs = (P(None, "gx", "gy", "gz"),)
    out_specs = P(None, "gx", "gy", "gz")
    return jax.shard_map(body, mesh=mesh, in_specs=in_specs, out_specs=out_specs, check_vma=False)
```

```python
import functools

import jax
import jax.numpy as jnp
import numpy as np
from jax import lax
from jax.experimental import pallas as pl
from jax.experimental.pallas import tpu as pltpu
from jax.sharding import PartitionSpec as P

LEVELS = 5
SWEEPS = 3
COARSE_ITERS = 24


F32 = jnp.float32
LANES = 128
VMEM_LIMIT = 16 * 1024 * 1024
PEAK_FLOPS_PER_US = 1150000000.0


def weight(level):
    return 4.0**level / 7.0


def shape(*extent):
    return jax.ShapeDtypeStruct(extent, F32)


def call(kernel, outs, scratch, microseconds, *args, after=(), **specs):
    flops = int(microseconds * PEAK_FLOPS_PER_US)
    if after:
        inner, first, last = kernel, len(args), len(args) + len(after)

        def kernel(*refs):
            inner(*refs[:first], *refs[last:])

        args = (*args, *after)
    return pl.pallas_call(
        kernel,
        out_shape=outs,
        scratch_shapes=[pltpu.VMEM(s, F32) if isinstance(s, tuple) else s for s in scratch],
        compiler_params=pltpu.CompilerParams(vmem_limit_bytes=VMEM_LIMIT),
        **specs,
        cost_estimate=pl.CostEstimate(flops=flops, bytes_accessed=0, transcendentals=0),
    )(*args)


def iota(extent, dim):
    return lax.broadcasted_iota(jnp.int32, extent, dim)


def one_hot(condition):
    rows = iota((LANES, LANES), 0)
    columns = iota((LANES, LANES), 1)
    return jnp.where(condition(rows, columns), 1.0, 0.0).astype(jnp.bfloat16)


def dot(left, right):
    return lax.dot_general(
        left,
        right,
        (((1,), (0,)), ((), ())),
        precision=lax.Precision.HIGHEST,
        preferred_element_type=F32,
    )


def dot_ones(left, right):
    large = left.astype(jnp.bfloat16)
    rest = left - large.astype(F32)
    middle = rest.astype(jnp.bfloat16)
    small = (rest - middle.astype(F32)).astype(jnp.bfloat16)
    return lax.dot_general(
        jnp.concatenate([large, middle, small], axis=1),
        jnp.concatenate([right, right, right], axis=0),
        (((1,), (0,)), ((), ())),
        preferred_element_type=F32,
    )


def seven_sum(source, plane, below, above, wanted=None):
    tiles = source.shape[0]
    rows = source.shape[2]
    center = [source[t, plane] for t in range(tiles)]
    left = [pltpu.roll(v, 1, 1) for v in center]
    right = [pltpu.roll(v, LANES - 1, 1) for v in center]
    if tiles > 1:
        lane = iota((rows, LANES), 1)
        left = [jnp.where(lane == 0, left[t - 1], left[t]) for t in range(tiles)]
        right = [
            jnp.where(lane == LANES - 1, right[(t + 1) % tiles], right[t]) for t in range(tiles)
        ]
    out = []
    for t in range(tiles if wanted is None else wanted):
        v = center[t]
        total = v + (source[t, below] + source[t, above])
        total = total + (pltpu.roll(v, 1, 0) + pltpu.roll(v, rows - 1, 0))
        out.append(total + (left[t] + right[t]))
    return out


def sweep(*args, **options):
    for _ in sweep_steps(*args, **options):
        pass


def together(*runs):
    waiting = list(runs)
    while waiting:
        for run in list(waiting):
            if next(run, "end") == "end":
                waiting.remove(run)


def sweep_steps(target, source, low, high, base=None, scale=None, period=None, span=None):
    for plane in range(low, high):
        below, above = plane - 1, plane + 1
        if period is not None:
            below, above = below % period, above % period
        for t, value in enumerate(seven_sum(source, plane, below, above)):
            if scale is not None:
                value = value * scale
            if base is not None and (span is None or span[0] <= plane < span[1]):
                value = value + base[t, plane]
            target[t, plane] = value
        yield


PLANE0 = 6
ROW0 = 8
SPILL = 5


def fill_source(field, target):
    planes, rows = field.shape[1], field.shape[2]
    lane = iota((rows, LANES), 1)
    row = iota((rows, LANES), 0)
    row8 = iota((8, LANES), 0)
    zero8 = jnp.zeros((8, LANES), F32)
    zeros = jnp.zeros((rows, LANES), F32)

    def one_plane(i, before):
        along_x, along_y, along_z = field[0, i], field[1, i], field[2, i]
        value = before - along_x - along_y - along_z
        value = value + jnp.where(row == 0, 0.0, pltpu.roll(along_y, 1, 0))
        turned = pltpu.roll(along_z, 1, 1)
        value = value + jnp.where(lane == 0, 0.0, turned)
        p = PLANE0 + i
        target[0, p, 0:ROW0] = zero8
        target[0, p, ROW0 : ROW0 + rows] = value
        last = pltpu.roll(along_y[rows - 8 : rows], 1, 0)
        target[0, p, ROW0 + rows : ROW0 + rows + 8] = jnp.where(row8 == 0, last, 0.0)
        target[1, p, 0:ROW0] = zero8
        target[1, p, ROW0 : ROW0 + rows] = jnp.where(lane == 0, turned, 0.0)
        target[1, p, ROW0 + rows : ROW0 + rows + 8] = zero8

    for i in range(planes):
        one_plane(i, field[0, i - 1] if i else zeros)
    p = PLANE0 + planes
    target[0, p] = jnp.zeros(target.shape[2:], F32)
    target[1, p] = jnp.zeros(target.shape[2:], F32)
    target[0, p, ROW0 : ROW0 + rows] = field[0, planes - 1]


def clear_planes(target, planes):
    for t in range(target.shape[0]):
        for p in planes:
            target[t, p] = jnp.zeros(target.shape[2:], F32)


def pack_lanes(read, count, first, width, spacing, rows):
    lane = iota((rows, LANES), 1)
    per_tile = LANES // spacing
    tiles = []
    for start in range(0, count, per_tile):
        packed = jnp.zeros((rows, LANES), F32)
        for k in range(min(per_tile, count - start)):
            turned = pltpu.roll(read(start + k), (spacing * k - first) % LANES, 1)
            inside = (lane >= spacing * k) & (lane < spacing * k + width)
            packed = jnp.where(inside, turned, packed)
        tiles.append(packed)
    return tiles


def unpacked(packed, k, spacing, offset, width, first, rows):
    lane = iota((rows, LANES), 1)
    turned = pltpu.roll(packed, (first - spacing * k - offset) % LANES, 1)
    inside = (lane >= first) & (lane < first + width)
    return jnp.where(inside, turned, 0.0)


def clear_margin(target, low, high):
    clear_planes(target, (low - 2, low - 1, high, high + 1))


def spread_kernel(field, message, g2_out, g1_out, zeroth, first, second, third, g1_a, g1_b):
    planes = field.shape[1]
    fill_source(field, zeroth)
    low, high = PLANE0, PLANE0 + planes + 1
    clear_margin(zeroth, low, high)
    powers = (zeroth, first, second, third)
    for k in (1, 2, 3):
        sweep(powers[k], powers[k - 1], low - k, high + k)
        clear_margin(powers[k], low - k, high + k)

    n1 = planes // 2
    rows1 = first.shape[2] // 2
    pieces = []
    for t in range(2):
        parts = []
        for c in range(-2, n1 + 2):
            p = PLANE0 + 2 * c
            total = third[t, p, pl.ds(0, rows1, stride=2), :]
            total = total + third[t, p, pl.ds(1, rows1, stride=2), :]
            total = total + third[t, p + 1, pl.ds(0, rows1, stride=2), :]
            total = total + third[t, p + 1, pl.ds(1, rows1, stride=2), :]
            parts.append(total)
        pieces.append(jnp.concatenate(parts, axis=0))
    main = one_hot(lambda r, c: c == 32 + r // 2)
    side = one_hot(lambda r, c: c == jnp.where(r < 64, 96 + r // 2, r // 2 - 32))
    g1 = (dot_ones(pieces[0], main) + dot_ones(pieces[1], side)) * (0.125 / 343.0)
    share = n1 + 4
    g1 = g1.reshape(share, rows1, LANES)
    g1_out[...] = g1

    clear_planes(g1_a, range(g1_a.shape[1]))
    clear_planes(g1_b, range(g1_b.shape[1]))
    for c in range(share):
        g1_a[0, 4 + c, 4 : 4 + rows1] = g1[c]
    sweep(g1_b, g1_a, 3, 5 + share)
    sweep(g1_a, g1_b, 2, 6 + share)
    sweep(g1_b, g1_a, 1, 7 + share)
    rows2 = g1_a.shape[2] // 2
    parts = []
    for c in range(g1_a.shape[1] // 2):
        total = g1_b[0, 2 * c, pl.ds(0, rows2, stride=2), :]
        total = total + g1_b[0, 2 * c, pl.ds(1, rows2, stride=2), :]
        total = total + g1_b[0, 2 * c + 1, pl.ds(0, rows2, stride=2), :]
        total = total + g1_b[0, 2 * c + 1, pl.ds(1, rows2, stride=2), :]
        parts.append(total)
    groups = -(-len(parts) // 3)
    parts.extend([jnp.zeros((rows2, LANES), F32)] * (3 * groups - len(parts)))
    g2 = None
    for slot in range(3):
        matrix = one_hot(
            lambda r, c: (c == r // 2 - 13 + 42 * slot) & (r // 2 >= 13) & (r // 2 < 51)
        )
        term = dot_ones(jnp.concatenate(parts[slot::3], axis=0), matrix)
        g2 = term if g2 is None else g2 + term
    g2_out[...] = g2 * (0.125 / 343.0)
    lane = iota((ROWS_SENT, LANES), 1)
    sides = jnp.zeros((ROWS_SENT, LANES), F32)
    for q in range(share // 2):
        even, odd = g1_out[2 * q, 2 : 2 + ROWS_SENT], g1_out[2 * q + 1, 2 : 2 + ROWS_SENT]
        value = jnp.where(lane < 64, pltpu.roll(even, LANES - 32, 1), pltpu.roll(odd, 32, 1))
        message[ROWS_SENT * q : ROWS_SENT * (q + 1)] = value
        for c, value in ((2 * q, even), (2 * q + 1, odd)):
            low = pltpu.roll(value, (8 * c - 28) % LANES, 1)
            high = pltpu.roll(value, (8 * c + 4 - 96) % LANES, 1)
            sides = jnp.where((lane >= 8 * c) & (lane < 8 * c + 4), low, sides)
            sides = jnp.where((lane >= 8 * c + 4) & (lane < 8 * c + 8), high, sides)
    size = ROWS_SENT * (share // 2)
    message[size : size + ROWS_SENT] = sides
    size = size + ROWS_SENT
    rows0 = zeroth.shape[2] - ROW0
    lane = iota((rows0, LANES), 1)

    def last_columns(i):
        p = PLANE0 + i
        return jnp.where(lane == 0, zeroth[1, p, ROW0:], zeroth[0, p, ROW0:])

    def first_columns(i):
        return zeroth[0, PLANE0 + i, ROW0:]

    last = pack_lanes(last_columns, planes + 1, LANES - SPILL, SPILL + 1, 7, rows0)[0]
    message[size : size + rows0] = last
    first = pack_lanes(first_columns, planes + 1, 0, SPILL + 1, 7, rows0)[0]
    message[size + rows0 :] = first


def gather_z_kernel(count, *refs):
    shares, out = refs[:count], refs[count]
    size = shares[0].shape[0]
    period = 32 * count
    rows2 = 16
    tiles, planes = out.shape[0], out.shape[1]
    lane = iota((size, LANES), 1)
    for slot in range(3):
        totals = [jnp.zeros((size, LANES), F32) for _ in range(tiles)]
        for o in range(count):
            shift = (32 * o + 13 - 42 * slot) % LANES
            turned = pltpu.roll(shares[o][...], shift, 1) if shift else shares[o][...]
            position = ((lane - shift) & (LANES - 1)) - 42 * slot
            inside = (position >= 0) & (position < 38)
            for t in range(tiles):
                lands = lax.rem(position + (32 * o + 13 + period), period) == lane + LANES * t
                totals[t] = totals[t] + jnp.where(inside & lands, turned, 0.0)
        for t in range(tiles):
            for c in range(slot, planes, 3):
                out[t, c] = totals[t][rows2 * (c // 3) : rows2 * (c // 3 + 1)]


ROWS_SENT = 20


def plane_sent(message, share, c):
    lane = iota((ROWS_SENT, LANES), 1)
    pair = message[ROWS_SENT * (c // 2) : ROWS_SENT * (c // 2 + 1)]
    inside = (lane >= 32) & (lane < 96)
    value = jnp.where(inside, pltpu.roll(pair, LANES - 32 if c % 2 else 32, 1), 0.0)
    start = ROWS_SENT * (share // 2)
    sides = message[start : start + ROWS_SENT]
    low = pltpu.roll(sides, (28 - 8 * c) % LANES, 1)
    high = pltpu.roll(sides, (92 - 8 * c) % LANES, 1)
    value = jnp.where((lane >= 28) & (lane < 32), low, value)
    return jnp.where((lane >= 96) & (lane < 100), high, value)


def rows_kernel(sources, strips, *refs):
    inputs, (out, up, down) = refs[:-3], refs[-3:]
    own, messages = inputs[0], inputs[1:]
    planes, share = out.shape[0], own.shape[0]
    read = {}
    for p in range(planes):
        total = None
        for index, offset in sources:
            c = p - 7 - 8 * offset + 2
            if not 0 <= c < share:
                continue
            if (index, c) not in read:
                if index == 0:
                    read[index, c] = own[c, 2 : 2 + ROWS_SENT]
                else:
                    read[index, c] = plane_sent(messages[index], share, c)
            value = read[index, c]
            total = value if total is None else total + value
        out[p] = total
        down[9 * p : 9 * p + 9] = total[0:9]
        up[9 * p : 9 * p + 9] = total[11:20]
    start = ROWS_SENT * (share // 2 + 1)
    inner = (messages[0].shape[0] - start) // 2
    place = 9 * planes
    for k in range(strips):
        for part in range(2):
            begin = start + inner * part
            down[place : place + 6] = messages[k][begin : begin + 6]
            last = begin + inner - 8 - SPILL
            up[place : place + 6] = messages[k][last : last + 6]
            place += 6


def columns_kernel(strips, g1, *refs):
    messages, (above, below), (out, up, down) = refs[:-5], refs[-5:-3], refs[-3:]
    planes, rows = out.shape[0], out.shape[1]
    for p in range(planes):
        out[p] = jnp.zeros((rows, LANES), F32)
        out[p, 6 : 6 + ROWS_SENT] = g1[p]
        out[p, 22:31] = out[p, 22:31] + above[9 * p : 9 * p + 9]
        out[p, 1:10] = out[p, 1:10] + below[9 * p : 9 * p + 9]
    share = planes - 10
    start = ROWS_SENT * (share // 2 + 1)
    inner = (messages[0].shape[0] - start) // 2
    for target, first, part in ((up, 89, 0), (down, 30, 1)):
        place = 0
        for packed in pack_lanes(lambda p: out[p], planes, first, 9, 9, rows):
            target[place : place + rows] = packed
            place += rows
        for k in range(strips):
            begin = start + inner * part
            six = 9 * planes + 6 * (2 * k + part)
            target[place : place + ROW0] = jnp.zeros((ROW0, LANES), F32)
            target[place + ROW0 : place + ROW0 + inner] = messages[k][begin : begin + inner]
            at = place + ROW0 - SPILL
            target[at : at + 6] = target[at : at + 6] + below[six : six + 6]
            at = place + ROW0 + inner - 8
            target[at : at + 6] = target[at : at + 6] + above[six : six + 6]
            place += ROW0 + inner


def fold_x_kernel(count, *refs):
    shares, out = refs[:count], refs[count]
    tiles, period = out.shape[0], out.shape[1]
    for t in range(tiles):
        for x in range(period):
            total = None
            for o in range(count):
                for c in range(10):
                    if (c - 3 + 4 * o) % period == x:
                        value = shares[o][t, c]
                        total = value if total is None else total + value
            out[t, x] = total


def fine_sweeps(base, first, second):
    seventh = 1.0 / 7.0
    planes = base.shape[1]
    yield from sweep_steps(first, base, 1, planes - 1, base, seventh)
    yield from sweep_steps(second, first, 2, planes - 2, base, seventh)
    yield from sweep_steps(first, second, 3, planes - 3, base, seventh)
    yield from sweep_steps(second, first, 4, planes - 4, base, seventh)


def window_kernel(g1, out, base, first, second):
    for p in range(base.shape[1]):
        base[0, p] = g1[p]
    together(fine_sweeps(base, first, second))
    for c in range(out.shape[0]):
        p = 5 + c
        out[c] = (seven_sum(second, p, p - 1, p + 1)[0] * (1.0 / 7.0) + base[0, p]) * weight(1)


WINDOW_LANES = 28


def window_edge_steps(f1, above, below, out, base, first, second):
    rows = base.shape[2]
    share = out.shape[0]
    size = share // 4
    planes = share + 10
    lane = iota((rows, LANES), 1)
    turned = []
    for begin in range(0, rows * -(-planes // 14), rows):
        turned.append((below[begin : begin + rows],
                       pltpu.roll(above[begin : begin + rows], 19, 1)))
    for j in range(base.shape[1]):
        value = jnp.zeros((rows, LANES), F32)
        for q in range(4):
            p = size * q + j
            lower, upper = turned[p // 14]
            shift = 9 * (p % 14)
            term = jnp.where(((lane - shift) & (LANES - 1)) < 14, lower, upper)
            shift = (WINDOW_LANES * q - shift) % LANES
            term = pltpu.roll(term, shift, 1) if shift else term
            place = lane - WINDOW_LANES * q
            inside = (place >= 0) & (place < WINDOW_LANES) & ((place < 9) | (place >= 19))
            value = jnp.where(inside, term, value)
        base[0, j] = value
        yield
    yield from fine_sweeps(base, first, second)
    for m in range(size):
        p = 5 + m
        value = seven_sum(second, p, p - 1, p + 1)[0] * (1.0 / 7.0) + base[0, p]
        value = value * weight(1)
        for q in range(4):
            c = size * q + m
            low = pltpu.roll(value, (25 - WINDOW_LANES * q) % LANES, 1)
            high = pltpu.roll(value, (75 - WINDOW_LANES * q) % LANES, 1)
            part = jnp.where((lane >= 89) & (lane < 98), high, 0.0)
            out[c] = f1[c] + jnp.where((lane >= 30) & (lane < 39), low, part)
        yield


def restrict_lanes(values, width, coarse_width, coarse_tiles):
    out = []
    for s in range(coarse_tiles):
        total = None
        for t, value in enumerate(values):
            matrix = one_hot(
                lambda r, c: ((LANES * t + r) // 2 == lax.rem(LANES * s + c, coarse_width))
                & (LANES * t + r < width)
            )
            term = dot_ones(value, matrix)
            total = term if total is None else total + term
        out.append(total)
    return out


def prolong_lanes(values, width, fine_tiles):
    out = []
    for s in range(fine_tiles):
        total = None
        for t, value in enumerate(values):
            matrix = one_hot(lambda r, c: LANES * t + r == lax.rem(LANES * s + c, width) // 2)
            term = dot_ones(value, matrix)
            total = term if total is None else total + term
        out.append(total)
    return out


def swept(values):
    rows = values[0].shape[0]
    out = []
    for p, v in enumerate(values):
        total = v + (values[p - 1] + values[(p + 1) % len(values)])
        total = total + (pltpu.roll(v, 1, 0) + pltpu.roll(v, rows - 1, 0))
        out.append((total + (pltpu.roll(v, 1, 1) + pltpu.roll(v, LANES - 1, 1))) * (1.0 / 7.0))
    return out


def real_waves(count):
    cells = np.arange(count)
    rows, eigenvalues = [], []
    for k in range(count // 2 + 1):
        angle = 2.0 * np.pi * k / count
        rows.append(np.cos(angle * cells))
        eigenvalues.append(2.0 * np.cos(angle))
        if 0 < k < count / 2:
            rows.append(np.sin(angle * cells))
            eigenvalues.append(2.0 * np.cos(angle))
    basis = np.stack(rows)
    basis = basis / np.sqrt(np.sum(basis * basis, axis=1, keepdims=True))
    return basis, np.array(eigenvalues)


def last_level_matrices(planes, rows, width):
    wave_x, value_x = real_waves(planes)
    wave_y, value_y = real_waves(rows)
    wave_z, value_z = real_waves(width)
    into = np.kron(np.repeat(wave_x, 2, axis=1), np.repeat(wave_y, 2, axis=1))
    level_values = value_x[:, None, None] + value_y[None, :, None] + value_z[None, None, :]
    factor = (1.0 + level_values) / 7.0
    total = sum(factor**k for k in range(COARSE_ITERS)) * weight(LEVELS - 1) * 0.125
    scale = np.zeros((planes * rows, LANES))
    scale[:, :width] = total.reshape(planes * rows, width)
    fine = 2 * width
    tiles = max(1, fine // LANES)
    lanes = np.arange(LANES * tiles)
    to_waves = np.zeros((LANES * tiles, LANES))
    to_waves[:fine, :width] = wave_z.T[lanes[:fine] // 2]
    from_waves = np.zeros((LANES, LANES * tiles))
    from_waves[:width] = wave_z[:, (lanes % fine) // 2]
    to_waves = to_waves.reshape(tiles, LANES, LANES)
    from_waves = from_waves.reshape(LANES, tiles, LANES).transpose(1, 0, 2)
    arrays = (into, into.T, to_waves, from_waves, scale)
    return [jnp.asarray(np.ascontiguousarray(a), F32) for a in arrays]


def solve_last(values, into, back, to_waves, from_waves, scale):
    values = dot(into[...], values)
    yield
    values = dot(values, to_waves[0]) * scale[...]
    yield
    values = dot(back[...], values)
    yield
    return dot(values, from_waves[0])


def solve(level, width, buffers, spectral):
    g, a, b = buffers[level]
    tiles, planes, rows = g.shape[0], g.shape[1], g.shape[2]
    seventh = 1.0 / 7.0
    w = weight(level)
    if level == LEVELS - 2:
        source = [g[0, p] for p in range(planes)]
        first = swept(source)
        yield
        second = swept(first)
        yield
        third = swept(second)
        yield
        before = [(x + y + z) * w for x, y, z in zip(source, first, second)]
        values = yield from solve_last(jnp.concatenate(third, axis=0), *spectral)
        error = [before[p] + values[rows * p : rows * (p + 1)] for p in range(planes)]
        yield
        for _ in range(SWEEPS):
            error = swept(error)
            yield
        for p in range(planes):
            g[0, p] = before[p] + error[p]
        return
    yield from sweep_steps(a, g, 0, planes, None, seventh, planes)
    yield from sweep_steps(b, a, 0, planes, None, seventh, planes)
    for t in range(tiles):
        for p in range(planes):
            g[t, p] = (g[t, p] + a[t, p] + b[t, p]) * w
    yield from sweep_steps(a, b, 0, planes, None, seventh, planes)
    half = rows // 2
    values = []
    for t in range(tiles):
        parts = []
        for c in range(planes // 2):
            total = a[t, 2 * c, pl.ds(0, half, stride=2), :]
            total = total + a[t, 2 * c, pl.ds(1, half, stride=2), :]
            total = total + a[t, 2 * c + 1, pl.ds(0, half, stride=2), :]
            total = total + a[t, 2 * c + 1, pl.ds(1, half, stride=2), :]
            parts.append(total)
        values.append(jnp.concatenate(parts, axis=0))
    coarse = buffers[level + 1][0]
    values = restrict_lanes(values, width, width // 2, coarse.shape[0])
    for t, value in enumerate(values):
        for c in range(planes // 2):
            coarse[t, c] = value[half * c : half * (c + 1)] * 0.125
    yield from solve(level + 1, width // 2, buffers, spectral)
    values = [
        jnp.concatenate([coarse[t, c] for c in range(planes // 2)], axis=0)
        for t in range(coarse.shape[0])
    ]
    values = prolong_lanes(values, width, tiles)
    for t, value in enumerate(values):
        for c in range(planes // 2):
            part = value[half * c : half * (c + 1)]
            for p in (2 * c, 2 * c + 1):
                b[t, p, pl.ds(0, half, stride=2), :] = part
                b[t, p, pl.ds(1, half, stride=2), :] = part
        for p in range(planes):
            b[t, p] = b[t, p] + g[t, p]
    yield from sweep_steps(a, b, 0, planes, None, seventh, planes)
    yield from sweep_steps(b, a, 0, planes, None, seventh, planes)
    yield from sweep_steps(a, b, 0, planes, None, seventh, planes)
    for t in range(tiles):
        for p in range(planes):
            g[t, p] = g[t, p] + a[t, p]


def coarse_steps(count, *refs):
    shares, spectral = refs[:count], refs[count : count + 5]
    out, scratch = refs[count + 5], refs[count + 6 :]
    buffers = {level: scratch[3 * (level - 2) : 3 * (level - 1)] for level in (2, 3)}
    g = buffers[2][0]
    tiles, planes = g.shape[0], g.shape[1]
    for t in range(tiles):
        for p in range(planes):
            for b in range(count):
                value = shares[b][t, p, 0:8] + shares[(b - 1) % count][t, p, 8:16]
                g[t, p, 8 * b : 8 * b + 8] = value
    yield from solve(2, LANES * tiles, buffers, spectral)
    for c in range(out.shape[0]):
        out[c] = g[0, (c - 3) % planes, 0:16]


def arrived_kernel(above, below, out):
    out[...] = jnp.zeros(out.shape, F32)


def late_kernel(count, sources, planes, *refs):
    shares, rest = refs[: count + 5], refs[count + 5 :]
    f1, above, below, own, e2_out, f1_out, edge_out = rest[:7]
    scratch = rest[7:]
    together(
        coarse_steps(count, *shares, e2_out, *scratch[:6]),
        window_edge_steps(f1, above, below, f1_out, *scratch[6:9]),
        fine_edge_steps(sources, planes, above, below, own, edge_out, *scratch[9:12]),
    )


def correct_kernel(e2, f1, u0_b, u1_a, u1_b, u0_a):
    share1 = f1.shape[0]
    share2 = e2.shape[0]
    rows2 = e2.shape[1]
    value = e2[...].reshape(share2 * rows2, LANES)
    value = dot_ones(value, one_hot(lambda r, c: r == c // 2))
    for c in range(share2):
        part = value[rows2 * c : rows2 * (c + 1)]
        for p in (2 * c, 2 * c + 1):
            u1_a[0, p, pl.ds(0, rows2, stride=2), :] = part
            u1_a[0, p, pl.ds(1, rows2, stride=2), :] = part
    count1 = 2 * share2
    sweep(u1_b, u1_a, 1, count1 - 1)
    sweep(u1_a, u1_b, 2, count1 - 2)
    sweep(u1_b, u1_a, 3, count1 - 3)
    rows1, sent = 24, 20
    parts = []
    for c in range(share1):
        parts.append(f1[c, 6 : 6 + rows1] + u1_b[0, 4 + c, 6 : 6 + rows1] * (1.0 / 343.0))
    value = jnp.concatenate(parts, axis=0)
    main = dot_ones(value, one_hot(lambda r, c: r == 32 + c // 2))
    side = dot_ones(value, one_hot(lambda r, c: r == jnp.where(c < 64, 96 + c // 2, c // 2 - 32)))
    for t, value in enumerate((main, side)):
        for c in range(share1):
            part = value[rows1 * c : rows1 * c + sent]
            for p in (2 * c, 2 * c + 1):
                u0_a[t, p, pl.ds(0, sent, stride=2), :] = part
                u0_a[t, p, pl.ds(1, sent, stride=2), :] = part
    count0 = 2 * share1
    sweep(u0_b, u0_a, 1, count0 - 1)
    sweep(u0_a, u0_b, 2, count0 - 2)
    sweep(u0_b, u0_a, 3, count0 - 3)


def plane_copies(source, target, semaphores):
    step = source.shape[1] // semaphores.shape[0]
    copies = []
    for k in range(semaphores.shape[0]):
        planes = pl.ds(step * k, step)
        copies.append(
            pltpu.make_async_copy(source.at[:, planes], target.at[:, planes], semaphores.at[k])
        )
    return copies


def finish_kernel(field, u0_b, f0, below_x, above_x, edge, result, out, finished):
    planes, rows = field.shape[1], field.shape[2]
    scale = 1.0 / 343.0
    lane = iota((rows, LANES), 1)
    row = iota((rows, LANES), 0)
    copies = plane_copies(out, result, finished)
    step = planes // len(copies)

    def potential(i):
        q, m = i // edge.shape[0], i % edge.shape[0]
        value = u0_b[0, 4 + i, 4 : 4 + rows] * scale + f0[fine_place(i + SPILL, planes + 11)]
        if i <= SPILL:
            value = value + below_x[1 + i]
        if i >= planes - SPILL:
            value = value + above_x[i - (planes - SPILL)]
        return value + edge_sides(edge[m, 0:rows], q)

    here = potential(0)
    for i in range(planes):
        above = potential(i + 1)
        out[0, i] = field[0, i] - (above - here)
        q, m = i // edge.shape[0], i % edge.shape[0]
        end = u0_b[0, 4 + i, 4 + rows : 5 + rows] * scale + f0[6, i + SPILL : i + SPILL + 1]
        if i <= SPILL:
            end = end + below_x[0, i + SPILL + planes : i + SPILL + planes + 1]
        if i >= planes - SPILL:
            end = end + above_x[6, i + SPILL - planes : i + SPILL - planes + 1]
        end = end + edge_sides(edge[m, rows : rows + 1], q)
        end = jnp.broadcast_to(end, (rows, LANES))
        next_y = jnp.where(row == rows - 1, end, pltpu.roll(here, rows - 1, 0))
        out[1, i] = field[1, i] - (next_y - here)
        part = edge[m, 0:rows]
        last = pltpu.roll(u0_b[1, 4 + i, 4 : 4 + rows], LANES - 1, 1) * scale
        last = last + turned_to_last(part, GROUP_LANES * q + HIGH_AT)
        last = last + turned_to_last(part, GROUP_LANES * q + OWN_AT + SPILL)
        next_z = jnp.where(lane == LANES - 1, last, pltpu.roll(here, LANES - 1, 1))
        out[2, i] = field[2, i] - (next_z - here)
        if i % step == step - 1:
            copies[i // step].start()
        here = above
    for copy in copies:
        copy.wait()


def fine_place(p, share):
    if p <= SPILL:
        return p
    return p - share + 13 if p >= share - 6 else p + 7


def fine_own_kernel(zeroth, first, second, third, field, main, down, up, field_out, fourth):
    share = main.shape[0]
    field_out[...] = field[...]
    low, high = PLANE0, zeroth.shape[1] - 6
    sweep(fourth, third, low - 4, high + 4)
    clear_margin(fourth, low - 4, high + 4)
    powers = (zeroth, first, second, third, fourth)
    for k in range(share):
        p = low - SPILL + k
        total = seven_sum(fourth, p, p - 1, p + 1, 1)[0] * (weight(0) / 7.0**5)
        for n, power in enumerate(powers):
            if low - n <= p < high + n:
                total = total + power[0, p] * (weight(0) / 7.0**n)
        main[k] = total
        down[k] = total[1:9]
        up[k] = total[40:48]


GROUPS = 3
GROUP_LANES = 42
LOW_END, HIGH_AT, OWN_AT = 5, 16, 22


def fine_edge_steps(sources, planes, above, below, own, out, base, first, second):
    rows = base.shape[2]
    size = out.shape[0]
    lane = iota((rows, LANES), 1)
    strips = 1 + max(index for index, offset in sources)
    start = above.shape[0] - rows * strips
    turned = []
    for index in range(strips):
        begin = start + rows * index
        turned.append((below[begin : begin + rows],
                       pltpu.roll(above[begin : begin + rows], HIGH_AT, 1),
                       pltpu.roll(own[begin : begin + rows], OWN_AT, 1)))
    spread = SPILL + 1
    for j in range(base.shape[1]):
        value = jnp.zeros((rows, LANES), F32)
        for q in range(GROUPS):
            total = None
            for index, offset in sources:
                i = size * q + j - SPILL - offset * planes
                if not 0 <= i <= planes:
                    continue
                low, high, last = turned[index]
                place = (lane - 7 * i) & (LANES - 1)
                term = jnp.where(place < OWN_AT, jnp.where(place < HIGH_AT, low, high), last)
                shift = (GROUP_LANES * q - 7 * i) % LANES
                term = pltpu.roll(term, shift, 1) if shift else term
                total = term if total is None else total + term
            if total is None:
                continue
            place = lane - GROUP_LANES * q
            inside = (place >= 0) & (place < OWN_AT + spread)
            inside = inside & ((place < spread) | (place >= HIGH_AT))
            value = jnp.where(inside, total, value)
        base[0, j] = value
        yield
    seventh = 1.0 / 7.0
    yield from fine_sweeps(base, first, second)
    kept = out.shape[1]
    for i in range(size):
        p = SPILL + i
        value = (seven_sum(second, p, p - 1, p + 1)[0] * seventh + base[0, p]) * weight(0)
        out[i] = value[ROW0 : ROW0 + kept]
        yield


def edge_sides(part, q):
    lane = iota(part.shape, 1)
    low = pltpu.roll(part, (-GROUP_LANES * q - LOW_END) % LANES, 1)
    high = pltpu.roll(part, (LANES - SPILL - GROUP_LANES * q - LOW_END - 6) % LANES, 1)
    return jnp.where(lane <= SPILL, low, jnp.where(lane >= LANES - SPILL, high, 0.0))


def turned_to_last(value, lane):
    return pltpu.roll(value, (LANES - 1 - lane) % LANES, 1)


def fine_y_kernel(main, above, below, out, work):
    share = main.shape[0]
    rows = out.shape[1]
    out[6] = jnp.zeros((rows, LANES), F32)
    for p in range(share):
        work[p] = main[p]
        work[p, 33:41] = work[p, 33:41] + above[p]
        work[p, 8:16] = work[p, 8:16] + below[p]
        out[fine_place(p, share)] = work[p, ROW0 : ROW0 + rows]
        out[6, p : p + 1] = work[p, ROW0 + rows : ROW0 + rows + 1]


def body(field):
    nx, ny, nz = field.shape[1:]
    size_x, size_y, size_z = lax.axis_size("gx"), lax.axis_size("gy"), lax.axis_size("gz")
    n1 = nx // 2
    share1 = n1 + 4
    rows0 = ny + 16
    rows1 = ny // 2 + 8
    planes0 = nx + 13

    def from_offset(value, axis, offset):
        count = lax.axis_size(axis)
        pairs = [(source, (source - offset) % count) for source in range(count)]
        return lax.ppermute(value, axis, pairs)

    level0 = (2, planes0, rows0, LANES)
    level1 = (1, n1 + 12, ny // 2 + 16, LANES)
    packed = -(-(n1 // 2 + 6) // 3) * 16
    inner0 = rows0 - ROW0
    sent1 = ROWS_SENT * (share1 // 2 + 1)
    message, g2, g1, *powers = call(
        spread_kernel,
        [shape(sent1 + 2 * inner0, LANES), shape(packed, LANES),
         shape(share1, rows1, LANES)] + [shape(*level0)] * 4,
        [level1, level1],
        2.9,
        field,
    )
    shares = [g2] + [from_offset(g2, "gz", o) for o in range(1, size_z)]
    messages = {0: message}
    sources = []
    for o in (0, 1, -1, 2, -2):
        key = [k for k in messages if k % size_x == o % size_x]
        if not key:
            messages[o] = from_offset(message, "gx", o)
            key = [o]
        sources.append((list(messages).index(key[0]), o))
    messages = list(messages.values())
    strips = min(3, size_x)
    planes1 = n1 + 14
    sent_y = 9 * planes1 + 12 * strips
    rows_g1, up, down = call(
        functools.partial(rows_kernel, tuple(sources), strips),
        [shape(planes1, ROWS_SENT, LANES), shape(sent_y, LANES), shape(sent_y, LANES)],
        [],
        0.2,
        g1, *messages,
    )
    window = (1, planes1, ny // 2 + 16, LANES)
    sent_z = window[2] * -(-planes1 // 14) + rows0 * strips
    window_g1, up, down = call(
        functools.partial(columns_kernel, strips),
        [shape(*window[1:]), shape(sent_z, LANES), shape(sent_z, LANES)],
        [],
        0.3,
        rows_g1, *messages[:strips], from_offset(down, "gy", 1), from_offset(up, "gy", -1),
    )
    above = from_offset(down, "gz", 1)
    below = from_offset(up, "gz", -1)
    f1 = call(
        window_kernel,
        shape(share1, *window[2:]),
        [window, window, window],
        0.01,
        window_g1,
    )
    packed = (1, share1 // 4 + 10, *window[2:])
    share0 = nx + 11
    main, f_down, f_up, kept = call(
        fine_own_kernel,
        [shape(share0, rows0, LANES), shape(share0, 8, LANES), shape(share0, 8, LANES),
         shape(*field.shape)],
        [level0],
        3.0,
        *powers, field,
        after=(messages[1],),
    )
    f_above = from_offset(f_down, "gy", 1)
    f_below = from_offset(f_up, "gy", -1)

    tiles = size_z * 32 // LANES
    g2 = call(
        functools.partial(gather_z_kernel, size_z),
        shape(tiles, n1 // 2 + 6, 16, LANES),
        [],
        0.15,
        *shares,
        after=(rows_g1, main,),
    )
    shares = [g2] + [from_offset(g2, "gx", o) for o in range(1, size_x)]
    g2 = call(
        functools.partial(fold_x_kernel, size_x),
        shape(tiles, 4 * size_x, 16, LANES),
        [],
        0.05,
        *shares,
        after=(window_g1,),
    )
    shares = [g2] + [from_offset(g2, "gy", o) for o in range(1, size_y)]

    f0 = call(
        fine_y_kernel,
        shape(share0 + 1, ny, LANES),
        [(share0, rows0, LANES)],
        0.01,
        main, f_above, f_below,
        after=(g2,),
    )
    if size_x == 2:
        other = from_offset(f0[0:13], "gx", 1)
        f_above, f_below = other[0:7], other[6:13]
    else:
        f_above = from_offset(f0[0:7], "gx", 1)
        f_below = from_offset(f0[6:13], "gx", -1)
    group = -(-(nx + 1) // GROUPS)
    edges = (1, group + 2 * SPILL, rows0, LANES)
    scratch = []
    for level in (2, 3):
        cut = 2 ** (level - 2)
        extent = (max(1, tiles // cut), 4 * size_x // cut, 8 * size_y // cut, LANES)
        scratch.extend([extent] * 3)
    arrived = call(arrived_kernel, shape(8, LANES), [], 2.0, above, below)
    e2, f1, edge = call(
        functools.partial(late_kernel, size_y, tuple(sources[:3]), nx),
        [shape(n1 // 2 + 6, 16, LANES), shape(share1, *window[2:]), shape(group, ny + 8, LANES)],
        scratch + [packed] * 3 + [edges] * 3,
        3.0,
        *shares, *last_level_matrices(size_x, 2 * size_y, 8 * size_z), f1, above, below, up,
        after=(arrived,),
    )
    fine = (2, nx + 8, ny + 8, LANES)
    correction = call(
        correct_kernel,
        shape(*fine),
        [level1, level1, fine],
        2.2,
        e2, f1,
    )
    return call(
        finish_kernel,
        shape(*field.shape),
        [field.shape, pltpu.SemaphoreType.DMA((8,))],
        1.2,
        kept, correction, f0, f_below, f_above, edge,
        out_specs=pl.BlockSpec(memory_space=pltpu.HBM),
    )


def solution(mesh):
    in_specs = (P(None, "gx", "gy", "gz"),)
    out_specs = P(None, "gx", "gy", "gz")
    return jax.shard_map(body, mesh=mesh, in_specs=in_specs, out_specs=out_specs, check_vma=False)
```
